32 devices in a mesh: blk: 4 (over y, x), grp: 8 (over z, core).
Axes of the slice: x: 2, y: 2, z: 4, core: 2. Of those that a mesh axis runs over, the one named last changes fastest.
Arguments:
- amplitudes: bfloat16 [4, 512, 1024], P(None, 'blk'), may hold values from -6 to 6
- pair_screen: int32 [4, 32], P(None, 'blk'), may hold values 0 or 1
- integrals: bfloat16 [32, 1024, 1024], P(('blk', 'grp')), may hold values from -0.1875 to 0.1875
- tile_ab: int32 [4, 8], replicated, may hold values from 0 to 49, as said below
- tile_cd: int32 [4, 8], replicated, may hold values from 0 to 3
- residual_in: float32 [512, 50, 1024], P(('blk', 'grp')), may hold values from -6 to 6
Outputs:
- residual: float32 [512, 50, 1024], P(('blk', 'grp'))
The draws below stay inside these ranges and needn't reach their ends.
Inputs may be any that keep to these rules, and one draw needn't show every extreme that they name: `tile_ab`: the 4 integral tiles that share a column g name 2 to 4 distinct b tiles, and in every draw some column names exactly 4.
All inputs are finite; a program needn't handle non-finite values. No bound on the sum of `pair_screen` on one device may be relied on, other than what follows from the above.
Results may differ from the reference program's by a relative error of at most 0.0003.
Values may be sent and summed in bfloat16 or wider, within the bound.
No kernel may reach another device: no remote copies, remote signals or barrier semaphores. Data moves between devices by JAX's collectives and lax.ppermute only.
A program may use at most 128 MiB of HBM per device.

```python
import jax
import jax.numpy as jnp
from jax import lax

NCD = 4
PBR = 16
UNIQ = 4
NAB = 50
K = 1024
PAIRS = 512
NT = 32
N_BLK = 4
N_GRP = 8


def draw_tile_ab(key, part):
    key_count, key_widest, key_cands, key_picks, key_order = jax.random.split(key, 5)
    counts = jax.random.randint(key_count, (N_GRP,), 2, UNIQ + 1)
    widest = jax.random.randint(key_widest, (), 0, N_GRP)
    counts = jnp.where(jnp.arange(N_GRP) == widest, UNIQ, counts)
    cand_keys = jax.random.split(key_cands, N_GRP)
    candidates = jax.vmap(lambda single: jax.random.permutation(single, NAB)[:UNIQ])(cand_keys)
    picks = jax.random.randint(key_picks, (N_BLK, N_GRP), 0, 1 << 20) % counts[None, :]
    ranks = jnp.arange(N_BLK)[:, None]
    picks = jnp.where(ranks < counts[None, :], ranks, picks)
    order_keys = jax.random.split(key_order, N_GRP)
    orders = jax.vmap(lambda single: jax.random.permutation(single, N_BLK))(order_keys)
    picks = jnp.take_along_axis(picks, orders.T, axis=0)
    chosen = jnp.take_along_axis(candidates.T, picks, axis=0)
    return chosen.astype(jnp.int32)


def plant(drawn, own_key, smallest, largest):
    longest = drawn.shape.index(max(drawn.shape))
    spots = []
    for shift in (0, 1):
        where = [jax.random.randint(jax.random.fold_in(own_key, axis), (), 0, length) for axis, length in enumerate(drawn.shape)]
        where[longest] = (where[longest] + shift) % drawn.shape[longest]
        spots.append(tuple(where))
    return drawn.at[spots[0]].set(smallest).at[spots[1]].set(largest)


def block_scale(key, extent, cuts, smallest, largest):
    def one(dim, parts):
        heights = jax.random.uniform(jax.random.fold_in(jax.random.fold_in(key, 6), dim), (parts,), jnp.float32, smallest / len(cuts), largest / len(cuts))
        return jnp.repeat(jnp.exp(heights), extent[dim] // parts).reshape((-1,) + (1,) * (len(extent) - dim - 1))

    factor_of = one(*cuts[0])
    for cut in cuts[1:]:
        factor_of = factor_of * one(*cut)
    return factor_of


def normal_values(stream_key, extent, scale, reach, cuts=(), kind=jnp.bfloat16):
    drawn = jax.random.normal(stream_key, extent, jnp.float32) * scale
    if len(cuts) > 0:
        drawn = block_scale(stream_key, extent, cuts, -0.22, 0.18) * drawn
    return jnp.clip(drawn, min=-reach, max=reach).astype(kind)


def setup_inputs(seed: int = 0) -> dict:
    seeds = jax.random.split(jax.random.key(seed), 7)
    amplitudes = normal_values(seeds[0], (NCD, PAIRS, K), 1.0, 6.0, ((1, 4),))
    pair_screen = plant((jax.random.randint(seeds[1], (NCD, PAIRS // PBR), 0, 4) < 3).astype(jnp.int32), jax.random.fold_in(seeds[1], 1), 0, 1)
    integrals = normal_values(seeds[2], (NT, K, K), K ** -0.5, 0.1875, ((0, 32),))
    tile_ab = draw_tile_ab(jax.random.fold_in(seeds[6], 71), 0)
    tile_cd = plant(jax.random.randint(seeds[4], (N_BLK, N_GRP), 0, NCD), jax.random.fold_in(seeds[4], 1), 0, NCD - 1).astype(jnp.int32)
    residual_in = normal_values(seeds[5], (PAIRS, NAB, K), 1.0, 6.0, ((0, 32),), jnp.float32)
    return {"amplitudes": amplitudes, "pair_screen": pair_screen, "integrals": integrals, "tile_ab": tile_ab, "tile_cd": tile_cd, "residual_in": residual_in}


def reference(amplitudes, pair_screen, integrals, tile_ab, tile_cd, residual_in):
    row_mask = jnp.repeat(pair_screen, PBR, axis=1).astype(jnp.bfloat16)
    masked = amplitudes * row_mask[:, :, None]
    flat_ab = tile_ab.reshape(-1).astype(jnp.int32)
    flat_cd = tile_cd.reshape(-1).astype(jnp.int32)

    def add_tile(position, running):
        position = jnp.asarray(position).astype(jnp.int32)
        cd_index = flat_cd[position].astype(jnp.int32)
        ab_index = flat_ab[position].astype(jnp.int32)
        rows_in = lax.dynamic_index_in_dim(masked, cd_index, 0, keepdims=False)
        panel = lax.dynamic_index_in_dim(integrals, position, 0, keepdims=False)
        product = jnp.dot(rows_in, panel, preferred_element_type=jnp.float32)
        earlier = lax.dynamic_index_in_dim(running, ab_index, 1, keepdims=False)
        return lax.dynamic_update_index_in_dim(running, earlier + product, ab_index, 1)

    return lax.fori_loop(0, NT, add_tile, residual_in)
```

```python
import jax
import jax.numpy as jnp
from jax import lax
from jax.sharding import PartitionSpec as P


def shards(amplitudes, pair_screen, integrals, tile_ab, tile_cd, residual_in):
    blk_count = lax.axis_size("blk")
    grp_count = lax.axis_size("grp")
    grp_position = lax.axis_index("grp")
    owner_rows, ab_tiles, tile_width = residual_in.shape
    group_rows = amplitudes.shape[1]
    row_mask = jnp.repeat(pair_screen, owner_rows, axis=1).astype(jnp.bfloat16)
    masked = amplitudes * row_mask[:, :, None]
    column_cd = lax.dynamic_index_in_dim(tile_cd, grp_position, 1, keepdims=False)
    outgoing = jnp.stack(
        [lax.dynamic_index_in_dim(masked, column_cd[p], 0, keepdims=False) for p in range(blk_count)]
    )
    rows_in = lax.all_to_all(outgoing, "blk", split_axis=0, concat_axis=0, tiled=True)
    rows_in = rows_in.reshape(blk_count * group_rows, -1)
    product = jnp.dot(rows_in, integrals[0], preferred_element_type=jnp.float32)
    coded = product.astype(jnp.float16).reshape(blk_count * grp_count, owner_rows, tile_width)
    arrived = lax.all_to_all(coded, ("blk", "grp"), split_axis=0, concat_axis=0, tiled=True)
    blocks = arrived.astype(jnp.float32)
    summed = jax.ops.segment_sum(blocks, tile_ab.reshape(-1), num_segments=ab_tiles)
    return residual_in + jnp.transpose(summed, (1, 0, 2))


def solution(mesh):
    in_specs = (
        P(None, "blk", None),
        P(None, "blk"),
        P(("blk", "grp"), None, None),
        P(),
        P(),
        P(("blk", "grp"), None, None),
    )
    out_specs = P(("blk", "grp"), None, None)
    return jax.shard_map(shards, mesh=mesh, in_specs=in_specs, out_specs=out_specs, check_vma=False)
```

```python
import jax
import jax.numpy as jnp
from jax import lax
from jax.experimental import pallas as pl
from jax.experimental.pallas import tpu as pltpu
from jax.sharding import PartitionSpec as P


def pick_kernel(tile_cd, amplitudes, outgoing, sems):
    grp = lax.axis_index("grp")
    copies = []
    for p in range(outgoing.shape[0]):
        copies.append(pltpu.make_async_copy(amplitudes.at[tile_cd[p, grp]], outgoing.at[p], sems.at[p]))
    for copy in copies:
        copy.start()
    for copy in copies:
        copy.wait()


def pick(tile_cd, amplitudes):
    columns = tile_cd.shape[0]
    return pl.pallas_call(
        pick_kernel,
        out_shape=jax.ShapeDtypeStruct((columns,) + amplitudes.shape[1:], amplitudes.dtype),
        in_specs=[pl.BlockSpec(memory_space=pltpu.SMEM), pl.BlockSpec(memory_space=pl.ANY)],
        out_specs=pl.BlockSpec(memory_space=pl.ANY),
        scratch_shapes=[pltpu.SemaphoreType.DMA((columns,))],
        name="pick_cd_blocks",
    )(tile_cd, amplitudes)


def add_kernel(pieces, tile_ab, tile_cd, pair_screen, blocks, residual_in, residual, held, in_sems, out_sems):
    grp = lax.axis_index("grp")
    ab_tiles = residual.shape[0]
    columns, grp_count = tile_ab.shape
    bounds = [ab_tiles * piece // pieces for piece in range(pieces + 1)]
    parts = [pl.ds(low, high - low) for low, high in zip(bounds[:-1], bounds[1:])]
    arrivals = [pltpu.make_async_copy(residual_in.at[part], held.at[part], in_sems.at[i]) for i, part in enumerate(parts)]
    leaves = [pltpu.make_async_copy(held.at[part], residual.at[part], out_sems.at[i]) for i, part in enumerate(parts)]
    for copy in arrivals:
        copy.start()
    for copy in arrivals:
        copy.wait()

    def add_tile(tile, carry):
        p, g = tile // grp_count, tile % grp_count

        @pl.when(pair_screen[tile_cd[p, g], grp] != 0)
        def _():
            ab = tile_ab[p, g]
            held[ab] = held[ab] + blocks[tile]

        return carry

    lax.fori_loop(0, columns * grp_count, add_tile, 0)
    for copy in leaves:
        copy.start()
    for copy in leaves:
        copy.wait()


def add_blocks(tile_ab, tile_cd, pair_screen, blocks, residual_in):
    pieces = 5
    smem = pl.BlockSpec(memory_space=pltpu.SMEM)
    return pl.pallas_call(
        lambda *refs: add_kernel(pieces, *refs),
        out_shape=jax.ShapeDtypeStruct(residual_in.shape, residual_in.dtype),
        in_specs=[smem, smem, smem, pl.BlockSpec(memory_space=pltpu.VMEM), pl.BlockSpec(memory_space=pl.ANY)],
        out_specs=pl.BlockSpec(memory_space=pl.ANY),
        scratch_shapes=[
            pltpu.VMEM(residual_in.shape, residual_in.dtype),
            pltpu.SemaphoreType.DMA((pieces,)),
            pltpu.SemaphoreType.DMA((pieces,)),
        ],
        compiler_params=pltpu.CompilerParams(vmem_limit_bytes=32 * 1024 * 1024),
        name="add_contributions",
    )(tile_ab, tile_cd, pair_screen, blocks, residual_in)


def shards(amplitudes, pair_screen, integrals, tile_ab, tile_cd, residual_in):
    blk_count = lax.axis_size("blk")
    grp_count = lax.axis_size("grp")
    owner_rows, ab_tiles, tile_width = residual_in.shape
    group_rows = amplitudes.shape[1]
    outgoing = pick(tile_cd, amplitudes)
    rows_in = lax.all_to_all(outgoing, "blk", split_axis=0, concat_axis=0, tiled=True)
    rows_in = rows_in.reshape(blk_count * group_rows, -1)
    product = jnp.dot(rows_in, integrals[0], preferred_element_type=jnp.float32)
    coded = product.astype(jnp.float16).reshape(blk_count * grp_count, owner_rows, tile_width)
    arrived = lax.all_to_all(coded, ("blk", "grp"), split_axis=0, concat_axis=0, tiled=True)
    blocks = arrived.astype(jnp.float32)
    by_tile = jnp.transpose(residual_in, (1, 0, 2))
    return jnp.transpose(add_blocks(tile_ab, tile_cd, pair_screen, blocks, by_tile), (1, 0, 2))


def solution(mesh):
    in_specs = (
        P(None, "blk", None),
        P(None, "blk"),
        P(("blk", "grp"), None, None),
        P(),
        P(),
        P(("blk", "grp"), None, None),
    )
    out_specs = P(("blk", "grp"), None, None)
    return jax.shard_map(shards, mesh=mesh, in_specs=in_specs, out_specs=out_specs, check_vma=False)
```

```python
import jax
import jax.numpy as jnp
from jax import lax
from jax.experimental import pallas as pl
from jax.experimental.pallas import tpu as pltpu
from jax.sharding import PartitionSpec as P


def pick_kernel(tile_cd, amplitudes, outgoing, sems):
    grp = lax.axis_index("grp")
    copies = []
    for p in range(outgoing.shape[0]):
        copies.append(pltpu.make_async_copy(amplitudes.at[tile_cd[p, grp]], outgoing.at[p], sems.at[p]))
    for copy in copies:
        copy.start()
    for copy in copies:
        copy.wait()


def pick(tile_cd, amplitudes):
    columns = tile_cd.shape[0]
    return pl.pallas_call(
        pick_kernel,
        out_shape=jax.ShapeDtypeStruct((columns,) + amplitudes.shape[1:], amplitudes.dtype),
        in_specs=[pl.BlockSpec(memory_space=pltpu.SMEM), pl.BlockSpec(memory_space=pl.ANY)],
        out_specs=pl.BlockSpec(memory_space=pltpu.VMEM),
        scratch_shapes=[pltpu.SemaphoreType.DMA((columns,))],
        name="pick_cd_blocks",
    )(tile_cd, amplitudes)


def add_kernel(pieces, tile_ab, tile_cd, pair_screen, blocks, residual_in, residual, held, in_sems, out_sems):
    grp = lax.axis_index("grp")
    ab_tiles = residual.shape[0]
    columns, grp_count = tile_ab.shape
    bounds = [ab_tiles * piece // pieces for piece in range(pieces + 1)]
    parts = [pl.ds(low, high - low) for low, high in zip(bounds[:-1], bounds[1:])]
    arrivals = [pltpu.make_async_copy(residual_in.at[part], held.at[part], in_sems.at[i]) for i, part in enumerate(parts)]
    leaves = [pltpu.make_async_copy(held.at[part], residual.at[part], out_sems.at[i]) for i, part in enumerate(parts)]
    for copy in arrivals:
        copy.start()
    for copy in arrivals:
        copy.wait()

    def add_tile(tile, carry):
        p, g = tile // grp_count, tile % grp_count

        @pl.when(pair_screen[tile_cd[p, g], grp] != 0)
        def _():
            ab = tile_ab[p, g]
            held[ab] = held[ab] + blocks[tile]

        return carry

    lax.fori_loop(0, columns * grp_count, add_tile, 0)
    for copy in leaves:
        copy.start()
    for copy in leaves:
        copy.wait()


def add_blocks(tile_ab, tile_cd, pair_screen, blocks, residual_in):
    pieces = 5
    smem = pl.BlockSpec(memory_space=pltpu.SMEM)
    return pl.pallas_call(
        lambda *refs: add_kernel(pieces, *refs),
        out_shape=jax.ShapeDtypeStruct(residual_in.shape, residual_in.dtype),
        in_specs=[smem, smem, smem, pl.BlockSpec(memory_space=pltpu.VMEM), pl.BlockSpec(memory_space=pl.ANY)],
        out_specs=pl.BlockSpec(memory_space=pl.ANY),
        scratch_shapes=[
            pltpu.VMEM(residual_in.shape, residual_in.dtype),
            pltpu.SemaphoreType.DMA((pieces,)),
            pltpu.SemaphoreType.DMA((pieces,)),
        ],
        compiler_params=pltpu.CompilerParams(vmem_limit_bytes=32 * 1024 * 1024),
        name="add_contributions",
    )(tile_ab, tile_cd, pair_screen, blocks, residual_in)


def shards(amplitudes, pair_screen, integrals, tile_ab, tile_cd, residual_in):
    blk_count = lax.axis_size("blk")
    grp_count = lax.axis_size("grp")
    owner_rows, ab_tiles, tile_width = residual_in.shape
    group_rows = amplitudes.shape[1]
    outgoing = pick(tile_cd, amplitudes)
    rows_in = lax.all_to_all(outgoing, "blk", split_axis=0, concat_axis=0, tiled=True)
    rows_in = rows_in.reshape(blk_count * group_rows, -1)
    product = jnp.dot(rows_in, integrals[0], preferred_element_type=jnp.float32)
    coded = product.astype(jnp.float16).reshape(blk_count * grp_count, owner_rows, tile_width)
    arrived = lax.all_to_all(coded, ("blk", "grp"), split_axis=0, concat_axis=0, tiled=True)
    blocks = arrived.astype(jnp.float32)
    by_tile = jnp.transpose(residual_in, (1, 0, 2))
    return jnp.transpose(add_blocks(tile_ab, tile_cd, pair_screen, blocks, by_tile), (1, 0, 2))


def solution(mesh):
    in_specs = (
        P(None, "blk", None),
        P(None, "blk"),
        P(("blk", "grp"), None, None),
        P(),
        P(),
        P(("blk", "grp"), None, None),
    )
    out_specs = P(("blk", "grp"), None, None)
    return jax.shard_map(shards, mesh=mesh, in_specs=in_specs, out_specs=out_specs, check_vma=False)
```

```python
import jax
import jax.numpy as jnp
from jax import lax
from jax.experimental import pallas as pl
from jax.experimental.pallas import tpu as pltpu
from jax.sharding import PartitionSpec as P


def pick_kernel(tile_cd, amplitudes, *rest):
    outgoing, sems = rest[:-1], rest[-1]
    blk, grp = lax.axis_index("blk"), lax.axis_index("grp")
    copies = []
    for step, picked in enumerate(outgoing):
        cd = tile_cd[jnp.bitwise_xor(blk, step), grp]
        copies.append(pltpu.make_async_copy(amplitudes.at[cd], picked, sems.at[step]))
    for copy in copies:
        copy.start()
    for copy in copies:
        copy.wait()


def pick(tile_cd, amplitudes):
    columns = tile_cd.shape[0]
    block = jax.ShapeDtypeStruct(amplitudes.shape[1:], amplitudes.dtype)
    return pl.pallas_call(
        pick_kernel,
        out_shape=[block] * columns,
        in_specs=[pl.BlockSpec(memory_space=pltpu.SMEM), pl.BlockSpec(memory_space=pl.ANY)],
        out_specs=[pl.BlockSpec(memory_space=pltpu.VMEM)] * columns,
        scratch_shapes=[pltpu.SemaphoreType.DMA((columns,))],
        name="pick_cd_blocks",
    )(tile_cd, amplitudes)


def add_kernel(pieces, tile_ab, tile_cd, pair_screen, *rest):
    blocks, (residual_in, residual, held, in_sems, out_sems) = rest[:-5], rest[-5:]
    blk, grp = lax.axis_index("blk"), lax.axis_index("grp")
    ab_tiles = residual.shape[0]
    columns, grp_count = tile_ab.shape
    bounds = [ab_tiles * piece // pieces for piece in range(pieces + 1)]
    parts = [pl.ds(low, high - low) for low, high in zip(bounds[:-1], bounds[1:])]
    arrivals = [pltpu.make_async_copy(residual_in.at[part], held.at[part], in_sems.at[i]) for i, part in enumerate(parts)]
    leaves = [pltpu.make_async_copy(held.at[part], residual.at[part], out_sems.at[i]) for i, part in enumerate(parts)]
    for copy in arrivals:
        copy.start()
    for copy in arrivals:
        copy.wait()

    for step, group_blocks in enumerate(blocks):
        p = jnp.bitwise_xor(blk, step)

        def add_tile(g, carry):
            @pl.when(pair_screen[tile_cd[p, g], grp] != 0)
            def _():
                ab = tile_ab[p, g]
                held[ab] = held[ab] + group_blocks[g]

            return carry

        lax.fori_loop(0, grp_count, add_tile, 0)
    for copy in leaves:
        copy.start()
    for copy in leaves:
        copy.wait()


def add_blocks(tile_ab, tile_cd, pair_screen, blocks, residual_in):
    pieces = 5
    smem = pl.BlockSpec(memory_space=pltpu.SMEM)
    vmem = pl.BlockSpec(memory_space=pltpu.VMEM)
    return pl.pallas_call(
        lambda *refs: add_kernel(pieces, *refs),
        out_shape=jax.ShapeDtypeStruct(residual_in.shape, residual_in.dtype),
        in_specs=[smem, smem, smem] + [vmem] * len(blocks) + [pl.BlockSpec(memory_space=pl.ANY)],
        out_specs=pl.BlockSpec(memory_space=pl.ANY),
        scratch_shapes=[
            pltpu.VMEM(residual_in.shape, residual_in.dtype),
            pltpu.SemaphoreType.DMA((pieces,)),
            pltpu.SemaphoreType.DMA((pieces,)),
        ],
        compiler_params=pltpu.CompilerParams(vmem_limit_bytes=32 * 1024 * 1024),
        name="add_contributions",
    )(tile_ab, tile_cd, pair_screen, *blocks, residual_in)


def shards(amplitudes, pair_screen, integrals, tile_ab, tile_cd, residual_in):
    blk_count = lax.axis_size("blk")
    grp_count = lax.axis_size("grp")
    owner_rows, ab_tiles, tile_width = residual_in.shape

    def swap(value, step):
        return lax.ppermute(value, "blk", [(b, b ^ step) for b in range(blk_count)])

    picked = pick(tile_cd, amplitudes)
    rows_in = [picked[0]] + [swap(picked[step], step) for step in range(1, blk_count)]
    blocks = []
    for step in range(blk_count):
        product = jnp.dot(rows_in[step], integrals[0], preferred_element_type=jnp.float32)
        coded = product.astype(jnp.float16).reshape(grp_count, owner_rows, tile_width)
        spread = lax.all_to_all(coded, "grp", split_axis=0, concat_axis=0, tiled=True)
        blocks.append((swap(spread, step) if step else spread).astype(jnp.float32))
    by_tile = jnp.transpose(residual_in, (1, 0, 2))
    return jnp.transpose(add_blocks(tile_ab, tile_cd, pair_screen, blocks, by_tile), (1, 0, 2))


def solution(mesh):
    in_specs = (
        P(None, "blk", None),
        P(None, "blk"),
        P(("blk", "grp"), None, None),
        P(),
        P(),
        P(("blk", "grp"), None, None),
    )
    out_specs = P(("blk", "grp"), None, None)
    return jax.shard_map(shards, mesh=mesh, in_specs=in_specs, out_specs=out_specs, check_vma=False)
```

```python
import jax
import jax.numpy as jnp
from jax import lax
from jax.experimental import pallas as pl
from jax.experimental.pallas import tpu as pltpu
from jax.sharding import PartitionSpec as P

LARGEST = 32766.0
SCALE_STEPS = 64.0
SCALE_SHIFT = 8192
SCALE_BITS = 16
LANES = 128


def encode(values):
    largest = jnp.max(jnp.abs(values), axis=1, keepdims=True)
    logarithm = jnp.log2(jnp.maximum(largest, 2.0**-100))
    exponent = jnp.floor(logarithm * SCALE_STEPS) + 2.0
    scaled = values * (LARGEST * jnp.exp2(exponent * (-1.0 / SCALE_STEPS)))
    scaled = jnp.clip(scaled, -LARGEST, LARGEST)
    code = jnp.floor(scaled + 0.5).astype(jnp.int32)
    head = code[:, :LANES]
    lane = lax.broadcasted_iota(jnp.int32, head.shape, 1)
    stored = exponent.astype(jnp.int32) + SCALE_SHIFT
    stored = jnp.broadcast_to(stored, head.shape)
    bit = lax.shift_right_logical(stored, jnp.minimum(lane, SCALE_BITS)) & 1
    head = jnp.where(lane < SCALE_BITS, (head & -2) | bit, head)
    return head.astype(jnp.int16), code[:, LANES:].astype(jnp.int16)


def decode(code):
    code = code.astype(jnp.int32)
    head = code[:, :LANES]
    lane = lax.broadcasted_iota(jnp.int32, head.shape, 1)
    bits = lax.shift_left(head & 1, jnp.minimum(lane, SCALE_BITS))
    bits = jnp.where(lane < SCALE_BITS, bits, 0).astype(jnp.float32)
    stored = jnp.sum(bits, axis=1, keepdims=True)
    scale = jnp.exp2((stored - SCALE_SHIFT) * (1.0 / SCALE_STEPS)) * (1.0 / LARGEST)
    return code.astype(jnp.float32) * scale


def pick_kernel(tile_cd, amplitudes, *rest):
    outgoing, sems = rest[:-1], rest[-1]
    blk, grp = lax.axis_index("blk"), lax.axis_index("grp")
    copies = []
    for step, picked in enumerate(outgoing):
        cd = tile_cd[jnp.bitwise_xor(blk, step), grp]
        copies.append(pltpu.make_async_copy(amplitudes.at[cd], picked, sems.at[step]))
    for copy in copies:
        copy.start()
    for copy in copies:
        copy.wait()


def pick(tile_cd, amplitudes):
    columns = tile_cd.shape[0]
    block = jax.ShapeDtypeStruct(amplitudes.shape[1:], amplitudes.dtype)
    return pl.pallas_call(
        pick_kernel,
        out_shape=[block] * columns,
        in_specs=[pl.BlockSpec(memory_space=pltpu.SMEM), pl.BlockSpec(memory_space=pl.ANY)],
        out_specs=[pl.BlockSpec(memory_space=pltpu.VMEM)] * columns,
        scratch_shapes=[pltpu.SemaphoreType.DMA((columns,))],
        name="pick_cd_blocks",
    )(tile_cd, amplitudes)


def product_kernel(rows, tile, *rest):
    outgoing, product = rest[:-1], rest[-1]
    grp = lax.axis_index("grp")
    owner_rows = outgoing[0].shape[0]
    product[...] = jnp.dot(rows[...], tile[0], preferred_element_type=jnp.float32)
    for step, coded in enumerate(outgoing):
        first = pl.multiple_of(jnp.bitwise_xor(grp, step) * owner_rows, owner_rows)
        head, tail = encode(product[pl.ds(first, owner_rows), :])
        coded[:, :LANES] = head
        coded[:, LANES:] = tail


def contract(rows, tile, owner_rows):
    group_rows, tile_width = rows.shape[0], tile.shape[2]
    owners = group_rows // owner_rows
    vmem = pl.BlockSpec(memory_space=pltpu.VMEM)
    return pl.pallas_call(
        product_kernel,
        out_shape=[jax.ShapeDtypeStruct((owner_rows, tile_width), jnp.int16)] * owners,
        in_specs=[vmem, vmem],
        out_specs=[vmem] * owners,
        scratch_shapes=[pltpu.VMEM((group_rows, tile_width), jnp.float32)],
        compiler_params=pltpu.CompilerParams(vmem_limit_bytes=32 * 1024 * 1024),
        cost_estimate=pl.CostEstimate(
            flops=2 * group_rows * tile.shape[1] * tile_width,
            bytes_accessed=2 * tile.shape[1] * tile_width,
            transcendentals=0,
        ),
        name="contract_group",
    )(rows, tile)


def add_kernel(pieces, tile_ab, tile_cd, pair_screen, *rest):
    blocks, (residual_in, residual, held, in_sems, out_sems) = rest[:-5], rest[-5:]
    blk, grp = lax.axis_index("blk"), lax.axis_index("grp")
    ab_tiles = residual.shape[0]
    columns, grp_count = tile_ab.shape
    bounds = [ab_tiles * piece // pieces for piece in range(pieces + 1)]
    parts = [pl.ds(low, high - low) for low, high in zip(bounds[:-1], bounds[1:])]
    arrivals = [pltpu.make_async_copy(residual_in.at[part], held.at[part], in_sems.at[i]) for i, part in enumerate(parts)]
    leaves = [pltpu.make_async_copy(held.at[part], residual.at[part], out_sems.at[i]) for i, part in enumerate(parts)]
    for copy in arrivals:
        copy.start()
    for copy in arrivals:
        copy.wait()

    for index, coded in enumerate(blocks):
        p = jnp.bitwise_xor(blk, index // grp_count)
        g = jnp.bitwise_xor(grp, index % grp_count)

        @pl.when(pair_screen[tile_cd[p, g], grp] != 0)
        def _():
            ab = tile_ab[p, g]
            held[ab] = held[ab] + decode(coded[...])

    for copy in leaves:
        copy.start()
    for copy in leaves:
        copy.wait()


def add_blocks(tile_ab, tile_cd, pair_screen, blocks, residual_in):
    pieces = 5
    smem = pl.BlockSpec(memory_space=pltpu.SMEM)
    vmem = pl.BlockSpec(memory_space=pltpu.VMEM)
    return pl.pallas_call(
        lambda *refs: add_kernel(pieces, *refs),
        out_shape=jax.ShapeDtypeStruct(residual_in.shape, residual_in.dtype),
        in_specs=[smem, smem, smem] + [vmem] * len(blocks) + [pl.BlockSpec(memory_space=pl.ANY)],
        out_specs=pl.BlockSpec(memory_space=pl.ANY),
        scratch_shapes=[
            pltpu.VMEM(residual_in.shape, residual_in.dtype),
            pltpu.SemaphoreType.DMA((pieces,)),
            pltpu.SemaphoreType.DMA((pieces,)),
        ],
        compiler_params=pltpu.CompilerParams(vmem_limit_bytes=32 * 1024 * 1024),
        name="add_contributions",
    )(tile_ab, tile_cd, pair_screen, *blocks, residual_in)


def shards(amplitudes, pair_screen, integrals, tile_ab, tile_cd, residual_in):
    blk_count = lax.axis_size("blk")
    grp_count = lax.axis_size("grp")
    owner_rows = residual_in.shape[0]

    def swap(value, blk_step, grp_step):
        step = blk_step * grp_count + grp_step
        pairs = [(device, device ^ step) for device in range(blk_count * grp_count)]
        return lax.ppermute(value, ("blk", "grp"), pairs)

    picked = pick(tile_cd, amplitudes)
    rows_in = [picked[0]] + [swap(picked[step], step, 0) for step in range(1, blk_count)]
    blocks = []
    for blk_step in range(blk_count):
        coded = contract(rows_in[blk_step], integrals, owner_rows)
        arrived = {}
        for grp_step in reversed(range(grp_count)):
            own = blk_step == 0 and grp_step == 0
            arrived[grp_step] = coded[grp_step] if own else swap(coded[grp_step], blk_step, grp_step)
        blocks += [arrived[grp_step] for grp_step in range(grp_count)]
    by_tile = jnp.transpose(residual_in, (1, 0, 2))
    return jnp.transpose(add_blocks(tile_ab, tile_cd, pair_screen, blocks, by_tile), (1, 0, 2))


def solution(mesh):
    in_specs = (
        P(None, "blk", None),
        P(None, "blk"),
        P(("blk", "grp"), None, None),
        P(),
        P(),
        P(("blk", "grp"), None, None),
    )
    out_specs = P(("blk", "grp"), None, None)
    return jax.shard_map(shards, mesh=mesh, in_specs=in_specs, out_specs=out_specs, check_vma=False)
```

```python
import jax
import jax.numpy as jnp
from jax import lax
from jax.experimental import pallas as pl
from jax.experimental.pallas import tpu as pltpu
from jax.sharding import PartitionSpec as P

LARGEST = 32766.0
SCALE_STEPS = 64.0
SCALE_SHIFT = 8192
SCALE_BITS = 16
LANES = 128
CORES = 2


def encode(values):
    largest = jnp.max(jnp.abs(values), axis=1, keepdims=True)
    logarithm = jnp.log2(jnp.maximum(largest, 2.0**-100))
    exponent = jnp.floor(logarithm * SCALE_STEPS) + 2.0
    scaled = values * (LARGEST * jnp.exp2(exponent * (-1.0 / SCALE_STEPS)))
    scaled = jnp.clip(scaled, -LARGEST, LARGEST)
    code = jnp.floor(scaled + 0.5).astype(jnp.int32)
    head = code[:, :LANES]
    lane = lax.broadcasted_iota(jnp.int32, head.shape, 1)
    stored = exponent.astype(jnp.int32) + SCALE_SHIFT
    stored = jnp.broadcast_to(stored, head.shape)
    bit = lax.shift_right_logical(stored, jnp.minimum(lane, SCALE_BITS)) & 1
    head = jnp.where(lane < SCALE_BITS, (head & -2) | bit, head)
    return head.astype(jnp.int16), code[:, LANES:].astype(jnp.int16)


def decode(code):
    code = code.astype(jnp.int32)
    head = code[:, :LANES]
    lane = lax.broadcasted_iota(jnp.int32, head.shape, 1)
    bits = lax.shift_left(head & 1, jnp.minimum(lane, SCALE_BITS))
    bits = jnp.where(lane < SCALE_BITS, bits, 0).astype(jnp.float32)
    stored = jnp.sum(bits, axis=1, keepdims=True)
    scale = jnp.exp2((stored - SCALE_SHIFT) * (1.0 / SCALE_STEPS)) * (1.0 / LARGEST)
    return code.astype(jnp.float32) * scale


def pick_kernel(tile_cd, amplitudes, *rest):
    outgoing, sems = rest[:-1], rest[-1]
    blk, grp = lax.axis_index("blk"), lax.axis_index("grp")
    copies = []
    for step, picked in enumerate(outgoing):
        cd = tile_cd[jnp.bitwise_xor(blk, step), grp]
        copies.append(pltpu.make_async_copy(amplitudes.at[cd], picked, sems.at[step]))
    for copy in copies:
        copy.start()
    for copy in copies:
        copy.wait()


def pick(tile_cd, amplitudes):
    columns = tile_cd.shape[0]
    block = jax.ShapeDtypeStruct(amplitudes.shape[1:], amplitudes.dtype)
    return pl.pallas_call(
        pick_kernel,
        out_shape=[block] * columns,
        in_specs=[pl.BlockSpec(memory_space=pltpu.SMEM), pl.BlockSpec(memory_space=pl.ANY)],
        out_specs=[pl.BlockSpec(memory_space=pltpu.VMEM)] * columns,
        scratch_shapes=[pltpu.SemaphoreType.DMA((columns,))],
        name="pick_cd_blocks",
    )(tile_cd, amplitudes)


def product_kernel(rows, tile, *rest):
    outgoing, product = rest[:-1], rest[-1]
    grp = lax.axis_index("grp")
    chip_rows = outgoing[0].shape[0]
    product[...] = jnp.dot(rows[...], tile[0], preferred_element_type=jnp.float32)
    for step, coded in enumerate(outgoing):
        chip = jnp.bitwise_xor(grp // CORES, step)
        first = pl.multiple_of(chip * chip_rows, chip_rows)
        head, tail = encode(product[pl.ds(first, chip_rows), :])
        coded[:, :LANES] = head
        coded[:, LANES:] = tail


def contract(rows, tile, chip_rows):
    group_rows, tile_width = rows.shape[0], tile.shape[2]
    chips = group_rows // chip_rows
    vmem = pl.BlockSpec(memory_space=pltpu.VMEM)
    return pl.pallas_call(
        product_kernel,
        out_shape=[jax.ShapeDtypeStruct((chip_rows, tile_width), jnp.int16)] * chips,
        in_specs=[vmem, vmem],
        out_specs=[vmem] * chips,
        scratch_shapes=[pltpu.VMEM((group_rows, tile_width), jnp.float32)],
        compiler_params=pltpu.CompilerParams(vmem_limit_bytes=32 * 1024 * 1024),
        cost_estimate=pl.CostEstimate(
            flops=2 * group_rows * tile.shape[1] * tile_width,
            bytes_accessed=2 * tile.shape[1] * tile_width,
            transcendentals=0,
        ),
        name="contract_group",
    )(rows, tile)


def other_core_kernel(*refs):
    blocks, (halves, sems) = refs[:-2], refs[-2:]
    owner_rows = blocks[0].shape[0] // CORES
    other = 1 - lax.axis_index("grp") % CORES
    first = pl.multiple_of(other * owner_rows, owner_rows)
    copies = []
    for index, coded in enumerate(blocks):
        place = halves.at[pl.ds(index * owner_rows, owner_rows)]
        copies.append(pltpu.make_async_copy(coded.at[pl.ds(first, owner_rows)], place, sems.at[index]))
    for copy in copies:
        copy.start()
    for copy in copies:
        copy.wait()


def other_core_rows(blocks):
    chip_rows, tile_width = blocks[0].shape
    vmem = pl.BlockSpec(memory_space=pltpu.VMEM)
    return pl.pallas_call(
        other_core_kernel,
        out_shape=jax.ShapeDtypeStruct((len(blocks) * chip_rows // CORES, tile_width), blocks[0].dtype),
        in_specs=[vmem] * len(blocks),
        out_specs=vmem,
        scratch_shapes=[pltpu.SemaphoreType.DMA((len(blocks),))],
        name="rows_of_other_core",
    )(*blocks)


def add_kernel(pieces, tile_ab, tile_cd, pair_screen, *rest):
    blocks, (swapped, residual_in, residual, held, in_sems, out_sems) = rest[:-6], rest[-6:]
    blk, grp = lax.axis_index("blk"), lax.axis_index("grp")
    ab_tiles, owner_rows, _ = residual.shape
    chips = tile_ab.shape[1] // CORES
    bounds = [ab_tiles * piece // pieces for piece in range(pieces + 1)]
    parts = [pl.ds(low, high - low) for low, high in zip(bounds[:-1], bounds[1:])]
    arrivals = [pltpu.make_async_copy(residual_in.at[part], held.at[part], in_sems.at[i]) for i, part in enumerate(parts)]
    leaves = [pltpu.make_async_copy(held.at[part], residual.at[part], out_sems.at[i]) for i, part in enumerate(parts)]
    for copy in arrivals:
        copy.start()
    for copy in arrivals:
        copy.wait()

    def add_tile(p, g, rows):
        @pl.when(pair_screen[tile_cd[p, g], grp] != 0)
        def _():
            ab = tile_ab[p, g]
            held[ab] = held[ab] + decode(rows())

    own_first = pl.multiple_of(grp % CORES * owner_rows, owner_rows)
    for index, coded in enumerate(blocks):
        p = jnp.bitwise_xor(blk, index // chips)
        g = jnp.bitwise_xor(grp, index % chips * CORES)
        add_tile(p, g, lambda: coded[pl.ds(own_first, owner_rows), :])
        add_tile(p, jnp.bitwise_xor(g, 1), lambda: swapped[pl.ds(index * owner_rows, owner_rows), :])

    for copy in leaves:
        copy.start()
    for copy in leaves:
        copy.wait()


def add_blocks(tile_ab, tile_cd, pair_screen, blocks, swapped, residual_in):
    pieces = 5
    smem = pl.BlockSpec(memory_space=pltpu.SMEM)
    vmem = pl.BlockSpec(memory_space=pltpu.VMEM)
    return pl.pallas_call(
        lambda *refs: add_kernel(pieces, *refs),
        out_shape=jax.ShapeDtypeStruct(residual_in.shape, residual_in.dtype),
        in_specs=[smem, smem, smem] + [vmem] * (len(blocks) + 1) + [pl.BlockSpec(memory_space=pl.ANY)],
        out_specs=pl.BlockSpec(memory_space=pl.ANY),
        scratch_shapes=[
            pltpu.VMEM(residual_in.shape, residual_in.dtype),
            pltpu.SemaphoreType.DMA((pieces,)),
            pltpu.SemaphoreType.DMA((pieces,)),
        ],
        compiler_params=pltpu.CompilerParams(vmem_limit_bytes=32 * 1024 * 1024),
        name="add_contributions",
    )(tile_ab, tile_cd, pair_screen, *blocks, swapped, residual_in)


def shards(amplitudes, pair_screen, integrals, tile_ab, tile_cd, residual_in):
    blk_count = lax.axis_size("blk")
    grp_count = lax.axis_size("grp")
    owner_rows = residual_in.shape[0]

    def swap(value, blk_step, grp_step):
        step = blk_step * grp_count + grp_step
        pairs = [(device, device ^ step) for device in range(blk_count * grp_count)]
        return lax.ppermute(value, ("blk", "grp"), pairs)

    picked = pick(tile_cd, amplitudes)
    rows_in = [picked[0]] + [swap(picked[step], step, 0) for step in range(1, blk_count)]
    blocks = []
    chips = grp_count // CORES
    for blk_step in range(blk_count):
        coded = contract(rows_in[blk_step], integrals, CORES * owner_rows)
        arrived = {}
        for chip_step in reversed(range(chips)):
            own = blk_step == 0 and chip_step == 0
            arrived[chip_step] = coded[chip_step] if own else swap(coded[chip_step], blk_step, CORES * chip_step)
        blocks += [arrived[chip_step] for chip_step in range(chips)]
    swapped = swap(other_core_rows(blocks), 0, 1)
    by_tile = jnp.transpose(residual_in, (1, 0, 2))
    return jnp.transpose(add_blocks(tile_ab, tile_cd, pair_screen, blocks, swapped, by_tile), (1, 0, 2))


def solution(mesh):
    in_specs = (
        P(None, "blk", None),
        P(None, "blk"),
        P(("blk", "grp"), None, None),
        P(),
        P(),
        P(("blk", "grp"), None, None),
    )
    out_specs = P(("blk", "grp"), None, None)
    return jax.shard_map(shards, mesh=mesh, in_specs=in_specs, out_specs=out_specs, check_vma=False)
```

```python
import math

import jax
import jax.numpy as jnp
from jax import lax
from jax.experimental import pallas as pl
from jax.experimental.pallas import tpu as pltpu
from jax.sharding import PartitionSpec as P

LARGEST = 32766.0
SCALE_STEPS = 64.0
SCALE_SHIFT = 8192
SCALE_BITS = 16
LANES = 128
MEBIBYTE = 1 << 20
SMEM = pl.BlockSpec(memory_space=pltpu.SMEM)
VMEM = pl.BlockSpec(memory_space=pltpu.VMEM)


def vmem_limit(*arrays):
    total = sum(math.prod(array.shape) * jnp.dtype(array.dtype).itemsize for array in arrays)
    return pltpu.CompilerParams(vmem_limit_bytes=total + 4 * MEBIBYTE)


def encode(values):
    largest = jnp.max(jnp.abs(values), axis=1, keepdims=True)
    logarithm = jnp.log2(jnp.maximum(largest, 2.0**-100))
    exponent = jnp.floor(logarithm * SCALE_STEPS) + 2.0
    scaled = values * (LARGEST * jnp.exp2(exponent * (-1.0 / SCALE_STEPS)))
    scaled = jnp.clip(scaled, -LARGEST, LARGEST)
    code = jnp.floor(scaled + 0.5).astype(jnp.int32)
    head = code[:, :LANES]
    lane = lax.broadcasted_iota(jnp.int32, head.shape, 1)
    stored = exponent.astype(jnp.int32) + SCALE_SHIFT
    stored = jnp.broadcast_to(stored, head.shape)
    bit = lax.shift_right_logical(stored, jnp.minimum(lane, SCALE_BITS)) & 1
    head = jnp.where(lane < SCALE_BITS, (head & -2) | bit, head)
    return head.astype(jnp.int16), code[:, LANES:].astype(jnp.int16)


def row_scale(head):
    head = head.astype(jnp.int32)
    lane = lax.broadcasted_iota(jnp.int32, head.shape, 1)
    bits = lax.shift_left(head & 1, jnp.minimum(lane, SCALE_BITS))
    bits = jnp.where(lane < SCALE_BITS, bits, 0).astype(jnp.float32)
    stored = jnp.broadcast_to(jnp.sum(bits, axis=1, keepdims=True), head.shape)
    return jnp.exp2((stored - SCALE_SHIFT) * (1.0 / SCALE_STEPS)) * (1.0 / LARGEST)


def pick_kernel(tile_cd, amplitudes, *rest):
    outgoing, sems = rest[:-1], rest[-1]
    blk, grp = lax.axis_index("blk"), lax.axis_index("grp")
    copies = []
    for step, picked in enumerate(outgoing):
        cd = tile_cd[jnp.bitwise_xor(blk, step), grp]
        copies.append(pltpu.make_async_copy(amplitudes.at[cd], picked, sems.at[step]))
    for copy in copies:
        copy.start()
    for copy in copies:
        copy.wait()


def pick(tile_cd, amplitudes):
    columns = tile_cd.shape[0]
    block = jax.ShapeDtypeStruct(amplitudes.shape[1:], amplitudes.dtype)
    return pl.pallas_call(
        pick_kernel,
        out_shape=[block] * columns,
        in_specs=[SMEM, pl.BlockSpec(memory_space=pl.ANY)],
        out_specs=[VMEM] * columns,
        scratch_shapes=[pltpu.SemaphoreType.DMA((columns,))],
        compiler_params=vmem_limit(*[block] * columns),
        name="pick_cd_blocks",
    )(tile_cd, amplitudes)


def code_rows(rows, tile, product, coded, first):
    group_rows = rows.shape[0]
    product[...] = jnp.dot(rows[...], tile[0], preferred_element_type=jnp.float32)
    for part in range(0, group_rows, 16):
        head, tail = encode(product[part : part + 16, :])
        place = pl.ds(first + part, 16)
        coded[place, :LANES] = head
        coded[place, LANES:] = tail


def early_kernel(*refs):
    groups, (tile, coded, product) = refs[:-3], refs[-3:]
    for index, rows in enumerate(groups):
        code_rows(rows, tile, product, coded, index * rows.shape[0])


def last_kernel(rows, tile, early, coded, product):
    blk = lax.axis_index("blk")
    group_rows = rows.shape[0]
    groups = coded.shape[0] // group_rows
    for step in range(groups - 1):
        first = pl.multiple_of(jnp.bitwise_xor(blk, step) * group_rows, group_rows)
        coded[pl.ds(first, group_rows), :] = early[step * group_rows : (step + 1) * group_rows, :]
    first = pl.multiple_of(jnp.bitwise_xor(blk, groups - 1) * group_rows, group_rows)
    code_rows(rows, tile, product, coded, first)


def cost(rows, tile):
    flops = 2 * rows * tile.shape[1] * tile.shape[2]
    return pl.CostEstimate(flops=flops, bytes_accessed=2 * tile.shape[1] * tile.shape[2], transcendentals=0)


def contract_early(groups, tile):
    group_rows, tile_width = groups[0].shape[0], tile.shape[2]
    coded = jax.ShapeDtypeStruct((len(groups) * group_rows, tile_width), jnp.int16)
    product = jax.ShapeDtypeStruct((group_rows, tile_width), jnp.float32)
    return pl.pallas_call(
        early_kernel,
        out_shape=coded,
        in_specs=[VMEM] * (len(groups) + 1),
        out_specs=VMEM,
        scratch_shapes=[pltpu.VMEM(product.shape, product.dtype)],
        compiler_params=vmem_limit(*groups, tile, coded, product),
        cost_estimate=cost(len(groups) * group_rows, tile),
        name="contract_early_groups",
    )(*groups, tile)


def contract_last(rows, tile, early):
    group_rows, tile_width = rows.shape[0], tile.shape[2]
    coded = jax.ShapeDtypeStruct((early.shape[0] + group_rows, tile_width), early.dtype)
    product = jax.ShapeDtypeStruct((group_rows, tile_width), jnp.float32)
    return pl.pallas_call(
        last_kernel,
        out_shape=coded,
        in_specs=[VMEM] * 3,
        out_specs=VMEM,
        scratch_shapes=[pltpu.VMEM(product.shape, product.dtype)],
        compiler_params=vmem_limit(rows, tile, early, coded, product),
        cost_estimate=cost(group_rows, tile),
        name="contract_last_group",
    )(rows, tile, early)


def add_kernel(pieces, tile_ab, tile_cd, pair_screen, arrived, residual_in, residual, held, sems):
    grp = lax.axis_index("grp")
    ab_tiles, _, tile_width = residual.shape
    columns, grp_count = tile_ab.shape
    bounds = [ab_tiles * piece // pieces for piece in range(pieces + 1)]
    parts = [pl.ds(low, high - low) for low, high in zip(bounds[:-1], bounds[1:])]
    leaves = [pltpu.make_async_copy(held.at[part], residual.at[part], sems.at[i]) for i, part in enumerate(parts)]

    def hold(ab, carry):
        held[ab] = residual_in[ab]
        return carry

    lax.fori_loop(0, ab_tiles, hold, 0)

    def add_group(p, carry):
        scales = []
        for g in range(grp_count):
            kept = pair_screen[tile_cd[p, g], grp].astype(jnp.float32)
            scales.append(row_scale(arrived[p * grp_count + g, :, :LANES]) * kept)
        for g in range(grp_count):
            ab = tile_ab[p, g]
            for lane in range(0, tile_width, LANES):
                code = arrived[p * grp_count + g, :, lane : lane + LANES]
                term = code.astype(jnp.float32) * scales[g]
                held[ab, :, lane : lane + LANES] = held[ab, :, lane : lane + LANES] + term
        return carry

    lax.fori_loop(0, columns, add_group, 0)
    for copy in leaves:
        copy.start()
    for copy in leaves:
        copy.wait()


def add_blocks(tile_ab, tile_cd, pair_screen, arrived, residual_in):
    pieces = 5
    return pl.pallas_call(
        lambda *refs: add_kernel(pieces, *refs),
        out_shape=jax.ShapeDtypeStruct(residual_in.shape, residual_in.dtype),
        in_specs=[SMEM] * 3 + [VMEM] * 2,
        out_specs=pl.BlockSpec(memory_space=pl.ANY),
        scratch_shapes=[pltpu.VMEM(residual_in.shape, residual_in.dtype), pltpu.SemaphoreType.DMA((pieces,))],
        compiler_params=vmem_limit(arrived, residual_in, residual_in),
        name="add_contributions",
    )(tile_ab, tile_cd, pair_screen, arrived, residual_in)


def shards(amplitudes, pair_screen, integrals, tile_ab, tile_cd, residual_in):
    blk_count = lax.axis_size("blk")
    grp_count = lax.axis_size("grp")
    owner_rows, _, tile_width = residual_in.shape

    def swap(value, step):
        return lax.ppermute(value, "blk", [(b, b ^ step) for b in range(blk_count)])

    picked = pick(tile_cd, amplitudes)
    rows_in = [picked[0]] + [swap(picked[step], step) for step in range(1, blk_count)]
    early = contract_early(rows_in[:-1], integrals)
    coded = contract_last(rows_in[-1], integrals, early)
    coded = coded.reshape(blk_count * grp_count, owner_rows, tile_width)
    arrived = lax.all_to_all(coded, ("blk", "grp"), split_axis=0, concat_axis=0, tiled=True)
    by_tile = jnp.transpose(residual_in, (1, 0, 2))
    return jnp.transpose(add_blocks(tile_ab, tile_cd, pair_screen, arrived, by_tile), (1, 0, 2))


def solution(mesh):
    in_specs = (
        P(None, "blk", None),
        P(None, "blk"),
        P(("blk", "grp"), None, None),
        P(),
        P(),
        P(("blk", "grp"), None, None),
    )
    out_specs = P(("blk", "grp"), None, None)
    return jax.shard_map(shards, mesh=mesh, in_specs=in_specs, out_specs=out_specs, check_vma=False)
```

```python
import math

import jax
import jax.numpy as jnp
from jax import lax
from jax.experimental import pallas as pl
from jax.experimental.pallas import tpu as pltpu
from jax.sharding import PartitionSpec as P

LARGEST = 32766.0
SCALE_STEPS = 64.0
SCALE_SHIFT = 8192
SCALE_BITS = 16
LANES = 128
CORES = 2
MEBIBYTE = 1 << 20
SMEM = pl.BlockSpec(memory_space=pltpu.SMEM)
VMEM = pl.BlockSpec(memory_space=pltpu.VMEM)
ANY = pl.BlockSpec(memory_space=pl.ANY)


def vmem_limit(*arrays):
    total = sum(math.prod(array.shape) * jnp.dtype(array.dtype).itemsize for array in arrays)
    return pltpu.CompilerParams(vmem_limit_bytes=total + 4 * MEBIBYTE)


def encode(values):
    largest = jnp.max(jnp.abs(values), axis=1, keepdims=True)
    logarithm = jnp.log2(jnp.maximum(largest, 2.0**-100))
    exponent = jnp.floor(logarithm * SCALE_STEPS) + 2.0
    scaled = values * (LARGEST * jnp.exp2(exponent * (-1.0 / SCALE_STEPS)))
    scaled = jnp.clip(scaled, -LARGEST, LARGEST)
    code = jnp.floor(scaled + 0.5).astype(jnp.int32)
    head = code[:, :LANES]
    lane = lax.broadcasted_iota(jnp.int32, head.shape, 1)
    stored = exponent.astype(jnp.int32) + SCALE_SHIFT
    stored = jnp.broadcast_to(stored, head.shape)
    bit = lax.shift_right_logical(stored, jnp.minimum(lane, SCALE_BITS)) & 1
    head = jnp.where(lane < SCALE_BITS, (head & -2) | bit, head)
    return head.astype(jnp.int16), code[:, LANES:].astype(jnp.int16)


def row_scale(head):
    head = head.astype(jnp.int32)
    lane = lax.broadcasted_iota(jnp.int32, head.shape, 1)
    bits = lax.shift_left(head & 1, jnp.minimum(lane, SCALE_BITS))
    bits = jnp.where(lane < SCALE_BITS, bits, 0).astype(jnp.float32)
    stored = jnp.broadcast_to(jnp.sum(bits, axis=1, keepdims=True), head.shape)
    return jnp.exp2((stored - SCALE_SHIFT) * (1.0 / SCALE_STEPS)) * (1.0 / LARGEST)


def cost(rows, tile):
    flops = 2 * rows * tile.shape[-2] * tile.shape[-1]
    return pl.CostEstimate(flops=flops, bytes_accessed=2 * tile.shape[-2] * tile.shape[-1], transcendentals=0)


def start_all(copies):
    for copy in copies:
        copy.start()


def wait_all(copies):
    for copy in copies:
        copy.wait()


def pick_kernel(tile_cd, amplitudes, *rest):
    outgoing, sems = rest[:-1], rest[-1]
    blk, grp = lax.axis_index("blk"), lax.axis_index("grp")
    copies = []
    for step, picked in enumerate(outgoing):
        cd = tile_cd[jnp.bitwise_xor(blk, step), grp]
        copies.append(pltpu.make_async_copy(amplitudes.at[cd], picked, sems.at[step]))
    start_all(copies)
    wait_all(copies)


def pick(tile_cd, amplitudes):
    groups = tile_cd.shape[0]
    block = jax.ShapeDtypeStruct(amplitudes.shape[1:], amplitudes.dtype)
    return pl.pallas_call(
        pick_kernel,
        out_shape=[block] * groups,
        in_specs=[SMEM, ANY],
        out_specs=[VMEM] * groups,
        scratch_shapes=[pltpu.SemaphoreType.DMA((groups,))],
        compiler_params=vmem_limit(*[block] * groups),
        name="pick_cd_blocks",
    )(tile_cd, amplitudes)


def code_chips(rows, tile, product, outgoing, first):
    product[...] = jnp.dot(rows[...], tile[...], preferred_element_type=jnp.float32)
    chip_rows = product.shape[0] // len(outgoing)
    chip = lax.axis_index("grp") // CORES
    for step, coded in enumerate(outgoing):
        source = pl.multiple_of(jnp.bitwise_xor(chip, step) * chip_rows, chip_rows)
        code, tail = encode(product[pl.ds(source, chip_rows), :])
        coded[first : first + chip_rows, :LANES] = code
        coded[first : first + chip_rows, LANES:] = tail


def own_kernel(rows, far_picked, tile, *rest):
    outgoing, (far_rows, product) = rest[:-2], rest[-2:]
    far_rows[...] = far_picked[...]
    code_chips(rows, tile, product, outgoing, 0)


def contract_own(rows, far_picked, tile, chips):
    group_rows, tile_width = rows.shape[0], tile.shape[1]
    coded = jax.ShapeDtypeStruct((group_rows // chips, tile_width), jnp.int16)
    product = jax.ShapeDtypeStruct((group_rows, tile_width), jnp.float32)
    outputs = [coded] * chips + [jax.ShapeDtypeStruct(rows.shape, rows.dtype)]
    return pl.pallas_call(
        own_kernel,
        out_shape=outputs,
        in_specs=[VMEM] * 3,
        out_specs=[VMEM] * len(outputs),
        scratch_shapes=[pltpu.VMEM(product.shape, product.dtype)],
        compiler_params=vmem_limit(rows, far_picked, tile, *outputs, product),
        cost_estimate=cost(group_rows, tile),
        name="contract_own_group",
    )(rows, far_picked, tile)


def near_kernel(near, *refs):
    groups, tile, outgoing, product = refs[:near], refs[near], refs[near + 1 : -1], refs[-1]
    chip_rows = product.shape[0] // len(outgoing)
    for index, rows in enumerate(groups):
        code_chips(rows, tile, product, outgoing, index * chip_rows)


def contract_near(groups, tile, chips):
    group_rows, tile_width = groups[0].shape[0], tile.shape[1]
    coded = jax.ShapeDtypeStruct((len(groups) * group_rows // chips, tile_width), jnp.int16)
    product = jax.ShapeDtypeStruct((group_rows, tile_width), jnp.float32)
    return pl.pallas_call(
        lambda *refs: near_kernel(len(groups), *refs),
        out_shape=[coded] * chips,
        in_specs=[VMEM] * (len(groups) + 1),
        out_specs=[VMEM] * chips,
        scratch_shapes=[pltpu.VMEM(product.shape, product.dtype)],
        compiler_params=vmem_limit(*groups, tile, *[coded] * chips, product),
        cost_estimate=cost(len(groups) * group_rows, tile),
        name="contract_near_groups",
    )(*groups, tile)


def far_kernel(chips, rows, tile, *rest):
    coded, product = rest[-2:]
    chip_rows = product.shape[0] // chips
    parts = [coded.at[pl.ds(step * chip_rows, chip_rows)] for step in range(chips)]
    code_chips(rows, tile, product, parts, 0)


def contract_far(rows, tile, chips, earlier):
    coded = jax.ShapeDtypeStruct((rows.shape[0], tile.shape[1]), jnp.int16)
    product = jax.ShapeDtypeStruct(coded.shape, jnp.float32)
    return pl.pallas_call(
        lambda *refs: far_kernel(chips, *refs),
        out_shape=coded,
        in_specs=[VMEM] * 2 + [ANY] * len(earlier),
        out_specs=VMEM,
        scratch_shapes=[pltpu.VMEM(product.shape, product.dtype)],
        compiler_params=vmem_limit(rows, tile, coded, product),
        cost_estimate=cost(rows.shape[0], tile),
        name="contract_far_group",
    )(rows, tile, *earlier)


def regroup_kernel(count, *refs):
    sources, targets = refs[:count], refs[count:]
    part_rows = sources[0].shape[0] // len(targets)
    for j, source in enumerate(sources):
        for i, target in enumerate(targets):
            target[j * part_rows : (j + 1) * part_rows, :] = source[i * part_rows : (i + 1) * part_rows, :]


def regroup(sources, parts, name):
    rows, tile_width = sources[0].shape
    target = jax.ShapeDtypeStruct((len(sources) * rows // parts, tile_width), sources[0].dtype)
    return pl.pallas_call(
        lambda *refs: regroup_kernel(len(sources), *refs),
        out_shape=[target] * parts,
        in_specs=[VMEM] * len(sources),
        out_specs=[VMEM] * parts,
        compiler_params=vmem_limit(*sources, *[target] * parts),
        name=name,
    )(*sources)


def pieces_of(arrays, owner_rows):
    return [(array, first) for array in arrays for first in range(0, array.shape[0], CORES * owner_rows)]


def other_core_kernel(owner_rows, *refs):
    arrays, halves = refs[:-1], refs[-1]
    other = 1 - lax.axis_index("grp") % CORES
    for index, (array, first) in enumerate(pieces_of(arrays, owner_rows)):
        source = pl.multiple_of(first + other * owner_rows, owner_rows)
        halves[index * owner_rows : (index + 1) * owner_rows, :] = array[pl.ds(source, owner_rows), :]


def other_core_rows(arrays, owner_rows):
    rows = sum(array.shape[0] for array in arrays) // CORES
    halves = jax.ShapeDtypeStruct((rows, arrays[0].shape[1]), arrays[0].dtype)
    return pl.pallas_call(
        lambda *refs: other_core_kernel(owner_rows, *refs),
        out_shape=halves,
        in_specs=[VMEM] * len(arrays),
        out_specs=VMEM,
        compiler_params=vmem_limit(*arrays, halves),
        name="rows_of_other_core",
    )(*arrays)


def add_kernel(parts, tile_ab, tile_cd, pair_screen, *rest):
    arrays, (swapped, residual_in, residual, held, sems) = rest[:-5], rest[-5:]
    blk, grp = lax.axis_index("blk"), lax.axis_index("grp")
    ab_tiles, owner_rows, tile_width = residual.shape
    chips = tile_ab.shape[1] // CORES
    bounds = [ab_tiles * part // parts for part in range(parts + 1)]
    spans = [pl.ds(low, high - low) for low, high in zip(bounds[:-1], bounds[1:])]
    leaves = [pltpu.make_async_copy(held.at[span], residual.at[span], sems.at[i]) for i, span in enumerate(spans)]

    def hold(ab, carry):
        held[ab] = residual_in[ab]
        return carry

    lax.fori_loop(0, ab_tiles, hold, 0)
    pieces = pieces_of(arrays, owner_rows)
    own = grp % CORES * owner_rows
    for start in range(0, len(pieces), chips):
        terms = []
        for index in range(start, start + chips):
            array, first = pieces[index]
            p = jnp.bitwise_xor(blk, index // chips)
            g = jnp.bitwise_xor(grp, index % chips * CORES)
            here = pl.ds(pl.multiple_of(first + own, owner_rows), owner_rows)
            there = pl.ds(index * owner_rows, owner_rows)
            for source, span, column in ((array, here, g), (swapped, there, jnp.bitwise_xor(g, 1))):
                kept = pair_screen[tile_cd[p, column], grp].astype(jnp.float32)
                scale = row_scale(source[span, :LANES]) * kept
                terms.append((source, span, scale, tile_ab[p, column]))
        for source, span, scale, ab in terms:
            for lane in range(0, tile_width, LANES):
                term = source[span, lane : lane + LANES].astype(jnp.float32) * scale
                held[ab, :, lane : lane + LANES] = held[ab, :, lane : lane + LANES] + term
    start_all(leaves)
    wait_all(leaves)


def add_blocks(tile_ab, tile_cd, pair_screen, arrays, swapped, residual_in):
    parts = 5
    return pl.pallas_call(
        lambda *refs: add_kernel(parts, *refs),
        out_shape=jax.ShapeDtypeStruct(residual_in.shape, residual_in.dtype),
        in_specs=[SMEM] * 3 + [VMEM] * (len(arrays) + 2),
        out_specs=ANY,
        scratch_shapes=[pltpu.VMEM(residual_in.shape, residual_in.dtype), pltpu.SemaphoreType.DMA((parts,))],
        compiler_params=vmem_limit(*arrays, swapped, residual_in, residual_in),
        name="add_contributions",
    )(tile_ab, tile_cd, pair_screen, *arrays, swapped, residual_in)


def shards(amplitudes, pair_screen, integrals, tile_ab, tile_cd, residual_in):
    blk_count = lax.axis_size("blk")
    grp_count = lax.axis_size("grp")
    chips = grp_count // CORES
    owner_rows = residual_in.shape[0]
    far = blk_count - 1

    def swap(value, blk_step, chip_step, core_step=0):
        step = blk_step * grp_count + chip_step * CORES + core_step
        pairs = [(device, device ^ step) for device in range(blk_count * grp_count)]
        return lax.ppermute(value, ("blk", "grp"), pairs)

    def along_chips(outgoing):
        arrived = {step: swap(outgoing[step], 0, step) for step in reversed(range(1, chips))}
        return [outgoing[0]] + [arrived[step] for step in range(1, chips)]

    tile = integrals[0]
    own_rows, *near_picked, far_picked = pick(tile_cd, amplitudes)
    near_rows = [swap(rows, index + 1, 0) for index, rows in enumerate(near_picked)]
    *own_out, far_picked = contract_own(own_rows, far_picked, tile, chips)
    own_in = along_chips(own_out)
    far_rows = swap(far_picked, far, 0)
    near_in = along_chips(contract_near(near_rows, tile, chips))
    near_back = regroup(near_in, blk_count - 2, "regroup_by_group")
    near_in = [swap(rows, index + 1, 0) for index, rows in enumerate(near_back)]
    far_back = swap(contract_far(far_rows, tile, chips, own_in[1:]), far, 0)
    far_in = along_chips(regroup([far_back], chips, "regroup_by_chip"))
    arrays = [*own_in, *near_in, *far_in]
    swapped = swap(other_core_rows(arrays, owner_rows), 0, 0, 1)
    by_tile = jnp.transpose(residual_in, (1, 0, 2))
    added = add_blocks(tile_ab, tile_cd, pair_screen, arrays, swapped, by_tile)
    return jnp.transpose(added, (1, 0, 2))


def solution(mesh):
    in_specs = (
        P(None, "blk", None),
        P(None, "blk"),
        P(("blk", "grp"), None, None),
        P(),
        P(),
        P(("blk", "grp"), None, None),
    )
    out_specs = P(("blk", "grp"), None, None)
    return jax.shard_map(shards, mesh=mesh, in_specs=in_specs, out_specs=out_specs, check_vma=False)
```

```python
import math

import jax
import jax.numpy as jnp
from jax import lax
from jax.experimental import pallas as pl
from jax.experimental.pallas import tpu as pltpu
from jax.sharding import PartitionSpec as P

LARGEST = 32766.0
SCALE_STEPS = 64.0
SCALE_SHIFT = 8192
SCALE_BITS = 16
LANES = 128
CORES = 2
MEBIBYTE = 1 << 20
SMEM = pl.BlockSpec(memory_space=pltpu.SMEM)
VMEM = pl.BlockSpec(memory_space=pltpu.VMEM)
ANY = pl.BlockSpec(memory_space=pl.ANY)


def vmem_limit(*arrays):
    total = sum(math.prod(array.shape) * jnp.dtype(array.dtype).itemsize for array in arrays)
    return pltpu.CompilerParams(vmem_limit_bytes=total + 4 * MEBIBYTE)


def encode(values):
    largest = jnp.max(jnp.abs(values), axis=1, keepdims=True)
    logarithm = jnp.log2(jnp.maximum(largest, 2.0**-100))
    exponent = jnp.floor(logarithm * SCALE_STEPS) + 2.0
    scaled = values * (LARGEST * jnp.exp2(exponent * (-1.0 / SCALE_STEPS)))
    scaled = jnp.clip(scaled, -LARGEST, LARGEST)
    code = jnp.floor(scaled + 0.5).astype(jnp.int32)
    head = code[:, :LANES]
    lane = lax.broadcasted_iota(jnp.int32, head.shape, 1)
    stored = exponent.astype(jnp.int32) + SCALE_SHIFT
    stored = jnp.broadcast_to(stored, head.shape)
    bit = lax.shift_right_logical(stored, jnp.minimum(lane, SCALE_BITS)) & 1
    head = jnp.where(lane < SCALE_BITS, (head & -2) | bit, head)
    return head.astype(jnp.int16), code[:, LANES:].astype(jnp.int16)


def row_scale(head):
    head = head.astype(jnp.int32)
    lane = lax.broadcasted_iota(jnp.int32, head.shape, 1)
    bits = lax.shift_left(head & 1, jnp.minimum(lane, SCALE_BITS))
    bits = jnp.where(lane < SCALE_BITS, bits, 0).astype(jnp.float32)
    stored = jnp.broadcast_to(jnp.sum(bits, axis=1, keepdims=True), head.shape)
    return jnp.exp2((stored - SCALE_SHIFT) * (1.0 / SCALE_STEPS)) * (1.0 / LARGEST)


def cost(rows, tile):
    flops = 2 * rows * tile.shape[-2] * tile.shape[-1]
    return pl.CostEstimate(flops=flops, bytes_accessed=2 * tile.shape[-2] * tile.shape[-1], transcendentals=0)


def blk_steps(blk_count, core):
    near = blk_count - 2
    steps = [slot + 1 + core * (near - 1 - 2 * slot) for slot in range(near)]
    return [0] + steps + [blk_count - 1]


def start_all(copies):
    for copy in copies:
        copy.start()


def wait_all(copies):
    for copy in copies:
        copy.wait()


def pick_kernel(tile_cd, amplitudes, *rest):
    outgoing, sems = rest[:-1], rest[-1]
    blk, grp = lax.axis_index("blk"), lax.axis_index("grp")
    copies = []
    for slot, step in enumerate(blk_steps(len(outgoing), grp % CORES)):
        cd = tile_cd[jnp.bitwise_xor(blk, step), grp]
        copies.append(pltpu.make_async_copy(amplitudes.at[cd], outgoing[slot], sems.at[slot]))
    start_all(copies)
    wait_all(copies)


def pick(tile_cd, amplitudes):
    groups = tile_cd.shape[0]
    block = jax.ShapeDtypeStruct(amplitudes.shape[1:], amplitudes.dtype)
    return pl.pallas_call(
        pick_kernel,
        out_shape=[block] * groups,
        in_specs=[SMEM, ANY],
        out_specs=[VMEM] * groups,
        scratch_shapes=[pltpu.SemaphoreType.DMA((groups,))],
        compiler_params=vmem_limit(*[block] * groups),
        name="pick_cd_blocks",
    )(tile_cd, amplitudes)


def code_chips(rows, tile, product, outgoing, first):
    product[...] = jnp.dot(rows[...], tile[...], preferred_element_type=jnp.float32)
    chip_rows = product.shape[0] // len(outgoing)
    chip = lax.axis_index("grp") // CORES
    for step, coded in enumerate(outgoing):
        source = pl.multiple_of(jnp.bitwise_xor(chip, step) * chip_rows, chip_rows)
        code, tail = encode(product[pl.ds(source, chip_rows), :])
        coded[first : first + chip_rows, :LANES] = code
        coded[first : first + chip_rows, LANES:] = tail


def own_kernel(rows, tile, far_picked, *rest):
    outgoing, (tile_out, far_out, product, sem) = rest[:-4], rest[-4:]
    copy = pltpu.make_async_copy(tile, tile_out, sem)
    copy.start()
    far_out[...] = far_picked[...]
    code_chips(rows, tile, product, outgoing, 0)
    copy.wait()


def contract_own(rows, tile, far_picked, chips):
    group_rows, tile_width = rows.shape[0], tile.shape[1]
    coded = jax.ShapeDtypeStruct((group_rows // chips, tile_width), jnp.int16)
    product = jax.ShapeDtypeStruct((group_rows, tile_width), jnp.float32)
    outputs = [coded] * chips + [jax.ShapeDtypeStruct(array.shape, array.dtype) for array in (tile, far_picked)]
    return pl.pallas_call(
        own_kernel,
        out_shape=outputs,
        in_specs=[VMEM] * 3,
        out_specs=[VMEM] * len(outputs),
        scratch_shapes=[pltpu.VMEM(product.shape, product.dtype), pltpu.SemaphoreType.DMA],
        compiler_params=vmem_limit(rows, tile, far_picked, *outputs, product),
        cost_estimate=cost(group_rows, tile),
        name="contract_own_group",
    )(rows, tile, far_picked)


def near_kernel(near, *refs):
    groups, tile, outgoing, product = refs[:near], refs[near], refs[near + 1 : -1], refs[-1]
    chip_rows = product.shape[0] // len(outgoing)
    for index, rows in enumerate(groups):
        code_chips(rows, tile, product, outgoing, index * chip_rows)


def contract_near(groups, tile, chips):
    group_rows, tile_width = groups[0].shape[0], tile.shape[1]
    coded = jax.ShapeDtypeStruct((len(groups) * group_rows // chips, tile_width), jnp.int16)
    product = jax.ShapeDtypeStruct((group_rows, tile_width), jnp.float32)
    return pl.pallas_call(
        lambda *refs: near_kernel(len(groups), *refs),
        out_shape=[coded] * chips,
        in_specs=[VMEM] * (len(groups) + 1),
        out_specs=[VMEM] * chips,
        scratch_shapes=[pltpu.VMEM(product.shape, product.dtype)],
        compiler_params=vmem_limit(*groups, tile, *[coded] * chips, product),
        cost_estimate=cost(len(groups) * group_rows, tile),
        name="contract_near_groups",
    )(*groups, tile)


def far_kernel(chips, rows, tile, *rest):
    coded, product = rest[-2:]
    chip_rows = product.shape[0] // chips
    parts = [coded.at[pl.ds(step * chip_rows, chip_rows)] for step in range(chips)]
    code_chips(rows, tile, product, parts, 0)


def contract_far(rows, tile, chips, earlier):
    coded = jax.ShapeDtypeStruct((rows.shape[0], tile.shape[1]), jnp.int16)
    product = jax.ShapeDtypeStruct(coded.shape, jnp.float32)
    return pl.pallas_call(
        lambda *refs: far_kernel(chips, *refs),
        out_shape=coded,
        in_specs=[VMEM] * 2 + [ANY] * len(earlier),
        out_specs=VMEM,
        scratch_shapes=[pltpu.VMEM(product.shape, product.dtype)],
        compiler_params=vmem_limit(rows, tile, coded, product),
        cost_estimate=cost(rows.shape[0], tile),
        name="contract_far_group",
    )(rows, tile, *earlier)


def regroup_kernel(count, *refs):
    sources, targets = refs[:count], refs[count:]
    part_rows = sources[0].shape[0] // len(targets)
    for j, source in enumerate(sources):
        for i, target in enumerate(targets):
            target[j * part_rows : (j + 1) * part_rows, :] = source[i * part_rows : (i + 1) * part_rows, :]


def regroup(sources, parts, name):
    rows, tile_width = sources[0].shape
    target = jax.ShapeDtypeStruct((len(sources) * rows // parts, tile_width), sources[0].dtype)
    return pl.pallas_call(
        lambda *refs: regroup_kernel(len(sources), *refs),
        out_shape=[target] * parts,
        in_specs=[VMEM] * len(sources),
        out_specs=[VMEM] * parts,
        compiler_params=vmem_limit(*sources, *[target] * parts),
        name=name,
    )(*sources)


def pieces_of(arrays, owner_rows):
    return [(array, first) for array in arrays for first in range(0, array.shape[0], CORES * owner_rows)]


def other_core_kernel(owner_rows, *refs):
    arrays, halves = refs[:-1], refs[-1]
    other = 1 - lax.axis_index("grp") % CORES
    for index, (array, first) in enumerate(pieces_of(arrays, owner_rows)):
        source = pl.multiple_of(first + other * owner_rows, owner_rows)
        halves[index * owner_rows : (index + 1) * owner_rows, :] = array[pl.ds(source, owner_rows), :]


def other_core_rows(arrays, owner_rows):
    rows = sum(array.shape[0] for array in arrays) // CORES
    halves = jax.ShapeDtypeStruct((rows, arrays[0].shape[1]), arrays[0].dtype)
    return pl.pallas_call(
        lambda *refs: other_core_kernel(owner_rows, *refs),
        out_shape=halves,
        in_specs=[VMEM] * len(arrays),
        out_specs=VMEM,
        compiler_params=vmem_limit(*arrays, halves),
        name="rows_of_other_core",
    )(*arrays)


def add_kernel(parts, tile_ab, tile_cd, pair_screen, *rest):
    arrays, (swapped, residual_in, residual, held, sems) = rest[:-5], rest[-5:]
    blk, grp = lax.axis_index("blk"), lax.axis_index("grp")
    ab_tiles, owner_rows, tile_width = residual.shape
    chips = tile_ab.shape[1] // CORES
    bounds = [ab_tiles * part // parts for part in range(parts + 1)]
    spans = [pl.ds(low, high - low) for low, high in zip(bounds[:-1], bounds[1:])]
    leaves = [pltpu.make_async_copy(held.at[span], residual.at[span], sems.at[i]) for i, span in enumerate(spans)]

    def hold(ab, carry):
        held[ab] = residual_in[ab]
        return carry

    lax.fori_loop(0, ab_tiles, hold, 0)
    pieces = pieces_of(arrays, owner_rows)
    core = grp % CORES
    steps_here, steps_there = blk_steps(tile_ab.shape[0], core), blk_steps(tile_ab.shape[0], 1 - core)
    own = core * owner_rows
    for start in range(0, len(pieces), chips):
        terms = []
        for index in range(start, start + chips):
            array, first = pieces[index]
            p_here = jnp.bitwise_xor(blk, steps_here[index // chips])
            p_there = jnp.bitwise_xor(blk, steps_there[index // chips])
            g = jnp.bitwise_xor(grp, index % chips * CORES)
            here = pl.ds(pl.multiple_of(first + own, owner_rows), owner_rows)
            there = pl.ds(index * owner_rows, owner_rows)
            for source, span, p, column in ((array, here, p_here, g), (swapped, there, p_there, jnp.bitwise_xor(g, 1))):
                kept = pair_screen[tile_cd[p, column], grp].astype(jnp.float32)
                scale = row_scale(source[span, :LANES]) * kept
                terms.append((source, span, scale, tile_ab[p, column]))
        for source, span, scale, ab in terms:
            for lane in range(0, tile_width, LANES):
                term = source[span, lane : lane + LANES].astype(jnp.float32) * scale
                held[ab, :, lane : lane + LANES] = held[ab, :, lane : lane + LANES] + term
    start_all(leaves)
    wait_all(leaves)


def add_blocks(tile_ab, tile_cd, pair_screen, arrays, swapped, residual_in):
    parts = 5
    return pl.pallas_call(
        lambda *refs: add_kernel(parts, *refs),
        out_shape=jax.ShapeDtypeStruct(residual_in.shape, residual_in.dtype),
        in_specs=[SMEM] * 3 + [VMEM] * (len(arrays) + 2),
        out_specs=ANY,
        scratch_shapes=[pltpu.VMEM(residual_in.shape, residual_in.dtype), pltpu.SemaphoreType.DMA((parts,))],
        compiler_params=vmem_limit(*arrays, swapped, residual_in, residual_in),
        name="add_contributions",
    )(tile_ab, tile_cd, pair_screen, *arrays, swapped, residual_in)


def shards(amplitudes, pair_screen, integrals, tile_ab, tile_cd, residual_in):
    blk_count = lax.axis_size("blk")
    grp_count = lax.axis_size("grp")
    chips = grp_count // CORES
    owner_rows = residual_in.shape[0]
    far = blk_count - 1

    def swap(value, slot, chip_step, core_step=0):
        pairs = []
        for device in range(blk_count * grp_count):
            blk_step = blk_steps(blk_count, device % CORES)[slot]
            pairs.append((device, device ^ (blk_step * grp_count + chip_step * CORES + core_step)))
        return lax.ppermute(value, ("blk", "grp"), pairs)

    def along_chips(outgoing):
        arrived = {step: swap(outgoing[step], 0, step) for step in reversed(range(1, chips))}
        return [outgoing[0]] + [arrived[step] for step in range(1, chips)]

    own_rows, *near_picked, far_picked = pick(tile_cd, amplitudes)
    near_rows = [swap(rows, index + 1, 0) for index, rows in enumerate(near_picked)]
    *own_out, tile, far_picked = contract_own(own_rows, integrals[0], far_picked, chips)
    own_in = along_chips(own_out)
    far_rows = swap(far_picked, far, 0)
    near_in = along_chips(contract_near(near_rows, tile, chips))
    near_back = regroup(near_in, blk_count - 2, "regroup_by_group")
    near_in = [swap(rows, index + 1, 0) for index, rows in enumerate(near_back)]
    far_back = swap(contract_far(far_rows, tile, chips, own_in[1:]), far, 0)
    far_in = along_chips(regroup([far_back], chips, "regroup_by_chip"))
    arrays = [*own_in, *near_in, *far_in]
    swapped = swap(other_core_rows(arrays, owner_rows), 0, 0, 1)
    by_tile = jnp.transpose(residual_in, (1, 0, 2))
    added = add_blocks(tile_ab, tile_cd, pair_screen, arrays, swapped, by_tile)
    return jnp.transpose(added, (1, 0, 2))


def solution(mesh):
    in_specs = (
        P(None, "blk", None),
        P(None, "blk"),
        P(("blk", "grp"), None, None),
        P(),
        P(),
        P(("blk", "grp"), None, None),
    )
    out_specs = P(("blk", "grp"), None, None)
    return jax.shard_map(shards, mesh=mesh, in_specs=in_specs, out_specs=out_specs, check_vma=False)
```

```python
import math

import jax
import jax.numpy as jnp
from jax import lax
from jax.experimental import pallas as pl
from jax.experimental.pallas import tpu as pltpu
from jax.sharding import PartitionSpec as P

LARGEST = 32766.0
SCALE_STEPS = 64.0
SCALE_SHIFT = 8192
SCALE_BITS = 16
LANES = 128
CORES = 2
MEBIBYTE = 1 << 20
SMEM = pl.BlockSpec(memory_space=pltpu.SMEM)
VMEM = pl.BlockSpec(memory_space=pltpu.VMEM)
ANY = pl.BlockSpec(memory_space=pl.ANY)


def vmem_limit(*arrays):
    total = sum(math.prod(array.shape) * jnp.dtype(array.dtype).itemsize for array in arrays)
    return pltpu.CompilerParams(vmem_limit_bytes=total + 4 * MEBIBYTE)


def encode(values):
    largest = jnp.max(jnp.abs(values), axis=1, keepdims=True)
    logarithm = jnp.log2(jnp.maximum(largest, 2.0**-100))
    exponent = jnp.floor(logarithm * SCALE_STEPS) + 2.0
    scaled = values * (LARGEST * jnp.exp2(exponent * (-1.0 / SCALE_STEPS)))
    scaled = jnp.clip(scaled, -LARGEST, LARGEST)
    code = jnp.floor(scaled + 0.5).astype(jnp.int32)
    head = code[:, :LANES]
    lane = lax.broadcasted_iota(jnp.int32, head.shape, 1)
    stored = exponent.astype(jnp.int32) + SCALE_SHIFT
    stored = jnp.broadcast_to(stored, head.shape)
    bit = lax.shift_right_logical(stored, jnp.minimum(lane, SCALE_BITS)) & 1
    head = jnp.where(lane < SCALE_BITS, (head & -2) | bit, head)
    return head.astype(jnp.int16), code[:, LANES:].astype(jnp.int16)


def row_scale(head):
    head = head.astype(jnp.int32)
    lane = lax.broadcasted_iota(jnp.int32, head.shape, 1)
    bits = lax.shift_left(head & 1, jnp.minimum(lane, SCALE_BITS))
    bits = jnp.where(lane < SCALE_BITS, bits, 0).astype(jnp.float32)
    stored = jnp.broadcast_to(jnp.sum(bits, axis=1, keepdims=True), head.shape)
    return jnp.exp2((stored - SCALE_SHIFT) * (1.0 / SCALE_STEPS)) * (1.0 / LARGEST)


def cost(rows, tile):
    flops = 2 * rows * tile.shape[-2] * tile.shape[-1]
    return pl.CostEstimate(flops=flops, bytes_accessed=2 * tile.shape[-2] * tile.shape[-1], transcendentals=0)


def blk_steps(blk_count, core):
    near = blk_count - 2
    steps = [slot + 1 + core * (near - 1 - 2 * slot) for slot in range(near)]
    return [0] + steps + [blk_count - 1]


def start_all(copies):
    for copy in copies:
        copy.start()


def wait_all(copies):
    for copy in copies:
        copy.wait()


def pick_kernel(tile_cd, amplitudes, *rest):
    outgoing, sems = rest[:-1], rest[-1]
    blk, grp = lax.axis_index("blk"), lax.axis_index("grp")
    copies = []
    for slot, step in enumerate(blk_steps(len(outgoing), grp % CORES)):
        cd = tile_cd[jnp.bitwise_xor(blk, step), grp]
        copies.append(pltpu.make_async_copy(amplitudes.at[cd], outgoing[slot], sems.at[slot]))
    start_all(copies)
    wait_all(copies)


def pick(tile_cd, amplitudes):
    groups = tile_cd.shape[0]
    block = jax.ShapeDtypeStruct(amplitudes.shape[1:], amplitudes.dtype)
    return pl.pallas_call(
        pick_kernel,
        out_shape=[block] * groups,
        in_specs=[SMEM, ANY],
        out_specs=[VMEM] * groups,
        scratch_shapes=[pltpu.SemaphoreType.DMA((groups,))],
        compiler_params=vmem_limit(*[block] * groups),
        name="pick_cd_blocks",
    )(tile_cd, amplitudes)


def code_chips(product, outgoing, first):
    chip_rows = product.shape[0] // len(outgoing)
    chip = lax.axis_index("grp") // CORES
    for step, coded in enumerate(outgoing):
        source = pl.multiple_of(jnp.bitwise_xor(chip, step) * chip_rows, chip_rows)
        code, tail = encode(product[pl.ds(source, chip_rows), :])
        coded[first : first + chip_rows, :LANES] = code
        coded[first : first + chip_rows, LANES:] = tail


def code_own(product, chips):
    group_rows, tile_width = product.shape
    coded = jax.ShapeDtypeStruct((group_rows // chips, tile_width), jnp.int16)
    return pl.pallas_call(
        lambda product, *outgoing: code_chips(product, outgoing, 0),
        out_shape=[coded] * chips,
        in_specs=[VMEM],
        out_specs=[VMEM] * chips,
        compiler_params=vmem_limit(product, *[coded] * chips),
        name="code_own_group",
    )(product)


def near_kernel(near, *refs):
    groups, tile, own, outgoing, product = refs[:near], refs[near], refs[near + 1], refs[near + 2 : -1], refs[-1]
    chip_rows = product.shape[0] // len(outgoing)
    outgoing[1][near * chip_rows :, :] = own[...]
    for index, rows in enumerate(groups):
        product[...] = jnp.dot(rows[...], tile[...], preferred_element_type=jnp.float32)
        code_chips(product, outgoing, index * chip_rows)


def contract_near(groups, tile, own, chips):
    group_rows, tile_width = groups[0].shape[0], tile.shape[1]
    chip_rows = group_rows // chips
    rows = [len(groups) * chip_rows] * chips
    rows[1] += chip_rows
    coded = [jax.ShapeDtypeStruct((count, tile_width), jnp.int16) for count in rows]
    product = jax.ShapeDtypeStruct((group_rows, tile_width), jnp.float32)
    return pl.pallas_call(
        lambda *refs: near_kernel(len(groups), *refs),
        out_shape=coded,
        in_specs=[VMEM] * (len(groups) + 2),
        out_specs=[VMEM] * chips,
        scratch_shapes=[pltpu.VMEM(product.shape, product.dtype)],
        compiler_params=vmem_limit(*groups, tile, own, *coded, product),
        cost_estimate=cost(len(groups) * group_rows, tile),
        name="contract_near_groups",
    )(*groups, tile, own)


def far_kernel(chips, rows, tile, *rest):
    coded, product = rest[-2:]
    chip_rows = product.shape[0] // chips
    parts = [coded.at[pl.ds(step * chip_rows, chip_rows)] for step in range(chips)]
    product[...] = jnp.dot(rows[...], tile[...], preferred_element_type=jnp.float32)
    code_chips(product, parts, 0)


def contract_far(rows, tile, chips, earlier):
    coded = jax.ShapeDtypeStruct((rows.shape[0], tile.shape[1]), jnp.int16)
    product = jax.ShapeDtypeStruct(coded.shape, jnp.float32)
    return pl.pallas_call(
        lambda *refs: far_kernel(chips, *refs),
        out_shape=coded,
        in_specs=[VMEM] * 2 + [ANY] * len(earlier),
        out_specs=VMEM,
        scratch_shapes=[pltpu.VMEM(product.shape, product.dtype)],
        compiler_params=vmem_limit(rows, tile, coded, product),
        cost_estimate=cost(rows.shape[0], tile),
        name="contract_far_group",
    )(rows, tile, *earlier)


def regroup_kernel(count, parts, part_rows, *refs):
    sources, targets = refs[:count], refs[-parts:]
    for j, source in enumerate(sources):
        for i, target in enumerate(targets):
            target[j * part_rows : (j + 1) * part_rows, :] = source[i * part_rows : (i + 1) * part_rows, :]


def regroup(sources, parts, part_rows, name, earlier=()):
    target = jax.ShapeDtypeStruct((len(sources) * part_rows, sources[0].shape[1]), sources[0].dtype)
    return pl.pallas_call(
        lambda *refs: regroup_kernel(len(sources), parts, part_rows, *refs),
        out_shape=[target] * parts,
        in_specs=[VMEM] * len(sources) + [ANY] * len(earlier),
        out_specs=[VMEM] * parts,
        compiler_params=vmem_limit(*sources, *[target] * parts),
        name=name,
    )(*sources, *earlier)


def other_core_kernel(pieces, owner_rows, *refs):
    arrays, halves = refs[:-1], refs[-1]
    other = 1 - lax.axis_index("grp") % CORES
    for index, (array, first) in enumerate(pieces):
        source = pl.multiple_of(first + other * owner_rows, owner_rows)
        halves[index * owner_rows : (index + 1) * owner_rows, :] = arrays[array][pl.ds(source, owner_rows), :]


def other_core_rows(arrays, pieces, owner_rows):
    halves = jax.ShapeDtypeStruct((len(pieces) * owner_rows, arrays[0].shape[1]), arrays[0].dtype)
    return pl.pallas_call(
        lambda *refs: other_core_kernel(pieces, owner_rows, *refs),
        out_shape=halves,
        in_specs=[VMEM] * len(arrays),
        out_specs=VMEM,
        compiler_params=vmem_limit(*arrays, halves),
        name="rows_of_other_core",
    )(*arrays)


def add_kernel(parts, pieces, tile_ab, tile_cd, pair_screen, *rest):
    arrays, (swapped, residual_in, residual, held, sems) = rest[:-5], rest[-5:]
    blk, grp = lax.axis_index("blk"), lax.axis_index("grp")
    ab_tiles, owner_rows, tile_width = residual.shape
    chips = tile_ab.shape[1] // CORES
    bounds = [ab_tiles * part // parts for part in range(parts + 1)]
    spans = [pl.ds(low, high - low) for low, high in zip(bounds[:-1], bounds[1:])]
    leaves = [pltpu.make_async_copy(held.at[span], residual.at[span], sems.at[i]) for i, span in enumerate(spans)]

    def hold(ab, carry):
        held[ab] = residual_in[ab]
        return carry

    lax.fori_loop(0, ab_tiles, hold, 0)
    core = grp % CORES
    steps_here, steps_there = blk_steps(tile_ab.shape[0], core), blk_steps(tile_ab.shape[0], 1 - core)
    own = core * owner_rows
    for start in range(0, len(pieces), chips):
        terms = []
        for index in range(start, start + chips):
            array, first = arrays[pieces[index][0]], pieces[index][1]
            p_here = jnp.bitwise_xor(blk, steps_here[index // chips])
            p_there = jnp.bitwise_xor(blk, steps_there[index // chips])
            g = jnp.bitwise_xor(grp, index % chips * CORES)
            here = pl.ds(pl.multiple_of(first + own, owner_rows), owner_rows)
            there = pl.ds(index * owner_rows, owner_rows)
            for source, span, p, column in ((array, here, p_here, g), (swapped, there, p_there, jnp.bitwise_xor(g, 1))):
                kept = pair_screen[tile_cd[p, column], grp].astype(jnp.float32)
                scale = row_scale(source[span, :LANES]) * kept
                terms.append((source, span, scale, tile_ab[p, column]))
        for source, span, scale, ab in terms:
            for lane in range(0, tile_width, LANES):
                term = source[span, lane : lane + LANES].astype(jnp.float32) * scale
                held[ab, :, lane : lane + LANES] = held[ab, :, lane : lane + LANES] + term
    start_all(leaves)
    wait_all(leaves)


def add_blocks(tile_ab, tile_cd, pair_screen, arrays, pieces, swapped, residual_in):
    parts = 5
    return pl.pallas_call(
        lambda *refs: add_kernel(parts, pieces, *refs),
        out_shape=jax.ShapeDtypeStruct(residual_in.shape, residual_in.dtype),
        in_specs=[SMEM] * 3 + [VMEM] * (len(arrays) + 2),
        out_specs=ANY,
        scratch_shapes=[pltpu.VMEM(residual_in.shape, residual_in.dtype), pltpu.SemaphoreType.DMA((parts,))],
        compiler_params=vmem_limit(*arrays, swapped, residual_in, residual_in),
        name="add_contributions",
    )(tile_ab, tile_cd, pair_screen, *arrays, swapped, residual_in)


def shards(amplitudes, pair_screen, integrals, tile_ab, tile_cd, residual_in):
    blk_count = lax.axis_size("blk")
    grp_count = lax.axis_size("grp")
    chips = grp_count // CORES
    owner_rows = residual_in.shape[0]
    far = blk_count - 1

    def swap(value, slot, chip_step, core_step=0):
        pairs = []
        for device in range(blk_count * grp_count):
            blk_step = blk_steps(blk_count, device % CORES)[slot]
            pairs.append((device, device ^ (blk_step * grp_count + chip_step * CORES + core_step)))
        return lax.ppermute(value, ("blk", "grp"), pairs)

    def along_chips(outgoing):
        arrived = {step: swap(outgoing[step], 0, step) for step in reversed(range(1, chips))}
        return [outgoing[0]] + [arrived[step] for step in range(1, chips)]

    tile = integrals[0]
    near = blk_count - 2
    chip_rows = CORES * owner_rows
    own_rows, *near_picked, far_picked = pick(tile_cd, amplitudes)
    near_rows = [swap(rows, index + 1, 0) for index, rows in enumerate(near_picked)]
    own_product = jnp.dot(own_rows, tile, preferred_element_type=jnp.float32)
    own_out = code_own(own_product, chips)
    own_in = [swap(own_out[step], 0, step) for step in range(2, chips)]
    (far_picked,) = regroup([far_picked], 1, far_picked.shape[0], "far_rows_after_near", [own_out[0]])
    far_rows = swap(far_picked, far, 0)
    near_out = contract_near(near_rows, tile, own_out[1], chips)
    near_in = along_chips(near_out)
    far_back = swap(contract_far(far_rows, tile, chips, [*own_in, near_out[0]]), far, 0)
    far_out = regroup([far_back], chips, chip_rows, "regroup_by_chip")
    far_in = along_chips(far_out)
    near_back = regroup(near_in, near, chip_rows, "regroup_by_group")
    back_in = [swap(rows, index + 1, 0) for index, rows in enumerate(near_back)]

    arrays = [own_out[0], near_in[1], *own_in, *back_in, *far_in]
    pieces = [(0, 0), (1, near * chip_rows)] + [(step, 0) for step in range(2, chips)]
    for group in range(near):
        pieces += [(chips + group, step * chip_rows) for step in range(chips)]
    pieces += [(chips + near + step, 0) for step in range(chips)]
    swapped = swap(other_core_rows(arrays, pieces, owner_rows), 0, 0, 1)
    by_tile = jnp.transpose(residual_in, (1, 0, 2))
    added = add_blocks(tile_ab, tile_cd, pair_screen, arrays, pieces, swapped, by_tile)
    return jnp.transpose(added, (1, 0, 2))


def solution(mesh):
    in_specs = (
        P(None, "blk", None),
        P(None, "blk"),
        P(("blk", "grp"), None, None),
        P(),
        P(),
        P(("blk", "grp"), None, None),
    )
    out_specs = P(("blk", "grp"), None, None)
    return jax.shard_map(shards, mesh=mesh, in_specs=in_specs, out_specs=out_specs, check_vma=False)
```

```python
import math

import jax
import jax.numpy as jnp
from jax import lax
from jax.experimental import pallas as pl
from jax.experimental.pallas import tpu as pltpu
from jax.sharding import PartitionSpec as P

LARGEST = 32766.0
SCALE_STEPS = 64.0
SCALE_SHIFT = 8192
SCALE_BITS = 16
LANES = 128
CORES = 2
MEBIBYTE = 1 << 20
PICK_LIMIT = 209 * MEBIBYTE // 4
SMEM = pl.BlockSpec(memory_space=pltpu.SMEM)
VMEM = pl.BlockSpec(memory_space=pltpu.VMEM)
ANY = pl.BlockSpec(memory_space=pl.ANY)


def vmem_limit(*arrays):
    total = sum(math.prod(array.shape) * jnp.dtype(array.dtype).itemsize for array in arrays)
    return pltpu.CompilerParams(vmem_limit_bytes=total + 4 * MEBIBYTE)


def encode(values):
    largest = jnp.max(jnp.abs(values), axis=1, keepdims=True)
    logarithm = jnp.log2(jnp.maximum(largest, 2.0**-100))
    exponent = jnp.floor(logarithm * SCALE_STEPS) + 2.0
    scaled = values * (LARGEST * jnp.exp2(exponent * (-1.0 / SCALE_STEPS)))
    scaled = jnp.clip(scaled, -LARGEST, LARGEST)
    code = jnp.floor(scaled + 0.5).astype(jnp.int32)
    head = code[:, :LANES]
    lane = lax.broadcasted_iota(jnp.int32, head.shape, 1)
    stored = exponent.astype(jnp.int32) + SCALE_SHIFT
    stored = jnp.broadcast_to(stored, head.shape)
    bit = lax.shift_right_logical(stored, jnp.minimum(lane, SCALE_BITS)) & 1
    head = jnp.where(lane < SCALE_BITS, (head & -2) | bit, head)
    return head.astype(jnp.int16), code[:, LANES:].astype(jnp.int16)


def row_scale(head):
    head = head.astype(jnp.int32)
    lane = lax.broadcasted_iota(jnp.int32, head.shape, 1)
    bits = lax.shift_left(head & 1, jnp.minimum(lane, SCALE_BITS))
    bits = jnp.where(lane < SCALE_BITS, bits, 0).astype(jnp.float32)
    stored = jnp.broadcast_to(jnp.sum(bits, axis=1, keepdims=True), head.shape)
    return jnp.exp2((stored - SCALE_SHIFT) * (1.0 / SCALE_STEPS)) * (1.0 / LARGEST)


def cost(rows, tile):
    flops = 2 * rows * tile.shape[-2] * tile.shape[-1]
    return pl.CostEstimate(flops=flops, bytes_accessed=2 * tile.shape[-2] * tile.shape[-1], transcendentals=0)


def blk_steps(blk_count, core):
    near = blk_count - 2
    steps = [slot + 1 + core * (near - 1 - 2 * slot) for slot in range(near)]
    return [0] + steps + [blk_count - 1]


def chip_steps(chips):
    return [0] + list(reversed(range(1, chips)))


def start_all(copies):
    for copy in copies:
        copy.start()


def wait_all(copies):
    for copy in copies:
        copy.wait()


def pick_kernel(tile_cd, amplitudes, *rest):
    outgoing, sems = rest[:-1], rest[-1]
    blk, grp = lax.axis_index("blk"), lax.axis_index("grp")
    copies = []
    for slot, step in enumerate(blk_steps(len(outgoing), grp % CORES)):
        cd = tile_cd[jnp.bitwise_xor(blk, step), grp]
        copies.append(pltpu.make_async_copy(amplitudes.at[cd], outgoing[slot], sems.at[slot]))
    start_all(copies)
    wait_all(copies)


def pick(tile_cd, amplitudes):
    groups = tile_cd.shape[0]
    block = jax.ShapeDtypeStruct(amplitudes.shape[1:], amplitudes.dtype)
    return pl.pallas_call(
        pick_kernel,
        out_shape=[block] * groups,
        in_specs=[SMEM, ANY],
        out_specs=[VMEM] * groups,
        scratch_shapes=[pltpu.SemaphoreType.DMA((groups,))],
        compiler_params=pltpu.CompilerParams(vmem_limit_bytes=PICK_LIMIT),
        name="pick_cd_blocks",
    )(tile_cd, amplitudes)


def code_chips(rows, tile, product, outgoing, first):
    product[...] = jnp.dot(rows[...], tile[...], preferred_element_type=jnp.float32)
    chip_rows = product.shape[0] // len(outgoing)
    chip = lax.axis_index("grp") // CORES
    for step, coded in zip(chip_steps(len(outgoing)), outgoing):
        source = pl.multiple_of(jnp.bitwise_xor(chip, step) * chip_rows, chip_rows)
        code, tail = encode(product[pl.ds(source, chip_rows), :])
        coded[first : first + chip_rows, :LANES] = code
        coded[first : first + chip_rows, LANES:] = tail


def own_kernel(rows, tile, far_picked, *rest):
    outgoing, (tile_out, far_out, product, sem) = rest[:-4], rest[-4:]
    copy = pltpu.make_async_copy(tile, tile_out, sem)
    copy.start()
    far_out[...] = far_picked[...]
    code_chips(rows, tile, product, outgoing, 0)
    copy.wait()


def contract_own(rows, tile, far_picked, chips):
    group_rows, tile_width = rows.shape[0], tile.shape[1]
    coded = jax.ShapeDtypeStruct((group_rows // chips, tile_width), jnp.int16)
    product = jax.ShapeDtypeStruct((group_rows, tile_width), jnp.float32)
    outputs = [coded] * chips + [jax.ShapeDtypeStruct(array.shape, array.dtype) for array in (tile, far_picked)]
    return pl.pallas_call(
        own_kernel,
        out_shape=outputs,
        in_specs=[VMEM] * 3,
        out_specs=[VMEM] * len(outputs),
        scratch_shapes=[pltpu.VMEM(product.shape, product.dtype), pltpu.SemaphoreType.DMA],
        compiler_params=vmem_limit(rows, tile, far_picked, *outputs, product),
        cost_estimate=cost(group_rows, tile),
        name="contract_own_group",
    )(rows, tile, far_picked)


def near_kernel(near, *refs):
    groups, tile, outgoing, product = refs[:near], refs[near], refs[near + 1 : -1], refs[-1]
    chip_rows = product.shape[0] // len(outgoing)
    for index, rows in enumerate(groups):
        code_chips(rows, tile, product, outgoing, index * chip_rows)


def contract_near(groups, tile, chips):
    group_rows, tile_width = groups[0].shape[0], tile.shape[1]
    coded = jax.ShapeDtypeStruct((len(groups) * group_rows // chips, tile_width), jnp.int16)
    product = jax.ShapeDtypeStruct((group_rows, tile_width), jnp.float32)
    return pl.pallas_call(
        lambda *refs: near_kernel(len(groups), *refs),
        out_shape=[coded] * chips,
        in_specs=[VMEM] * (len(groups) + 1),
        out_specs=[VMEM] * chips,
        scratch_shapes=[pltpu.VMEM(product.shape, product.dtype)],
        compiler_params=vmem_limit(*groups, tile, *[coded] * chips, product),
        cost_estimate=cost(len(groups) * group_rows, tile),
        name="contract_near_groups",
    )(*groups, tile)


def far_kernel(chips, rows, tile, *rest):
    coded, product = rest[-2:]
    chip_rows = product.shape[0] // chips
    parts = [coded.at[pl.ds(step * chip_rows, chip_rows)] for step in range(chips)]
    code_chips(rows, tile, product, parts, 0)


def contract_far(rows, tile, chips, earlier):
    coded = jax.ShapeDtypeStruct((rows.shape[0], tile.shape[1]), jnp.int16)
    product = jax.ShapeDtypeStruct(coded.shape, jnp.float32)
    return pl.pallas_call(
        lambda *refs: far_kernel(chips, *refs),
        out_shape=coded,
        in_specs=[VMEM] * 2 + [ANY] * len(earlier),
        out_specs=VMEM,
        scratch_shapes=[pltpu.VMEM(product.shape, product.dtype)],
        compiler_params=vmem_limit(rows, tile, coded, product),
        cost_estimate=cost(rows.shape[0], tile),
        name="contract_far_group",
    )(rows, tile, *earlier)


def regroup_kernel(count, *refs):
    sources, targets = refs[:count], refs[count:]
    part_rows = sources[0].shape[0] // len(targets)
    for j, source in enumerate(sources):
        for i, target in enumerate(targets):
            target[j * part_rows : (j + 1) * part_rows, :] = source[i * part_rows : (i + 1) * part_rows, :]


def regroup(sources, parts, name):
    rows, tile_width = sources[0].shape
    target = jax.ShapeDtypeStruct((len(sources) * rows // parts, tile_width), sources[0].dtype)
    return pl.pallas_call(
        lambda *refs: regroup_kernel(len(sources), *refs),
        out_shape=[target] * parts,
        in_specs=[VMEM] * len(sources),
        out_specs=[VMEM] * parts,
        compiler_params=vmem_limit(*sources, *[target] * parts),
        name=name,
    )(*sources)


def pieces_of(arrays, owner_rows):
    return [(i, first) for i, array in enumerate(arrays) for first in range(0, array.shape[0], CORES * owner_rows)]


def other_core_kernel(pieces, owner_rows, *refs):
    arrays, halves = refs[:-1], refs[-1]
    other = 1 - lax.axis_index("grp") % CORES
    for index, (array, first) in enumerate(pieces):
        source = pl.multiple_of(first + other * owner_rows, owner_rows)
        halves[index * owner_rows : (index + 1) * owner_rows, :] = arrays[array][pl.ds(source, owner_rows), :]


def other_core_rows(arrays, pieces, owner_rows):
    halves = jax.ShapeDtypeStruct((len(pieces) * owner_rows, arrays[0].shape[1]), arrays[0].dtype)
    return pl.pallas_call(
        lambda *refs: other_core_kernel(pieces, owner_rows, *refs),
        out_shape=halves,
        in_specs=[VMEM] * len(arrays),
        out_specs=VMEM,
        compiler_params=vmem_limit(*arrays, halves),
        name="rows_of_other_core",
    )(*arrays)


def add_rows(rows, tables, blk, grp, held):
    tile_ab, tile_cd, pair_screen = tables
    terms = []
    for source, span, p, g in rows:
        kept = pair_screen[tile_cd[p, g], grp].astype(jnp.float32)
        terms.append((source, span, row_scale(source[span, :LANES]) * kept, tile_ab[p, g]))
    for source, span, scale, ab in terms:
        for lane in range(0, held.shape[2], LANES):
            term = source[span, lane : lane + LANES].astype(jnp.float32) * scale
            held[ab, :, lane : lane + LANES] = held[ab, :, lane : lane + LANES] + term


def tile_of(index, blk, grp, core, chips, blk_count):
    p = jnp.bitwise_xor(blk, blk_steps(blk_count, core)[index // chips])
    chip_step = chip_steps(chips)[index % chips]
    return p, (jnp.bitwise_xor(grp // CORES, chip_step)) * CORES + core


def add_here_kernel(pieces, tile_ab, tile_cd, pair_screen, *rest):
    arrays, residual_in, held = rest[:-2], rest[-2], rest[-1]
    blk, grp = lax.axis_index("blk"), lax.axis_index("grp")
    ab_tiles, owner_rows, _ = held.shape
    blk_count, chips = tile_ab.shape[0], tile_ab.shape[1] // CORES
    core = grp % CORES

    def hold(ab, carry):
        held[ab] = residual_in[ab]
        return carry

    lax.fori_loop(0, ab_tiles, hold, 0)
    for start in range(0, len(pieces), 2 * chips):
        rows = []
        for index in range(start, min(start + 2 * chips, len(pieces))):
            array, first = pieces[index]
            span = pl.ds(pl.multiple_of(first + core * owner_rows, owner_rows), owner_rows)
            rows.append((arrays[array], span, *tile_of(index, blk, grp, core, chips, blk_count)))
        add_rows(rows, (tile_ab, tile_cd, pair_screen), blk, grp, held)


def add_here(tables, arrays, pieces, residual_in):
    return pl.pallas_call(
        lambda *refs: add_here_kernel(pieces, *refs),
        out_shape=jax.ShapeDtypeStruct(residual_in.shape, residual_in.dtype),
        in_specs=[SMEM] * 3 + [VMEM] * (len(arrays) + 1),
        out_specs=VMEM,
        compiler_params=vmem_limit(*arrays, residual_in, residual_in),
        name="add_contributions_here",
    )(*tables, *arrays, residual_in)


def add_there_kernel(parts, tile_ab, tile_cd, pair_screen, swapped, partial, residual, held, touched, part_sems, tile_sems):
    blk, grp = lax.axis_index("blk"), lax.axis_index("grp")
    ab_tiles, owner_rows, _ = residual.shape
    blk_count, chips = tile_ab.shape[0], tile_ab.shape[1] // CORES
    core = 1 - grp % CORES
    bounds = [ab_tiles * part // parts for part in range(parts + 1)]
    spans = [pl.ds(low, high - low) for low, high in zip(bounds[:-1], bounds[1:])]
    bulk = [pltpu.make_async_copy(partial.at[span], residual.at[span], part_sems.at[i]) for i, span in enumerate(spans)]
    start_all(bulk)

    def clear(ab, carry):
        touched[ab] = 0
        return carry

    lax.fori_loop(0, ab_tiles, clear, 0)
    rows, fresh = [], []
    for index in range(blk_count * chips):
        span = pl.ds(index * owner_rows, owner_rows)
        rows.append((swapped, span, *tile_of(index, blk, grp, core, chips, blk_count)))
    for _, _, p, g in rows:
        ab = tile_ab[p, g]
        fresh.append((ab, touched[ab] == 0))
        touched[ab] = 1
        held[ab] = partial[ab]
    for start in range(0, len(rows), 2 * chips):
        add_rows(rows[start : start + 2 * chips], (tile_ab, tile_cd, pair_screen), blk, grp, held)
    wait_all(bulk)
    for action in ("start", "wait"):
        for index, (ab, first) in enumerate(fresh):
            copy = pltpu.make_async_copy(held.at[ab], residual.at[ab], tile_sems.at[index])
            pl.when(first)(getattr(copy, action))


def add_there(tables, swapped, partial):
    parts, owner_rows = 5, partial.shape[1]
    return pl.pallas_call(
        lambda *refs: add_there_kernel(parts, *refs),
        out_shape=jax.ShapeDtypeStruct(partial.shape, partial.dtype),
        in_specs=[SMEM] * 3 + [VMEM] * 2,
        out_specs=ANY,
        scratch_shapes=[
            pltpu.VMEM(partial.shape, partial.dtype),
            pltpu.SMEM((partial.shape[0],), jnp.int32),
            pltpu.SemaphoreType.DMA((parts,)),
            pltpu.SemaphoreType.DMA((swapped.shape[0] // owner_rows,)),
        ],
        compiler_params=vmem_limit(swapped, partial, partial),
        name="add_contributions_there",
    )(*tables, swapped, partial)


def shards(amplitudes, pair_screen, integrals, tile_ab, tile_cd, residual_in):
    blk_count = lax.axis_size("blk")
    grp_count = lax.axis_size("grp")
    chips = grp_count // CORES
    owner_rows = residual_in.shape[0]
    far = blk_count - 1

    def swap(value, slot, chip_step, core_step=0):
        pairs = []
        for device in range(blk_count * grp_count):
            blk_step = blk_steps(blk_count, device % CORES)[slot]
            pairs.append((device, device ^ (blk_step * grp_count + chip_step * CORES + core_step)))
        return lax.ppermute(value, ("blk", "grp"), pairs)

    def along_chips(outgoing):
        steps = chip_steps(chips)
        return [outgoing[0]] + [swap(outgoing[slot], 0, steps[slot]) for slot in range(1, chips)]

    own_rows, *near_picked, far_picked = pick(tile_cd, amplitudes)
    near_rows = [swap(rows, index + 1, 0) for index, rows in enumerate(near_picked)]
    *own_out, tile, far_picked = contract_own(own_rows, integrals[0], far_picked, chips)
    own_in = along_chips(own_out)
    far_rows = swap(far_picked, far, 0)
    near_in = along_chips(contract_near(near_rows, tile, chips))
    near_back = regroup(near_in, blk_count - 2, "regroup_by_group")
    near_in = [swap(rows, index + 1, 0) for index, rows in enumerate(near_back)]
    far_back = swap(contract_far(far_rows, tile, chips, own_in[1:]), far, 0)
    far_in = along_chips(regroup([far_back], chips, "regroup_by_chip"))
    arrays = [*own_in, *near_in, *far_in]
    pieces = pieces_of(arrays, owner_rows)
    swapped = swap(other_core_rows(arrays, pieces, owner_rows), 0, 0, 1)
    tables = (tile_ab, tile_cd, pair_screen)
    partial = add_here(tables, arrays, pieces, jnp.transpose(residual_in, (1, 0, 2)))
    return jnp.transpose(add_there(tables, swapped, partial), (1, 0, 2))


def solution(mesh):
    in_specs = (
        P(None, "blk", None),
        P(None, "blk"),
        P(("blk", "grp"), None, None),
        P(),
        P(),
        P(("blk", "grp"), None, None),
    )
    out_specs = P(("blk", "grp"), None, None)
    return jax.shard_map(shards, mesh=mesh, in_specs=in_specs, out_specs=out_specs, check_vma=False)
```

```python
import math

import jax
import jax.numpy as jnp
from jax import lax
from jax.experimental import pallas as pl
from jax.experimental.pallas import tpu as pltpu
from jax.sharding import PartitionSpec as P

LARGEST = 32766.0
SCALE_STEPS = 64.0
SCALE_SHIFT = 8192
SCALE_BITS = 16
LANES = 128
CORES = 2
MEBIBYTE = 1 << 20
SMEM = pl.BlockSpec(memory_space=pltpu.SMEM)
VMEM = pl.BlockSpec(memory_space=pltpu.VMEM)
ANY = pl.BlockSpec(memory_space=pl.ANY)


def vmem_limit(*arrays):
    total = sum(math.prod(array.shape) * jnp.dtype(array.dtype).itemsize for array in arrays)
    return pltpu.CompilerParams(vmem_limit_bytes=total + 4 * MEBIBYTE)


def encode(values):
    largest = jnp.max(jnp.abs(values), axis=1, keepdims=True)
    logarithm = jnp.log2(jnp.maximum(largest, 2.0**-100))
    exponent = jnp.floor(logarithm * SCALE_STEPS) + 2.0
    scaled = values * (LARGEST * jnp.exp2(exponent * (-1.0 / SCALE_STEPS)))
    scaled = jnp.clip(scaled, -LARGEST, LARGEST)
    code = jnp.floor(scaled + 0.5).astype(jnp.int32)
    head = code[:, :LANES]
    lane = lax.broadcasted_iota(jnp.int32, head.shape, 1)
    stored = exponent.astype(jnp.int32) + SCALE_SHIFT
    stored = jnp.broadcast_to(stored, head.shape)
    bit = lax.shift_right_logical(stored, jnp.minimum(lane, SCALE_BITS)) & 1
    head = jnp.where(lane < SCALE_BITS, (head & -2) | bit, head)
    return head.astype(jnp.int16), code[:, LANES:].astype(jnp.int16)


def row_scale(head):
    head = head.astype(jnp.int32)
    lane = lax.broadcasted_iota(jnp.int32, head.shape, 1)
    bits = lax.shift_left(head & 1, jnp.minimum(lane, SCALE_BITS))
    bits = jnp.where(lane < SCALE_BITS, bits, 0).astype(jnp.float32)
    stored = jnp.broadcast_to(jnp.sum(bits, axis=1, keepdims=True), head.shape)
    return jnp.exp2((stored - SCALE_SHIFT) * (1.0 / SCALE_STEPS)) * (1.0 / LARGEST)


def cost(rows, tile):
    flops = 2 * rows * tile.shape[-2] * tile.shape[-1]
    return pl.CostEstimate(flops=flops, bytes_accessed=2 * tile.shape[-2] * tile.shape[-1], transcendentals=0)


def blk_steps(blk_count, core):
    near = blk_count - 2
    steps = [slot + 1 + core * (near - 1 - 2 * slot) for slot in range(near)]
    return [0] + steps + [blk_count - 1]


def chip_steps(chips):
    return [0] + list(reversed(range(1, chips)))


def start_all(copies):
    for copy in copies:
        copy.start()


def wait_all(copies):
    for copy in copies:
        copy.wait()


def pick_kernel(tile_cd, amplitudes, *rest):
    outgoing, sems = rest[:-1], rest[-1]
    blk, grp = lax.axis_index("blk"), lax.axis_index("grp")
    copies = []
    for slot, step in enumerate(blk_steps(len(outgoing), grp % CORES)):
        cd = tile_cd[jnp.bitwise_xor(blk, step), grp]
        copies.append(pltpu.make_async_copy(amplitudes.at[cd], outgoing[slot], sems.at[slot]))
    start_all(copies)
    wait_all(copies)


def pick(tile_cd, amplitudes):
    groups = tile_cd.shape[0]
    block = jax.ShapeDtypeStruct(amplitudes.shape[1:], amplitudes.dtype)
    return pl.pallas_call(
        pick_kernel,
        out_shape=[block] * groups,
        in_specs=[SMEM, ANY],
        out_specs=[VMEM] * groups,
        scratch_shapes=[pltpu.SemaphoreType.DMA((groups,))],
        compiler_params=vmem_limit(*[block] * groups),
        name="pick_cd_blocks",
    )(tile_cd, amplitudes)


def code_chips(product, outgoing, first):
    chip_rows = product.shape[0] // len(outgoing)
    chip = lax.axis_index("grp") // CORES
    for step, coded in zip(chip_steps(len(outgoing)), outgoing):
        source = pl.multiple_of(jnp.bitwise_xor(chip, step) * chip_rows, chip_rows)
        code, tail = encode(product[pl.ds(source, chip_rows), :])
        coded[first : first + chip_rows, :LANES] = code
        coded[first : first + chip_rows, LANES:] = tail


def chips_kernel(chips, before, passed, rows, tile, *rest):
    front, rest = rest[:before], rest[before:]
    handed, outgoing, product = rest[:passed], rest[-chips - passed - 1 : -1], rest[-1]
    for source, target in zip(handed, outgoing[chips:]):
        target[...] = source[...]
    product[...] = jnp.dot(rows[...], tile[...], preferred_element_type=jnp.float32)
    first = outgoing[0].shape[0] - product.shape[0] // chips
    for source, target in zip(front, outgoing):
        target[:first, :] = source[...]
    code_chips(product, outgoing[:chips], first)


def contract_for_chips(rows, tile, chips, front=(), passed=(), earlier=()):
    group_rows, tile_width = rows.shape[0], tile.shape[1]
    coded_rows = group_rows // chips + sum(array.shape[0] for array in front[:1])
    coded = jax.ShapeDtypeStruct((coded_rows, tile_width), jnp.int16)
    product = jax.ShapeDtypeStruct((group_rows, tile_width), jnp.float32)
    outputs = [coded] * chips + [jax.ShapeDtypeStruct(array.shape, array.dtype) for array in passed]
    inputs = [rows, tile, *front, *passed]
    return pl.pallas_call(
        lambda *refs: chips_kernel(chips, len(front), len(passed), *refs),
        out_shape=outputs,
        in_specs=[VMEM] * len(inputs) + [ANY] * len(earlier),
        out_specs=[VMEM] * len(outputs),
        scratch_shapes=[pltpu.VMEM(product.shape, product.dtype)],
        compiler_params=vmem_limit(*inputs, *outputs, product),
        cost_estimate=cost(group_rows, tile),
        name="contract_for_chips",
    )(*inputs, *earlier)


def one_kernel(chips, rows, tile, *rest):
    coded, product = rest[-2:]
    chip_rows = product.shape[0] // chips
    product[...] = jnp.dot(rows[...], tile[...], preferred_element_type=jnp.float32)
    code_chips(product, [coded.at[pl.ds(slot * chip_rows, chip_rows)] for slot in range(chips)], 0)


def contract_whole(rows, tile, chips, earlier):
    coded = jax.ShapeDtypeStruct((rows.shape[0], tile.shape[1]), jnp.int16)
    product = jax.ShapeDtypeStruct(coded.shape, jnp.float32)
    return pl.pallas_call(
        lambda *refs: one_kernel(chips, *refs),
        out_shape=coded,
        in_specs=[VMEM] * 2 + [ANY] * len(earlier),
        out_specs=VMEM,
        scratch_shapes=[pltpu.VMEM(product.shape, product.dtype)],
        compiler_params=vmem_limit(rows, tile, coded, product),
        cost_estimate=cost(rows.shape[0], tile),
        name="contract_far_group",
    )(rows, tile, *earlier)


def split_kernel(source, *targets):
    part_rows = targets[0].shape[0]
    for slot, target in enumerate(targets):
        target[...] = source[slot * part_rows : (slot + 1) * part_rows, :]


def split(source, parts):
    rows, tile_width = source.shape
    target = jax.ShapeDtypeStruct((rows // parts, tile_width), source.dtype)
    return pl.pallas_call(
        split_kernel,
        out_shape=[target] * parts,
        in_specs=[VMEM],
        out_specs=[VMEM] * parts,
        compiler_params=vmem_limit(source, source),
        name="split_by_chip",
    )(source)


def last_rows_kernel(count, *refs):
    sources, target = refs[:count], refs[-1]
    part_rows = target.shape[0] // count
    for slot, source in enumerate(sources):
        target[slot * part_rows : (slot + 1) * part_rows, :] = source[source.shape[0] - part_rows :, :]


def last_rows(sources, part_rows, earlier=()):
    target = jax.ShapeDtypeStruct((len(sources) * part_rows, sources[0].shape[1]), sources[0].dtype)
    return pl.pallas_call(
        lambda *refs: last_rows_kernel(len(sources), *refs),
        out_shape=target,
        in_specs=[VMEM] * len(sources) + [ANY] * len(earlier),
        out_specs=VMEM,
        compiler_params=vmem_limit(*sources, target),
        name="rows_of_one_group",
    )(*sources, *earlier)


def other_core_kernel(pieces, owner_rows, *refs):
    arrays, halves = refs[:-1], refs[-1]
    other = 1 - lax.axis_index("grp") % CORES
    for index, (array, first) in enumerate(pieces):
        source = pl.multiple_of(first + other * owner_rows, owner_rows)
        halves[index * owner_rows : (index + 1) * owner_rows, :] = arrays[array][pl.ds(source, owner_rows), :]


def other_core_rows(arrays, pieces, owner_rows):
    halves = jax.ShapeDtypeStruct((len(pieces) * owner_rows, arrays[0].shape[1]), arrays[0].dtype)
    return pl.pallas_call(
        lambda *refs: other_core_kernel(pieces, owner_rows, *refs),
        out_shape=halves,
        in_specs=[VMEM] * len(arrays),
        out_specs=VMEM,
        compiler_params=vmem_limit(*arrays, halves),
        name="rows_of_other_core",
    )(*arrays)


def add_rows(rows, tables, grp, held):
    tile_ab, tile_cd, pair_screen = tables
    terms = []
    for source, span, p, g in rows:
        kept = pair_screen[tile_cd[p, g], grp].astype(jnp.float32)
        terms.append((source, span, row_scale(source[span, :LANES]) * kept, tile_ab[p, g]))
    for source, span, scale, ab in terms:
        for lane in range(0, held.shape[2], LANES):
            term = source[span, lane : lane + LANES].astype(jnp.float32) * scale
            held[ab, :, lane : lane + LANES] = held[ab, :, lane : lane + LANES] + term


def tile_of(index, blk, grp, core, chips, blk_count):
    p = jnp.bitwise_xor(blk, blk_steps(blk_count, core)[index // chips])
    chip_step = chip_steps(chips)[index % chips]
    return p, (jnp.bitwise_xor(grp // CORES, chip_step)) * CORES + core


def write_kernel(parts, residual_in, *rest):
    residual, token, sems = rest[-3:]
    token[...] = jnp.zeros_like(token)
    ab_tiles = residual.shape[0]
    bounds = [ab_tiles * part // parts for part in range(parts + 1)]
    spans = [pl.ds(low, high - low) for low, high in zip(bounds[:-1], bounds[1:])]
    copies = [pltpu.make_async_copy(residual_in.at[span], residual.at[span], sems.at[i]) for i, span in enumerate(spans)]
    start_all(copies)
    wait_all(copies)


def write_residual(residual_in, earlier):
    parts = 5
    token = jax.ShapeDtypeStruct((8, LANES), jnp.int32)
    return pl.pallas_call(
        lambda *refs: write_kernel(parts, *refs),
        out_shape=[jax.ShapeDtypeStruct(residual_in.shape, residual_in.dtype), token],
        in_specs=[VMEM] + [ANY] * len(earlier),
        out_specs=[ANY, VMEM],
        scratch_shapes=[pltpu.SemaphoreType.DMA((parts,))],
        compiler_params=vmem_limit(residual_in),
        name="write_residual",
    )(residual_in, *earlier)


def add_and_write(rows, tables, grp, before, held, residual, touched, sems):
    def clear(ab, carry):
        touched[ab] = 0
        return carry

    lax.fori_loop(0, residual.shape[0], clear, 0)
    tile_ab = tables[0]
    fresh = []
    for _, _, p, g in rows:
        ab = tile_ab[p, g]
        fresh.append((ab, touched[ab] == 0))
        touched[ab] = 1
        if before is not None:
            held[ab] = before[ab]
    group = 8
    for start in range(0, len(rows), group):
        add_rows(rows[start : start + group], tables, grp, held)
    for action in ("start", "wait"):
        for index, (ab, first) in enumerate(fresh):
            copy = pltpu.make_async_copy(held.at[ab], residual.at[ab], sems.at[index])
            pl.when(first)(getattr(copy, action))


def add_here_kernel(pieces, *refs):
    tables, arrays, (residual_in, _, residual, held, touched, sems) = refs[:3], refs[3:-6], refs[-6:]
    blk, grp = lax.axis_index("blk"), lax.axis_index("grp")
    ab_tiles, owner_rows, _ = held.shape
    blk_count, chips = tables[0].shape[0], tables[0].shape[1] // CORES
    core = grp % CORES

    def hold(ab, carry):
        held[ab] = residual_in[ab]
        return carry

    lax.fori_loop(0, ab_tiles, hold, 0)
    rows = []
    for index, (array, first) in enumerate(pieces):
        span = pl.ds(pl.multiple_of(first + core * owner_rows, owner_rows), owner_rows)
        rows.append((arrays[array], span, *tile_of(index, blk, grp, core, chips, blk_count)))
    add_and_write(rows, tables, grp, None, held, residual, touched, sems)


def add_here(tables, arrays, pieces, residual_in, written):
    whole = jax.ShapeDtypeStruct(residual_in.shape, residual_in.dtype)
    return pl.pallas_call(
        lambda *refs: add_here_kernel(pieces, *refs),
        out_shape=[whole, whole],
        in_specs=[SMEM] * 3 + [VMEM] * (len(arrays) + 1) + [ANY],
        out_specs=[ANY, VMEM],
        scratch_shapes=[pltpu.SMEM(whole.shape[:1], jnp.int32), pltpu.SemaphoreType.DMA((len(pieces),))],
        input_output_aliases={3 + len(arrays) + 1: 0},
        compiler_params=vmem_limit(*arrays, residual_in, residual_in),
        name="add_contributions_here",
    )(*tables, *arrays, residual_in, written)


def add_there_kernel(*refs):
    tables, (swapped, partial, _, residual, held, touched, sems) = refs[:3], refs[3:]
    blk, grp = lax.axis_index("blk"), lax.axis_index("grp")
    owner_rows = residual.shape[1]
    blk_count, chips = tables[0].shape[0], tables[0].shape[1] // CORES
    core = 1 - grp % CORES
    rows = []
    for index in range(blk_count * chips):
        span = pl.ds(index * owner_rows, owner_rows)
        rows.append((swapped, span, *tile_of(index, blk, grp, core, chips, blk_count)))
    add_and_write(rows, tables, grp, partial, held, residual, touched, sems)


def add_there(tables, swapped, partial, written):
    whole, pieces = jax.ShapeDtypeStruct(partial.shape, partial.dtype), swapped.shape[0] // partial.shape[1]
    return pl.pallas_call(
        add_there_kernel,
        out_shape=whole,
        in_specs=[SMEM] * 3 + [VMEM] * 2 + [ANY],
        out_specs=ANY,
        scratch_shapes=[
            pltpu.VMEM(whole.shape, whole.dtype),
            pltpu.SMEM(whole.shape[:1], jnp.int32),
            pltpu.SemaphoreType.DMA((pieces,)),
        ],
        input_output_aliases={5: 0},
        compiler_params=vmem_limit(swapped, partial, partial),
        name="add_contributions_there",
    )(*tables, swapped, partial, written)


def shards(amplitudes, pair_screen, integrals, tile_ab, tile_cd, residual_in):
    blk_count = lax.axis_size("blk")
    grp_count = lax.axis_size("grp")
    chips = grp_count // CORES
    owner_rows = residual_in.shape[0]
    far = blk_count - 1

    def swap(value, slot, chip_step, core_step=0):
        pairs = []
        for device in range(blk_count * grp_count):
            blk_step = blk_steps(blk_count, device % CORES)[slot]
            pairs.append((device, device ^ (blk_step * grp_count + chip_step * CORES + core_step)))
        return lax.ppermute(value, ("blk", "grp"), pairs)

    def along_chips(outgoing):
        steps = chip_steps(chips)
        return [outgoing[0]] + [swap(outgoing[slot], 0, steps[slot]) for slot in range(1, chips)]

    chip_rows = CORES * owner_rows
    tile = integrals[0]
    own_rows, *near_picked, far_picked = pick(tile_cd, amplitudes)
    near_rows = [swap(rows, index + 1, 0) for index, rows in enumerate(near_picked)]
    *own_out, far_picked = contract_for_chips(own_rows, tile, chips, passed=[far_picked])
    far_rows = swap(far_picked, far, 0)
    by_tile = jnp.transpose(residual_in, (1, 0, 2))
    back_in = []
    near_in, front = [], own_out
    for rows in near_rows:
        near_in.append(along_chips(contract_for_chips(rows, tile, chips, front=front)))
        front = []
    far_coded = contract_whole(far_rows, tile, chips, [])
    written, token = write_residual(by_tile, [far_coded])
    for index, arrived in enumerate(near_in):
        back = last_rows(arrived, chip_rows, [token] if index else [])
        back_in.append(swap(back, index + 1, 0))
    far_in = along_chips(split(swap(far_coded, far, 0), chips))
    pieces = [(slot, 0) for slot in range(chips)]
    arrays = [*near_in[0], *back_in, *far_in]
    pieces += [(chips + group, slot * chip_rows) for group in range(len(back_in)) for slot in range(chips)]
    pieces += [(chips + len(back_in) + slot, 0) for slot in range(chips)]
    swapped = swap(other_core_rows(arrays, pieces, owner_rows), 0, 0, 1)
    tables = (tile_ab, tile_cd, pair_screen)
    written, partial = add_here(tables, arrays, pieces, by_tile, written)
    return jnp.transpose(add_there(tables, swapped, partial, written), (1, 0, 2))


def solution(mesh):
    in_specs = (
        P(None, "blk", None),
        P(None, "blk"),
        P(("blk", "grp"), None, None),
        P(),
        P(),
        P(("blk", "grp"), None, None),
    )
    out_specs = P(("blk", "grp"), None, None)
    return jax.shard_map(shards, mesh=mesh, in_specs=in_specs, out_specs=out_specs, check_vma=False)
```

```python
import math

import jax
import jax.numpy as jnp
from jax import lax
from jax.experimental import pallas as pl
from jax.experimental.pallas import tpu as pltpu
from jax.sharding import PartitionSpec as P

LARGEST = 32766.0
SCALE_STEPS = 64.0
SCALE_SHIFT = 8192
SCALE_BITS = 16
LANES = 128
CORES = 2
MEBIBYTE = 1 << 20
SMEM = pl.BlockSpec(memory_space=pltpu.SMEM)
VMEM = pl.BlockSpec(memory_space=pltpu.VMEM)
ANY = pl.BlockSpec(memory_space=pl.ANY)


def vmem_limit(*arrays):
    total = sum(math.prod(array.shape) * jnp.dtype(array.dtype).itemsize for array in arrays)
    return pltpu.CompilerParams(vmem_limit_bytes=total + 4 * MEBIBYTE)


def encode(values):
    largest = jnp.max(jnp.abs(values), axis=1, keepdims=True)
    logarithm = jnp.log2(jnp.maximum(largest, 2.0**-100))
    exponent = jnp.floor(logarithm * SCALE_STEPS) + 2.0
    scaled = values * (LARGEST * jnp.exp2(exponent * (-1.0 / SCALE_STEPS)))
    scaled = jnp.clip(scaled, -LARGEST, LARGEST)
    code = jnp.floor(scaled + 0.5).astype(jnp.int32)
    head = code[:, :LANES]
    lane = lax.broadcasted_iota(jnp.int32, head.shape, 1)
    stored = exponent.astype(jnp.int32) + SCALE_SHIFT
    stored = jnp.broadcast_to(stored, head.shape)
    bit = lax.shift_right_logical(stored, jnp.minimum(lane, SCALE_BITS)) & 1
    head = jnp.where(lane < SCALE_BITS, (head & -2) | bit, head)
    return head.astype(jnp.int16), code[:, LANES:].astype(jnp.int16)


def row_scale(head):
    head = head.astype(jnp.int32)
    lane = lax.broadcasted_iota(jnp.int32, head.shape, 1)
    bits = lax.shift_left(head & 1, jnp.minimum(lane, SCALE_BITS))
    bits = jnp.where(lane < SCALE_BITS, bits, 0).astype(jnp.float32)
    stored = jnp.broadcast_to(jnp.sum(bits, axis=1, keepdims=True), head.shape)
    return jnp.exp2((stored - SCALE_SHIFT) * (1.0 / SCALE_STEPS)) * (1.0 / LARGEST)


def cost(rows, tile):
    flops = 2 * rows * tile.shape[-2] * tile.shape[-1]
    return pl.CostEstimate(flops=flops, bytes_accessed=2 * tile.shape[-2] * tile.shape[-1], transcendentals=0)


def blk_steps(blk_count, core):
    near = blk_count - 2
    steps = [slot + 1 + core * (near - 1 - 2 * slot) for slot in range(near)]
    return [0] + steps + [blk_count - 1]


def chip_steps(chips):
    return [0] + list(reversed(range(1, chips)))


def start_all(copies):
    for copy in copies:
        copy.start()


def wait_all(copies):
    for copy in copies:
        copy.wait()


def pick_kernel(tile_cd, amplitudes, *rest):
    outgoing, sems = rest[:-1], rest[-1]
    blk, grp = lax.axis_index("blk"), lax.axis_index("grp")
    copies = []
    for slot, step in enumerate(blk_steps(len(outgoing), grp % CORES)):
        cd = tile_cd[jnp.bitwise_xor(blk, step), grp]
        copies.append(pltpu.make_async_copy(amplitudes.at[cd], outgoing[slot], sems.at[slot]))
    start_all(copies)
    wait_all(copies)


def pick(tile_cd, amplitudes):
    groups = tile_cd.shape[0]
    block = jax.ShapeDtypeStruct(amplitudes.shape[1:], amplitudes.dtype)
    return pl.pallas_call(
        pick_kernel,
        out_shape=[block] * groups,
        in_specs=[SMEM, ANY],
        out_specs=[VMEM] * groups,
        scratch_shapes=[pltpu.SemaphoreType.DMA((groups,))],
        compiler_params=vmem_limit(*[block] * groups),
        name="pick_cd_blocks",
    )(tile_cd, amplitudes)


def code_chips(product, outgoing, first):
    chip_rows = product.shape[0] // len(outgoing)
    chip = lax.axis_index("grp") // CORES
    for step, coded in zip(chip_steps(len(outgoing)), outgoing):
        source = pl.multiple_of(jnp.bitwise_xor(chip, step) * chip_rows, chip_rows)
        code, tail = encode(product[pl.ds(source, chip_rows), :])
        coded[first : first + chip_rows, :LANES] = code
        coded[first : first + chip_rows, LANES:] = tail


def chips_kernel(chips, before, passed, rows, tile, *rest):
    front, rest = rest[:before], rest[before:]
    handed, outgoing, product = rest[:passed], rest[-chips - passed - 1 : -1], rest[-1]
    for source, target in zip(handed, outgoing[chips:]):
        target[...] = source[...]
    product[...] = jnp.dot(rows[...], tile[...], preferred_element_type=jnp.float32)
    first = outgoing[0].shape[0] - product.shape[0] // chips
    for source, target in zip(front, outgoing):
        target[:first, :] = source[...]
    code_chips(product, outgoing[:chips], first)


def contract_for_chips(rows, tile, chips, front=(), passed=(), earlier=()):
    group_rows, tile_width = rows.shape[0], tile.shape[1]
    coded_rows = group_rows // chips + sum(array.shape[0] for array in front[:1])
    coded = jax.ShapeDtypeStruct((coded_rows, tile_width), jnp.int16)
    product = jax.ShapeDtypeStruct((group_rows, tile_width), jnp.float32)
    outputs = [coded] * chips + [jax.ShapeDtypeStruct(array.shape, array.dtype) for array in passed]
    inputs = [rows, tile, *front, *passed]
    return pl.pallas_call(
        lambda *refs: chips_kernel(chips, len(front), len(passed), *refs),
        out_shape=outputs,
        in_specs=[VMEM] * len(inputs) + [ANY] * len(earlier),
        out_specs=[VMEM] * len(outputs),
        scratch_shapes=[pltpu.VMEM(product.shape, product.dtype)],
        compiler_params=vmem_limit(*inputs, *outputs, product),
        cost_estimate=cost(group_rows, tile),
        name="contract_for_chips",
    )(*inputs, *earlier)


def one_kernel(chips, rows, tile, *rest):
    coded, product = rest[-2:]
    chip_rows = product.shape[0] // chips
    product[...] = jnp.dot(rows[...], tile[...], preferred_element_type=jnp.float32)
    code_chips(product, [coded.at[pl.ds(slot * chip_rows, chip_rows)] for slot in range(chips)], 0)


def contract_whole(rows, tile, chips, earlier):
    coded = jax.ShapeDtypeStruct((rows.shape[0], tile.shape[1]), jnp.int16)
    product = jax.ShapeDtypeStruct(coded.shape, jnp.float32)
    return pl.pallas_call(
        lambda *refs: one_kernel(chips, *refs),
        out_shape=coded,
        in_specs=[VMEM] * 2 + [ANY] * len(earlier),
        out_specs=VMEM,
        scratch_shapes=[pltpu.VMEM(product.shape, product.dtype)],
        compiler_params=vmem_limit(rows, tile, coded, product),
        cost_estimate=cost(rows.shape[0], tile),
        name="contract_far_group",
    )(rows, tile, *earlier)


def split_kernel(source, *targets):
    part_rows = targets[0].shape[0]
    for slot, target in enumerate(targets):
        target[...] = source[slot * part_rows : (slot + 1) * part_rows, :]


def split(source, parts):
    rows, tile_width = source.shape
    target = jax.ShapeDtypeStruct((rows // parts, tile_width), source.dtype)
    return pl.pallas_call(
        split_kernel,
        out_shape=[target] * parts,
        in_specs=[VMEM],
        out_specs=[VMEM] * parts,
        compiler_params=vmem_limit(source, source),
        name="split_by_chip",
    )(source)


def last_rows_kernel(count, *refs):
    sources, target = refs[:count], refs[-1]
    part_rows = target.shape[0] // count
    for slot, source in enumerate(sources):
        target[slot * part_rows : (slot + 1) * part_rows, :] = source[source.shape[0] - part_rows :, :]


def last_rows(sources, part_rows, earlier=()):
    target = jax.ShapeDtypeStruct((len(sources) * part_rows, sources[0].shape[1]), sources[0].dtype)
    return pl.pallas_call(
        lambda *refs: last_rows_kernel(len(sources), *refs),
        out_shape=target,
        in_specs=[VMEM] * len(sources) + [ANY] * len(earlier),
        out_specs=VMEM,
        compiler_params=vmem_limit(*sources, target),
        name="rows_of_one_group",
    )(*sources, *earlier)


def other_core_kernel(pieces, owner_rows, *refs):
    arrays, halves = refs[:-1], refs[-1]
    other = 1 - lax.axis_index("grp") % CORES
    for index, (array, first) in enumerate(pieces):
        source = pl.multiple_of(first + other * owner_rows, owner_rows)
        halves[index * owner_rows : (index + 1) * owner_rows, :] = arrays[array][pl.ds(source, owner_rows), :]


def other_core_rows(arrays, pieces, owner_rows):
    halves = jax.ShapeDtypeStruct((len(pieces) * owner_rows, arrays[0].shape[1]), arrays[0].dtype)
    return pl.pallas_call(
        lambda *refs: other_core_kernel(pieces, owner_rows, *refs),
        out_shape=halves,
        in_specs=[VMEM] * len(arrays),
        out_specs=VMEM,
        compiler_params=vmem_limit(*arrays, halves),
        name="rows_of_other_core",
    )(*arrays)


def add_rows(rows, tables, grp, held):
    tile_ab, tile_cd, pair_screen = tables
    terms = []
    for source, span, p, g in rows:
        kept = pair_screen[tile_cd[p, g], grp].astype(jnp.float32)
        terms.append((source, span, row_scale(source[span, :LANES]) * kept, tile_ab[p, g]))
    for source, span, scale, ab in terms:
        for lane in range(0, held.shape[2], LANES):
            term = source[span, lane : lane + LANES].astype(jnp.float32) * scale
            held[ab, :, lane : lane + LANES] = held[ab, :, lane : lane + LANES] + term


def tile_of(index, blk, grp, core, chips, blk_count):
    p = jnp.bitwise_xor(blk, blk_steps(blk_count, core)[index // chips])
    chip_step = chip_steps(chips)[index % chips]
    return p, (jnp.bitwise_xor(grp // CORES, chip_step)) * CORES + core


def add_kernel(parts, pieces, *refs):
    tables, arrays, (swapped, residual_in, residual, held, sems) = refs[:3], refs[3:-5], refs[-5:]
    blk, grp = lax.axis_index("blk"), lax.axis_index("grp")
    ab_tiles, owner_rows, _ = residual.shape
    blk_count, chips = tables[0].shape[0], tables[0].shape[1] // CORES
    core = grp % CORES
    bounds = [ab_tiles * part // parts for part in range(parts + 1)]
    spans = [pl.ds(low, high - low) for low, high in zip(bounds[:-1], bounds[1:])]
    leaves = [pltpu.make_async_copy(held.at[span], residual.at[span], sems.at[i]) for i, span in enumerate(spans)]

    def hold(ab, carry):
        held[ab] = residual_in[ab]
        return carry

    lax.fori_loop(0, ab_tiles, hold, 0)
    rows = []
    for index, (array, first) in enumerate(pieces):
        span = pl.ds(pl.multiple_of(first + core * owner_rows, owner_rows), owner_rows)
        rows.append((arrays[array], span, *tile_of(index, blk, grp, core, chips, blk_count)))
        span = pl.ds(index * owner_rows, owner_rows)
        rows.append((swapped, span, *tile_of(index, blk, grp, 1 - core, chips, blk_count)))
    group = 8
    for start in range(0, len(rows), group):
        add_rows(rows[start : start + group], tables, grp, held)
    start_all(leaves)
    wait_all(leaves)


def add_blocks(tables, arrays, pieces, swapped, residual_in):
    parts = 5
    return pl.pallas_call(
        lambda *refs: add_kernel(parts, pieces, *refs),
        out_shape=jax.ShapeDtypeStruct(residual_in.shape, residual_in.dtype),
        in_specs=[SMEM] * 3 + [VMEM] * (len(arrays) + 2),
        out_specs=ANY,
        scratch_shapes=[pltpu.VMEM(residual_in.shape, residual_in.dtype), pltpu.SemaphoreType.DMA((parts,))],
        compiler_params=vmem_limit(*arrays, swapped, residual_in, residual_in),
        name="add_contributions",
    )(*tables, *arrays, swapped, residual_in)


def shards(amplitudes, pair_screen, integrals, tile_ab, tile_cd, residual_in):
    blk_count = lax.axis_size("blk")
    grp_count = lax.axis_size("grp")
    chips = grp_count // CORES
    owner_rows = residual_in.shape[0]
    far = blk_count - 1

    def swap(value, slot, chip_step, core_step=0):
        pairs = []
        for device in range(blk_count * grp_count):
            blk_step = blk_steps(blk_count, device % CORES)[slot]
            pairs.append((device, device ^ (blk_step * grp_count + chip_step * CORES + core_step)))
        return lax.ppermute(value, ("blk", "grp"), pairs)

    def along_chips(outgoing):
        steps = chip_steps(chips)
        return [outgoing[0]] + [swap(outgoing[slot], 0, steps[slot]) for slot in range(1, chips)]

    chip_rows = CORES * owner_rows
    tile = integrals[0]
    own_rows, *near_picked, far_picked = pick(tile_cd, amplitudes)
    near_rows = [swap(rows, index + 1, 0) for index, rows in enumerate(near_picked)]
    *own_out, far_picked = contract_for_chips(own_rows, tile, chips, passed=[far_picked])
    far_rows = swap(far_picked, far, 0)
    near_in = []
    for index, rows in enumerate(near_rows):
        front = own_out if index == len(near_rows) - 1 else []
        near_in.append(along_chips(contract_for_chips(rows, tile, chips, front=front)))
    far_in = along_chips(split(swap(contract_whole(far_rows, tile, chips, []), far, 0), chips))
    back_in = []
    for index, arrived in enumerate(near_in):
        earlier = [] if index == len(near_in) - 1 else []
        back_in.append(swap(last_rows(arrived, chip_rows, earlier), index + 1, 0))
    arrays = [*near_in[-1], *back_in, *far_in]
    pieces = [(slot, 0) for slot in range(chips)]
    pieces += [(chips + group, slot * chip_rows) for group in range(len(back_in)) for slot in range(chips)]
    pieces += [(chips + len(back_in) + slot, 0) for slot in range(chips)]
    swapped = swap(other_core_rows(arrays, pieces, owner_rows), 0, 0, 1)
    by_tile = jnp.transpose(residual_in, (1, 0, 2))
    added = add_blocks((tile_ab, tile_cd, pair_screen), arrays, pieces, swapped, by_tile)
    return jnp.transpose(added, (1, 0, 2))


def solution(mesh):
    in_specs = (
        P(None, "blk", None),
        P(None, "blk"),
        P(("blk", "grp"), None, None),
        P(),
        P(),
        P(("blk", "grp"), None, None),
    )
    out_specs = P(("blk", "grp"), None, None)
    return jax.shard_map(shards, mesh=mesh, in_specs=in_specs, out_specs=out_specs, check_vma=False)
```

```python
import math

import jax
import jax.numpy as jnp
from jax import lax
from jax.experimental import pallas as pl
from jax.experimental.pallas import tpu as pltpu
from jax.sharding import PartitionSpec as P

LARGEST = 32766.0
SCALE_STEPS = 64.0
SCALE_SHIFT = 8192
SCALE_BITS = 16
LANES = 128
CORES = 2
MEBIBYTE = 1 << 20
ROOMY = pltpu.CompilerParams(vmem_limit_bytes=209 * MEBIBYTE // 4)
SMEM = pl.BlockSpec(memory_space=pltpu.SMEM)
VMEM = pl.BlockSpec(memory_space=pltpu.VMEM)
ANY = pl.BlockSpec(memory_space=pl.ANY)


def vmem_limit(*arrays):
    total = sum(math.prod(array.shape) * jnp.dtype(array.dtype).itemsize for array in arrays)
    return pltpu.CompilerParams(vmem_limit_bytes=total + 4 * MEBIBYTE)


def encode(values):
    largest = jnp.max(jnp.abs(values), axis=1, keepdims=True)
    logarithm = jnp.log2(jnp.maximum(largest, 2.0**-100))
    exponent = jnp.floor(logarithm * SCALE_STEPS) + 2.0
    scaled = values * (LARGEST * jnp.exp2(exponent * (-1.0 / SCALE_STEPS)))
    scaled = jnp.clip(scaled, -LARGEST, LARGEST)
    code = jnp.floor(scaled + 0.5).astype(jnp.int32)
    head = code[:, :LANES]
    lane = lax.broadcasted_iota(jnp.int32, head.shape, 1)
    stored = exponent.astype(jnp.int32) + SCALE_SHIFT
    stored = jnp.broadcast_to(stored, head.shape)
    bit = lax.shift_right_logical(stored, jnp.minimum(lane, SCALE_BITS)) & 1
    head = jnp.where(lane < SCALE_BITS, (head & -2) | bit, head)
    return head.astype(jnp.int16), code[:, LANES:].astype(jnp.int16)


def row_scale(head):
    head = head.astype(jnp.int32)
    lane = lax.broadcasted_iota(jnp.int32, head.shape, 1)
    bits = lax.shift_left(head & 1, jnp.minimum(lane, SCALE_BITS))
    bits = jnp.where(lane < SCALE_BITS, bits, 0).astype(jnp.float32)
    stored = jnp.broadcast_to(jnp.sum(bits, axis=1, keepdims=True), head.shape)
    return jnp.exp2((stored - SCALE_SHIFT) * (1.0 / SCALE_STEPS)) * (1.0 / LARGEST)


def cost(rows, tile):
    flops = 2 * rows * tile.shape[-2] * tile.shape[-1]
    return pl.CostEstimate(flops=flops, bytes_accessed=2 * tile.shape[-2] * tile.shape[-1], transcendentals=0)


def blk_steps(blk_count, core):
    near = blk_count - 2
    steps = [slot + 1 + core * (near - 1 - 2 * slot) for slot in range(near)]
    return [0] + steps + [blk_count - 1]


def copies_of(source, target, parts, sems, first):
    rows = target.shape[0] // parts
    spans = [pl.ds(part * rows, rows) for part in range(parts)]
    return [pltpu.make_async_copy(source.at[s], target.at[s], sems.at[first + i]) for i, s in enumerate(spans)]


def start_all(copies):
    for copy in copies:
        copy.start()


def wait_all(copies):
    for copy in copies:
        copy.wait()


def pick_kernel(parts, tile_cd, amplitudes, *rest):
    outgoing, sems = rest[:-1], rest[-1]
    blk, grp = lax.axis_index("blk"), lax.axis_index("grp")
    copies = []
    for slot, step in enumerate(blk_steps(len(outgoing), grp % CORES)):
        cd = tile_cd[jnp.bitwise_xor(blk, step), grp]
        copies += copies_of(amplitudes.at[cd], outgoing[slot], parts, sems, slot * parts)
    start_all(copies)
    wait_all(copies)


def pick(tile_cd, amplitudes):
    groups, parts = tile_cd.shape[0], 4
    block = jax.ShapeDtypeStruct(amplitudes.shape[1:], amplitudes.dtype)
    return pl.pallas_call(
        lambda *refs: pick_kernel(parts, *refs),
        out_shape=[block] * groups,
        in_specs=[SMEM, ANY],
        out_specs=[VMEM] * groups,
        scratch_shapes=[pltpu.SemaphoreType.DMA((groups * parts,))],
        compiler_params=ROOMY,
        name="pick_cd_blocks",
    )(tile_cd, amplitudes)


def code_chips(product, outgoing, first):
    chip_rows = product.shape[0] // len(outgoing)
    chip = lax.axis_index("grp") // CORES
    for step, coded in enumerate(outgoing):
        source = pl.multiple_of(jnp.bitwise_xor(chip, step) * chip_rows, chip_rows)
        code, tail = encode(product[pl.ds(source, chip_rows), :])
        coded[first : first + chip_rows, :LANES] = code
        coded[first : first + chip_rows, LANES:] = tail


def own_kernel(steps, parts, rows, integrals, far_picked, *rest):
    outgoing, (far_out, tile, product, sems) = rest[:-4], rest[-4:]
    depth = tile.shape[0] // steps
    spans = [pl.ds(step * depth, depth) for step in range(steps)]
    copies = [copies_of(integrals.at[0, s], tile.at[s], parts, sems, i * parts) for i, s in enumerate(spans)]
    for group in copies:
        start_all(group)
    far_out[...] = far_picked[...]
    for step, group in enumerate(copies):
        wait_all(group)
        here = slice(step * depth, (step + 1) * depth)
        term = jnp.dot(rows[:, here], tile[here, :], preferred_element_type=jnp.float32)
        product[...] = product[...] + term if step else term
    code_chips(product, outgoing, 0)


def contract_own(rows, integrals, far_picked, chips):
    group_rows, (_, depth, tile_width) = rows.shape[0], integrals.shape
    steps, parts = 4, 4
    coded = jax.ShapeDtypeStruct((group_rows // chips, tile_width), jnp.int16)
    return pl.pallas_call(
        lambda *refs: own_kernel(steps, parts, *refs),
        out_shape=[coded] * chips + [jax.ShapeDtypeStruct(far_picked.shape, far_picked.dtype)],
        in_specs=[VMEM, ANY, VMEM],
        out_specs=[VMEM] * (chips + 1),
        scratch_shapes=[
            pltpu.VMEM((depth, tile_width), integrals.dtype),
            pltpu.VMEM((group_rows, tile_width), jnp.float32),
            pltpu.SemaphoreType.DMA((steps * parts,)),
        ],
        compiler_params=ROOMY,
        cost_estimate=cost(group_rows, integrals),
        name="contract_own_group",
    )(rows, integrals, far_picked)


def near_kernel(near, *refs):
    groups, tile, outgoing, product = refs[:near], refs[near], refs[near + 1 : -1], refs[-1]
    chip_rows = product.shape[0] // len(outgoing)
    for index, rows in enumerate(groups):
        product[...] = jnp.dot(rows[...], tile[...], preferred_element_type=jnp.float32)
        code_chips(product, outgoing, index * chip_rows)


def contract_near(groups, tile, chips):
    group_rows, tile_width = groups[0].shape[0], tile.shape[1]
    coded = jax.ShapeDtypeStruct((len(groups) * group_rows // chips, tile_width), jnp.int16)
    product = jax.ShapeDtypeStruct((group_rows, tile_width), jnp.float32)
    return pl.pallas_call(
        lambda *refs: near_kernel(len(groups), *refs),
        out_shape=[coded] * chips,
        in_specs=[VMEM] * (len(groups) + 1),
        out_specs=[VMEM] * chips,
        scratch_shapes=[pltpu.VMEM(product.shape, product.dtype)],
        compiler_params=vmem_limit(*groups, tile, *[coded] * chips, product),
        cost_estimate=cost(len(groups) * group_rows, tile),
        name="contract_near_groups",
    )(*groups, tile)


def far_kernel(chips, rows, tile, *rest):
    coded, product = rest[-2:]
    chip_rows = product.shape[0] // chips
    parts = [coded.at[pl.ds(step * chip_rows, chip_rows)] for step in range(chips)]
    product[...] = jnp.dot(rows[...], tile[...], preferred_element_type=jnp.float32)
    code_chips(product, parts, 0)


def contract_far(rows, tile, chips, earlier):
    coded = jax.ShapeDtypeStruct((rows.shape[0], tile.shape[1]), jnp.int16)
    product = jax.ShapeDtypeStruct(coded.shape, jnp.float32)
    return pl.pallas_call(
        lambda *refs: far_kernel(chips, *refs),
        out_shape=coded,
        in_specs=[VMEM] * 2 + [ANY] * len(earlier),
        out_specs=VMEM,
        scratch_shapes=[pltpu.VMEM(product.shape, product.dtype)],
        compiler_params=vmem_limit(rows, tile, coded, product),
        cost_estimate=cost(rows.shape[0], tile),
        name="contract_far_group",
    )(rows, tile, *earlier)


def regroup_kernel(count, *refs):
    sources, targets = refs[:count], refs[count:]
    part_rows = sources[0].shape[0] // len(targets)
    for j, source in enumerate(sources):
        for i, target in enumerate(targets):
            target[j * part_rows : (j + 1) * part_rows, :] = source[i * part_rows : (i + 1) * part_rows, :]


def regroup(sources, parts, name):
    rows, tile_width = sources[0].shape
    target = jax.ShapeDtypeStruct((len(sources) * rows // parts, tile_width), sources[0].dtype)
    return pl.pallas_call(
        lambda *refs: regroup_kernel(len(sources), *refs),
        out_shape=[target] * parts,
        in_specs=[VMEM] * len(sources),
        out_specs=[VMEM] * parts,
        compiler_params=vmem_limit(*sources, *[target] * parts),
        name=name,
    )(*sources)


def pieces_of(arrays, owner_rows):
    return [(array, first) for array in arrays for first in range(0, array.shape[0], CORES * owner_rows)]


def other_core_kernel(owner_rows, *refs):
    arrays, halves = refs[:-2], refs[-2:]
    other = 1 - lax.axis_index("grp") % CORES
    pieces = pieces_of(arrays, owner_rows)
    for index, (array, first) in enumerate(pieces):
        half, place = divmod(index, len(pieces) // 2)
        source = pl.multiple_of(first + other * owner_rows, owner_rows)
        halves[half][place * owner_rows : (place + 1) * owner_rows, :] = array[pl.ds(source, owner_rows), :]


def other_core_rows(arrays, owner_rows):
    rows = sum(array.shape[0] for array in arrays) // CORES
    half = jax.ShapeDtypeStruct((rows // 2, arrays[0].shape[1]), arrays[0].dtype)
    return pl.pallas_call(
        lambda *refs: other_core_kernel(owner_rows, *refs),
        out_shape=[half] * 2,
        in_specs=[VMEM] * len(arrays),
        out_specs=[VMEM] * 2,
        compiler_params=vmem_limit(*arrays, half, half),
        name="rows_of_other_core",
    )(*arrays)


def add_kernel(parts, tile_ab, tile_cd, pair_screen, *rest):
    arrays, swapped, (residual_in, residual, held, sems) = rest[:-6], rest[-6:-4], rest[-4:]
    blk, grp = lax.axis_index("blk"), lax.axis_index("grp")
    ab_tiles, owner_rows, tile_width = residual.shape
    chips = tile_ab.shape[1] // CORES
    bounds = [ab_tiles * part // parts for part in range(parts + 1)]
    spans = [pl.ds(low, high - low) for low, high in zip(bounds[:-1], bounds[1:])]
    leaves = [pltpu.make_async_copy(held.at[span], residual.at[span], sems.at[i]) for i, span in enumerate(spans)]

    def hold(ab, carry):
        held[ab] = residual_in[ab]
        return carry

    lax.fori_loop(0, ab_tiles, hold, 0)
    pieces = pieces_of(arrays, owner_rows)
    core = grp % CORES
    steps_here, steps_there = blk_steps(tile_ab.shape[0], core), blk_steps(tile_ab.shape[0], 1 - core)
    own = core * owner_rows
    for start in range(0, len(pieces), chips):
        terms = []
        for index in range(start, start + chips):
            array, first = pieces[index]
            p_here = jnp.bitwise_xor(blk, steps_here[index // chips])
            p_there = jnp.bitwise_xor(blk, steps_there[index // chips])
            g = jnp.bitwise_xor(grp, index % chips * CORES)
            here = pl.ds(pl.multiple_of(first + own, owner_rows), owner_rows)
            half, place = divmod(index, len(pieces) // 2)
            there = pl.ds(place * owner_rows, owner_rows)
            for source, span, p, column in ((array, here, p_here, g), (swapped[half], there, p_there, jnp.bitwise_xor(g, 1))):
                kept = pair_screen[tile_cd[p, column], grp].astype(jnp.float32)
                scale = row_scale(source[span, :LANES]) * kept
                terms.append((source, span, scale, tile_ab[p, column]))
        for source, span, scale, ab in terms:
            for lane in range(0, tile_width, LANES):
                term = source[span, lane : lane + LANES].astype(jnp.float32) * scale
                held[ab, :, lane : lane + LANES] = held[ab, :, lane : lane + LANES] + term
    start_all(leaves)
    wait_all(leaves)


def add_blocks(tile_ab, tile_cd, pair_screen, arrays, swapped, residual_in):
    parts = residual_in.shape[0] // 2
    return pl.pallas_call(
        lambda *refs: add_kernel(parts, *refs),
        out_shape=jax.ShapeDtypeStruct(residual_in.shape, residual_in.dtype),
        in_specs=[SMEM] * 3 + [VMEM] * (len(arrays) + 3),
        out_specs=ANY,
        scratch_shapes=[pltpu.VMEM(residual_in.shape, residual_in.dtype), pltpu.SemaphoreType.DMA((parts,))],
        compiler_params=vmem_limit(*arrays, *swapped, residual_in, residual_in),
        name="add_contributions",
    )(tile_ab, tile_cd, pair_screen, *arrays, *swapped, residual_in)


def shards(amplitudes, pair_screen, integrals, tile_ab, tile_cd, residual_in):
    blk_count = lax.axis_size("blk")
    grp_count = lax.axis_size("grp")
    chips = grp_count // CORES
    owner_rows = residual_in.shape[0]
    far = blk_count - 1

    def swap(value, slot, chip_step, core_step=0):
        pairs = []
        for device in range(blk_count * grp_count):
            blk_step = blk_steps(blk_count, device % CORES)[slot]
            pairs.append((device, device ^ (blk_step * grp_count + chip_step * CORES + core_step)))
        return lax.ppermute(value, ("blk", "grp"), pairs)

    def along_chips(outgoing):
        arrived = {step: swap(outgoing[step], 0, step) for step in reversed(range(1, chips))}
        return [outgoing[0]] + [arrived[step] for step in range(1, chips)]

    own_rows, *near_picked, far_picked = pick(tile_cd, amplitudes)
    near_rows = [swap(rows, index + 1, 0) for index, rows in enumerate(near_picked)]
    *own_out, far_picked = contract_own(own_rows, integrals, far_picked, chips)
    tile = integrals[0]
    own_in = along_chips(own_out)
    far_rows = swap(far_picked, far, 0)
    near_in = along_chips(contract_near(near_rows, tile, chips))
    near_back = regroup(near_in, blk_count - 2, "regroup_by_group")
    near_in = [swap(rows, index + 1, 0) for index, rows in enumerate(near_back)]
    far_back = swap(contract_far(far_rows, tile, chips, own_in[1:]), far, 0)
    far_in = along_chips(regroup([far_back], chips, "regroup_by_chip"))
    arrays = [*own_in, *near_in, *far_in]
    swapped = [swap(half, 0, 0, 1) for half in other_core_rows(arrays, owner_rows)]
    by_tile = jnp.transpose(residual_in, (1, 0, 2))
    added = add_blocks(tile_ab, tile_cd, pair_screen, arrays, swapped, by_tile)
    return jnp.transpose(added, (1, 0, 2))


def solution(mesh):
    in_specs = (
        P(None, "blk", None),
        P(None, "blk"),
        P(("blk", "grp"), None, None),
        P(),
        P(),
        P(("blk", "grp"), None, None),
    )
    out_specs = P(("blk", "grp"), None, None)
    return jax.shard_map(shards, mesh=mesh, in_specs=in_specs, out_specs=out_specs, check_vma=False)
```

```python
import math

import jax
import jax.numpy as jnp
from jax import lax
from jax.experimental import pallas as pl
from jax.experimental.pallas import tpu as pltpu
from jax.sharding import PartitionSpec as P

LARGEST = 32766.0
SCALE_STEPS = 64.0
SCALE_SHIFT = 8192
SCALE_BITS = 16
LANES = 128
CORES = 2
MEBIBYTE = 1 << 20
SMEM = pl.BlockSpec(memory_space=pltpu.SMEM)
VMEM = pl.BlockSpec(memory_space=pltpu.VMEM)
ANY = pl.BlockSpec(memory_space=pl.ANY)


def vmem_limit(*arrays):
    total = sum(math.prod(array.shape) * jnp.dtype(array.dtype).itemsize for array in arrays)
    return pltpu.CompilerParams(vmem_limit_bytes=total + 4 * MEBIBYTE)


def encode(values):
    largest = jnp.max(jnp.abs(values), axis=1, keepdims=True)
    logarithm = jnp.log2(jnp.maximum(largest, 2.0**-100))
    exponent = jnp.floor(logarithm * SCALE_STEPS) + 2.0
    scaled = values * (LARGEST * jnp.exp2(exponent * (-1.0 / SCALE_STEPS)))
    scaled = jnp.clip(scaled, -LARGEST, LARGEST)
    code = jnp.floor(scaled + 0.5).astype(jnp.int32)
    head = code[:, :LANES]
    lane = lax.broadcasted_iota(jnp.int32, head.shape, 1)
    stored = exponent.astype(jnp.int32) + SCALE_SHIFT
    stored = jnp.broadcast_to(stored, head.shape)
    bit = lax.shift_right_logical(stored, jnp.minimum(lane, SCALE_BITS)) & 1
    head = jnp.where(lane < SCALE_BITS, (head & -2) | bit, head)
    return head.astype(jnp.int16), code[:, LANES:].astype(jnp.int16)


def row_scale(head):
    head = head.astype(jnp.int32)
    lane = lax.broadcasted_iota(jnp.int32, head.shape, 1)
    bits = lax.shift_left(head & 1, jnp.minimum(lane, SCALE_BITS))
    bits = jnp.where(lane < SCALE_BITS, bits, 0).astype(jnp.float32)
    stored = jnp.broadcast_to(jnp.sum(bits, axis=1, keepdims=True), head.shape)
    return jnp.exp2((stored - SCALE_SHIFT) * (1.0 / SCALE_STEPS)) * (1.0 / LARGEST)


def cost(rows, tile):
    flops = 2 * rows * tile.shape[-2] * tile.shape[-1]
    return pl.CostEstimate(flops=flops, bytes_accessed=2 * tile.shape[-2] * tile.shape[-1], transcendentals=0)


def blk_steps(blk_count, core):
    near = blk_count - 2
    steps = [slot + 1 + core * (near - 1 - 2 * slot) for slot in range(near)]
    return [0] + steps + [blk_count - 1]


def chip_steps(chips):
    return list(range(chips))


def start_all(copies):
    for copy in copies:
        copy.start()


def wait_all(copies):
    for copy in copies:
        copy.wait()


def pick_kernel(tile_cd, amplitudes, *rest):
    outgoing, sems = rest[:-1], rest[-1]
    blk, grp = lax.axis_index("blk"), lax.axis_index("grp")
    copies = []
    for slot, step in enumerate(blk_steps(len(outgoing), grp % CORES)):
        cd = tile_cd[jnp.bitwise_xor(blk, step), grp]
        copies.append(pltpu.make_async_copy(amplitudes.at[cd], outgoing[slot], sems.at[slot]))
    start_all(copies)
    wait_all(copies)


def pick(tile_cd, amplitudes):
    groups = tile_cd.shape[0]
    block = jax.ShapeDtypeStruct(amplitudes.shape[1:], amplitudes.dtype)
    return pl.pallas_call(
        pick_kernel,
        out_shape=[block] * groups,
        in_specs=[SMEM, ANY],
        out_specs=[VMEM] * groups,
        scratch_shapes=[pltpu.SemaphoreType.DMA((groups,))],
        compiler_params=vmem_limit(*[block] * groups),
        name="pick_cd_blocks",
    )(tile_cd, amplitudes)


def code_chips(rows, tile, product, outgoing, first):
    product[...] = jnp.dot(rows[...], tile[...], preferred_element_type=jnp.float32)
    chip_rows = product.shape[0] // len(outgoing)
    chip = lax.axis_index("grp") // CORES
    for step, coded in zip(chip_steps(len(outgoing)), outgoing):
        source = pl.multiple_of(jnp.bitwise_xor(chip, step) * chip_rows, chip_rows)
        code, tail = encode(product[pl.ds(source, chip_rows), :])
        coded[first : first + chip_rows, :LANES] = code
        coded[first : first + chip_rows, LANES:] = tail


def own_kernel(rows, tile, far_picked, *rest):
    outgoing, (tile_out, far_out, product, sem) = rest[:-4], rest[-4:]
    copy = pltpu.make_async_copy(tile, tile_out, sem)
    copy.start()
    far_out[...] = far_picked[...]
    code_chips(rows, tile, product, outgoing, 0)
    copy.wait()


def contract_own(rows, tile, far_picked, chips):
    group_rows, tile_width = rows.shape[0], tile.shape[1]
    coded = jax.ShapeDtypeStruct((group_rows // chips, tile_width), jnp.int16)
    product = jax.ShapeDtypeStruct((group_rows, tile_width), jnp.float32)
    outputs = [coded] * chips + [jax.ShapeDtypeStruct(array.shape, array.dtype) for array in (tile, far_picked)]
    return pl.pallas_call(
        own_kernel,
        out_shape=outputs,
        in_specs=[VMEM] * 3,
        out_specs=[VMEM] * len(outputs),
        scratch_shapes=[pltpu.VMEM(product.shape, product.dtype), pltpu.SemaphoreType.DMA],
        compiler_params=vmem_limit(rows, tile, far_picked, *outputs, product),
        cost_estimate=cost(group_rows, tile),
        name="contract_own_group",
    )(rows, tile, far_picked)


def near_kernel(near, *refs):
    groups, tile, outgoing, product = refs[:near], refs[near], refs[near + 1 : -1], refs[-1]
    chip_rows = product.shape[0] // len(outgoing)
    for index, rows in enumerate(groups):
        code_chips(rows, tile, product, outgoing, index * chip_rows)


def contract_near(groups, tile, chips):
    group_rows, tile_width = groups[0].shape[0], tile.shape[1]
    coded = jax.ShapeDtypeStruct((len(groups) * group_rows // chips, tile_width), jnp.int16)
    product = jax.ShapeDtypeStruct((group_rows, tile_width), jnp.float32)
    return pl.pallas_call(
        lambda *refs: near_kernel(len(groups), *refs),
        out_shape=[coded] * chips,
        in_specs=[VMEM] * (len(groups) + 1),
        out_specs=[VMEM] * chips,
        scratch_shapes=[pltpu.VMEM(product.shape, product.dtype)],
        compiler_params=vmem_limit(*groups, tile, *[coded] * chips, product),
        cost_estimate=cost(len(groups) * group_rows, tile),
        name="contract_near_groups",
    )(*groups, tile)


def far_kernel(chips, rows, tile, *rest):
    coded, product = rest[-2:]
    chip_rows = product.shape[0] // chips
    parts = [coded.at[pl.ds(step * chip_rows, chip_rows)] for step in range(chips)]
    code_chips(rows, tile, product, parts, 0)


def contract_far(rows, tile, chips, earlier):
    coded = jax.ShapeDtypeStruct((rows.shape[0], tile.shape[1]), jnp.int16)
    product = jax.ShapeDtypeStruct(coded.shape, jnp.float32)
    return pl.pallas_call(
        lambda *refs: far_kernel(chips, *refs),
        out_shape=coded,
        in_specs=[VMEM] * 2 + [ANY] * len(earlier),
        out_specs=VMEM,
        scratch_shapes=[pltpu.VMEM(product.shape, product.dtype)],
        compiler_params=vmem_limit(rows, tile, coded, product),
        cost_estimate=cost(rows.shape[0], tile),
        name="contract_far_group",
    )(rows, tile, *earlier)


def regroup_kernel(count, parts, *refs):
    sources, targets = refs[:count], refs[-parts:]
    part_rows = sources[0].shape[0] // parts
    for j, source in enumerate(sources):
        for i, target in enumerate(targets):
            target[j * part_rows : (j + 1) * part_rows, :] = source[i * part_rows : (i + 1) * part_rows, :]


def regroup(sources, parts, name, earlier=()):
    rows, tile_width = sources[0].shape
    target = jax.ShapeDtypeStruct((len(sources) * rows // parts, tile_width), sources[0].dtype)
    return pl.pallas_call(
        lambda *refs: regroup_kernel(len(sources), parts, *refs),
        out_shape=[target] * parts,
        in_specs=[VMEM] * len(sources) + [ANY] * len(earlier),
        out_specs=[VMEM] * parts,
        compiler_params=vmem_limit(*sources, *[target] * parts),
        name=name,
    )(*sources, *earlier)


def pieces_of(arrays, owner_rows):
    return [(i, first) for i, array in enumerate(arrays) for first in range(0, array.shape[0], CORES * owner_rows)]


def other_core_kernel(pieces, owner_rows, *refs):
    arrays, halves = refs[:-1], refs[-1]
    other = 1 - lax.axis_index("grp") % CORES
    for index, (array, first) in enumerate(pieces):
        source = pl.multiple_of(first + other * owner_rows, owner_rows)
        halves[index * owner_rows : (index + 1) * owner_rows, :] = arrays[array][pl.ds(source, owner_rows), :]


def other_core_rows(arrays, pieces, owner_rows, earlier=()):
    halves = jax.ShapeDtypeStruct((len(pieces) * owner_rows, arrays[0].shape[1]), arrays[0].dtype)
    return pl.pallas_call(
        lambda *refs: other_core_kernel(pieces, owner_rows, *refs),
        out_shape=halves,
        in_specs=[VMEM] * len(arrays) + [ANY] * len(earlier),
        out_specs=VMEM,
        compiler_params=vmem_limit(*arrays, halves),
        name="rows_of_other_core",
    )(*arrays, *earlier)


def write_kernel(parts, residual_in, *rest):
    residual, token, sems = rest[-3:]
    token[...] = jnp.zeros_like(token)
    ab_tiles = residual.shape[0]
    bounds = [ab_tiles * part // parts for part in range(parts + 1)]
    spans = [pl.ds(low, high - low) for low, high in zip(bounds[:-1], bounds[1:])]
    copies = [pltpu.make_async_copy(residual_in.at[span], residual.at[span], sems.at[i]) for i, span in enumerate(spans)]
    start_all(copies)
    wait_all(copies)


def write_residual(residual_in, earlier):
    parts = 5
    token = jax.ShapeDtypeStruct((8, LANES), jnp.int32)
    return pl.pallas_call(
        lambda *refs: write_kernel(parts, *refs),
        out_shape=[jax.ShapeDtypeStruct(residual_in.shape, residual_in.dtype), token],
        in_specs=[VMEM] + [ANY] * len(earlier),
        out_specs=[ANY, VMEM],
        scratch_shapes=[pltpu.SemaphoreType.DMA((parts,))],
        compiler_params=vmem_limit(residual_in),
        name="write_residual",
    )(residual_in, *earlier)


def tiles_of(count, core, tile_ab):
    blk, grp = lax.axis_index("blk"), lax.axis_index("grp")
    blk_count, chips = tile_ab.shape[0], tile_ab.shape[1] // CORES
    tiles = []
    for index in range(count):
        step = blk_steps(blk_count, core)[index // chips]
        chip = jnp.bitwise_xor(grp // CORES, chip_steps(chips)[index % chips])
        tiles.append((jnp.bitwise_xor(blk, step), chip * CORES + core))
    return tiles


def add_rows(tables, sources, tiles, held):
    tile_ab, tile_cd, pair_screen = tables
    grp = lax.axis_index("grp")
    group = 8
    for start in range(0, len(sources), group):
        terms = []
        for (source, span), (p, g) in zip(sources[start : start + group], tiles[start : start + group]):
            kept = pair_screen[tile_cd[p, g], grp].astype(jnp.float32)
            terms.append((source, span, row_scale(source[span, :LANES]) * kept, tile_ab[p, g]))
        for source, span, scale, ab in terms:
            for lane in range(0, held.shape[2], LANES):
                term = source[span, lane : lane + LANES].astype(jnp.float32) * scale
                held[ab, :, lane : lane + LANES] = held[ab, :, lane : lane + LANES] + term


def add_here_kernel(pieces, *refs):
    tables, arrays, (residual_in, held) = refs[:3], refs[3:-2], refs[-2:]
    core = lax.axis_index("grp") % CORES
    owner_rows = held.shape[1]

    def hold(ab, carry):
        held[ab] = residual_in[ab]
        return carry

    lax.fori_loop(0, held.shape[0], hold, 0)
    spans = [pl.ds(pl.multiple_of(first + core * owner_rows, owner_rows), owner_rows) for _, first in pieces]
    sources = [(arrays[array], span) for (array, _), span in zip(pieces, spans)]
    add_rows(tables, sources, tiles_of(len(pieces), core, tables[0]), held)


def add_here(tables, arrays, pieces, residual_in):
    return pl.pallas_call(
        lambda *refs: add_here_kernel(pieces, *refs),
        out_shape=jax.ShapeDtypeStruct(residual_in.shape, residual_in.dtype),
        in_specs=[SMEM] * 3 + [VMEM] * (len(arrays) + 1),
        out_specs=VMEM,
        compiler_params=vmem_limit(*arrays, residual_in, residual_in),
        name="add_contributions_here",
    )(*tables, *arrays, residual_in)


def add_there_kernel(count, *refs):
    tables, (swapped, partial, _, residual, held, touched, sems) = refs[:3], refs[3:]
    core = lax.axis_index("grp") % CORES
    owner_rows = held.shape[1]
    here, there = tiles_of(count, core, tables[0]), tiles_of(count, 1 - core, tables[0])

    def clear(ab, carry):
        touched[ab] = 0
        return carry

    def first_touch(tile):
        ab = tables[0][tile]
        fresh = touched[ab] == 0
        touched[ab] = 1
        return ab, fresh

    def copies_do(action, source, touches, first):
        for index, (ab, fresh) in enumerate(touches):
            copy = pltpu.make_async_copy(source.at[ab], residual.at[ab], sems.at[first + index])
            pl.when(fresh)(getattr(copy, action))

    lax.fori_loop(0, residual.shape[0], clear, 0)
    late = [first_touch(tile) for tile in there]
    early = [first_touch(tile) for tile in here]
    copies_do("start", partial, early, count)
    for ab, _ in late:
        held[ab] = partial[ab]
    sources = [(swapped, pl.ds(index * owner_rows, owner_rows)) for index in range(count)]
    add_rows(tables, sources, there, held)
    copies_do("start", held, late, 0)
    copies_do("wait", partial, early, count)
    copies_do("wait", held, late, 0)


def add_there(tables, swapped, partial, written):
    whole = jax.ShapeDtypeStruct(partial.shape, partial.dtype)
    count = swapped.shape[0] // partial.shape[1]
    return pl.pallas_call(
        lambda *refs: add_there_kernel(count, *refs),
        out_shape=whole,
        in_specs=[SMEM] * 3 + [VMEM] * 2 + [ANY],
        out_specs=ANY,
        scratch_shapes=[
            pltpu.VMEM(whole.shape, whole.dtype),
            pltpu.SMEM(whole.shape[:1], jnp.int32),
            pltpu.SemaphoreType.DMA((2 * count,)),
        ],
        input_output_aliases={5: 0},
        compiler_params=vmem_limit(swapped, partial, partial),
        name="add_contributions_there",
    )(*tables, swapped, partial, written)


def shards(amplitudes, pair_screen, integrals, tile_ab, tile_cd, residual_in):
    blk_count = lax.axis_size("blk")
    grp_count = lax.axis_size("grp")
    chips = grp_count // CORES
    owner_rows = residual_in.shape[0]
    far = blk_count - 1

    def swap(value, slot, chip_step, core_step=0):
        pairs = []
        for device in range(blk_count * grp_count):
            blk_step = blk_steps(blk_count, device % CORES)[slot]
            pairs.append((device, device ^ (blk_step * grp_count + chip_step * CORES + core_step)))
        return lax.ppermute(value, ("blk", "grp"), pairs)

    def along_chips(outgoing):
        steps = chip_steps(chips)
        return [outgoing[0]] + [swap(outgoing[slot], 0, steps[slot]) for slot in range(1, chips)]

    own_rows, *near_picked, far_picked = pick(tile_cd, amplitudes)
    near_rows = [swap(rows, index + 1, 0) for index, rows in enumerate(near_picked)]
    *own_out, tile, far_picked = contract_own(own_rows, integrals[0], far_picked, chips)
    own_in = along_chips(own_out)
    far_rows = swap(far_picked, far, 0)
    near_in = along_chips(contract_near(near_rows, tile, chips))
    by_tile = jnp.transpose(residual_in, (1, 0, 2))
    far_coded = contract_far(far_rows, tile, chips, own_in[1:])
    written, token = write_residual(by_tile, [far_coded])
    near_back = regroup(near_in, blk_count - 2, "regroup_by_group", [token])
    near_in = [swap(rows, index + 1, 0) for index, rows in enumerate(near_back)]
    far_in = along_chips(regroup([swap(far_coded, far, 0)], chips, "regroup_by_chip"))

    tables = (tile_ab, tile_cd, pair_screen)
    arrays = [*own_in, *near_in, *far_in]
    pieces = pieces_of(arrays, owner_rows)
    swapped = swap(other_core_rows(arrays, pieces, owner_rows), 0, 0, 1)
    partial = add_here(tables, arrays, pieces, by_tile)
    return jnp.transpose(add_there(tables, swapped, partial, written), (1, 0, 2))


def solution(mesh):
    in_specs = (
        P(None, "blk", None),
        P(None, "blk"),
        P(("blk", "grp"), None, None),
        P(),
        P(),
        P(("blk", "grp"), None, None),
    )
    out_specs = P(("blk", "grp"), None, None)
    return jax.shard_map(shards, mesh=mesh, in_specs=in_specs, out_specs=out_specs, check_vma=False)
```

```python
import math

import jax
import jax.numpy as jnp
from jax import lax
from jax.experimental import pallas as pl
from jax.experimental.pallas import tpu as pltpu
from jax.sharding import PartitionSpec as P

LARGEST = 32766.0
SCALE_STEPS = 64.0
SCALE_SHIFT = 8192
SCALE_BITS = 16
LANES = 128
CORES = 2
MEBIBYTE = 1 << 20
SMEM = pl.BlockSpec(memory_space=pltpu.SMEM)
VMEM = pl.BlockSpec(memory_space=pltpu.VMEM)
ANY = pl.BlockSpec(memory_space=pl.ANY)


def vmem_limit(*arrays):
    total = sum(math.prod(array.shape) * jnp.dtype(array.dtype).itemsize for array in arrays)
    return pltpu.CompilerParams(vmem_limit_bytes=total + 4 * MEBIBYTE)


def encode(values):
    largest = jnp.max(jnp.abs(values), axis=1, keepdims=True)
    logarithm = jnp.log2(jnp.maximum(largest, 2.0**-100))
    exponent = jnp.floor(logarithm * SCALE_STEPS) + 2.0
    scaled = values * (LARGEST * jnp.exp2(exponent * (-1.0 / SCALE_STEPS)))
    scaled = jnp.clip(scaled, -LARGEST, LARGEST)
    code = jnp.floor(scaled + 0.5).astype(jnp.int32)
    head = code[:, :LANES]
    lane = lax.broadcasted_iota(jnp.int32, head.shape, 1)
    stored = exponent.astype(jnp.int32) + SCALE_SHIFT
    stored = jnp.broadcast_to(stored, head.shape)
    bit = lax.shift_right_logical(stored, jnp.minimum(lane, SCALE_BITS)) & 1
    head = jnp.where(lane < SCALE_BITS, (head & -2) | bit, head)
    return head.astype(jnp.int16), code[:, LANES:].astype(jnp.int16)


def row_scale(head):
    head = head.astype(jnp.int32)
    lane = lax.broadcasted_iota(jnp.int32, head.shape, 1)
    bits = lax.shift_left(head & 1, jnp.minimum(lane, SCALE_BITS))
    bits = jnp.where(lane < SCALE_BITS, bits, 0).astype(jnp.float32)
    stored = jnp.broadcast_to(jnp.sum(bits, axis=1, keepdims=True), head.shape)
    return jnp.exp2((stored - SCALE_SHIFT) * (1.0 / SCALE_STEPS)) * (1.0 / LARGEST)


def cost(rows, tile):
    flops = 2 * rows * tile.shape[-2] * tile.shape[-1]
    return pl.CostEstimate(flops=flops, bytes_accessed=2 * tile.shape[-2] * tile.shape[-1], transcendentals=0)


def blk_steps(blk_count, core):
    near = blk_count - 2
    steps = [slot + 1 + core * (near - 1 - 2 * slot) for slot in range(near)]
    return [0] + steps + [blk_count - 1]


def chip_steps(chips):
    return list(range(chips))


def start_all(copies):
    for copy in copies:
        copy.start()


def wait_all(copies):
    for copy in copies:
        copy.wait()


def pick_kernel(tile_cd, amplitudes, *rest):
    outgoing, sems = rest[:-1], rest[-1]
    blk, grp = lax.axis_index("blk"), lax.axis_index("grp")
    copies = []
    for slot, step in enumerate(blk_steps(len(outgoing), grp % CORES)):
        cd = tile_cd[jnp.bitwise_xor(blk, step), grp]
        copies.append(pltpu.make_async_copy(amplitudes.at[cd], outgoing[slot], sems.at[slot]))
    start_all(copies)
    wait_all(copies)


def pick(tile_cd, amplitudes):
    groups = tile_cd.shape[0]
    block = jax.ShapeDtypeStruct(amplitudes.shape[1:], amplitudes.dtype)
    return pl.pallas_call(
        pick_kernel,
        out_shape=[block] * groups,
        in_specs=[SMEM, ANY],
        out_specs=[VMEM] * groups,
        scratch_shapes=[pltpu.SemaphoreType.DMA((groups,))],
        compiler_params=vmem_limit(*[block] * groups),
        name="pick_cd_blocks",
    )(tile_cd, amplitudes)


def code_chips(rows, tile, product, outgoing, first):
    product[...] = jnp.dot(rows[...], tile[...], preferred_element_type=jnp.float32)
    chip_rows = product.shape[0] // len(outgoing)
    chip = lax.axis_index("grp") // CORES
    for step, coded in zip(chip_steps(len(outgoing)), outgoing):
        source = pl.multiple_of(jnp.bitwise_xor(chip, step) * chip_rows, chip_rows)
        code, tail = encode(product[pl.ds(source, chip_rows), :])
        coded[first : first + chip_rows, :LANES] = code
        coded[first : first + chip_rows, LANES:] = tail


def own_kernel(rows, tile, far_picked, *rest):
    outgoing, (tile_out, far_out, product, sem) = rest[:-4], rest[-4:]
    copy = pltpu.make_async_copy(tile, tile_out, sem)
    copy.start()
    far_out[...] = far_picked[...]
    code_chips(rows, tile, product, outgoing, 0)
    copy.wait()


def contract_own(rows, tile, far_picked, chips):
    group_rows, tile_width = rows.shape[0], tile.shape[1]
    coded = jax.ShapeDtypeStruct((group_rows // chips, tile_width), jnp.int16)
    product = jax.ShapeDtypeStruct((group_rows, tile_width), jnp.float32)
    outputs = [coded] * chips + [jax.ShapeDtypeStruct(array.shape, array.dtype) for array in (tile, far_picked)]
    return pl.pallas_call(
        own_kernel,
        out_shape=outputs,
        in_specs=[VMEM] * 3,
        out_specs=[VMEM] * len(outputs),
        scratch_shapes=[pltpu.VMEM(product.shape, product.dtype), pltpu.SemaphoreType.DMA],
        compiler_params=vmem_limit(rows, tile, far_picked, *outputs, product),
        cost_estimate=cost(group_rows, tile),
        name="contract_own_group",
    )(rows, tile, far_picked)


def near_kernel(near, *refs):
    groups, tile, outgoing, product = refs[:near], refs[near], refs[near + 1 : -1], refs[-1]
    chip_rows = product.shape[0] // len(outgoing)
    for index, rows in enumerate(groups):
        code_chips(rows, tile, product, outgoing, index * chip_rows)


def contract_near(groups, tile, chips):
    group_rows, tile_width = groups[0].shape[0], tile.shape[1]
    coded = jax.ShapeDtypeStruct((len(groups) * group_rows // chips, tile_width), jnp.int16)
    product = jax.ShapeDtypeStruct((group_rows, tile_width), jnp.float32)
    return pl.pallas_call(
        lambda *refs: near_kernel(len(groups), *refs),
        out_shape=[coded] * chips,
        in_specs=[VMEM] * (len(groups) + 1),
        out_specs=[VMEM] * chips,
        scratch_shapes=[pltpu.VMEM(product.shape, product.dtype)],
        compiler_params=vmem_limit(*groups, tile, *[coded] * chips, product),
        cost_estimate=cost(len(groups) * group_rows, tile),
        name="contract_near_groups",
    )(*groups, tile)


def far_kernel(chips, rows, tile, *rest):
    outgoing, product = rest[-chips - 1 : -1], rest[-1]
    code_chips(rows, tile, product, outgoing, 0)


def contract_far(rows, tile, chips, earlier):
    group_rows, tile_width = rows.shape[0], tile.shape[1]
    coded = jax.ShapeDtypeStruct((group_rows // chips, tile_width), jnp.int16)
    product = jax.ShapeDtypeStruct((group_rows, tile_width), jnp.float32)
    return pl.pallas_call(
        lambda *refs: far_kernel(chips, *refs),
        out_shape=[coded] * chips,
        in_specs=[VMEM] * 2 + [ANY] * len(earlier),
        out_specs=[VMEM] * chips,
        scratch_shapes=[pltpu.VMEM(product.shape, product.dtype)],
        compiler_params=vmem_limit(rows, tile, *[coded] * chips, product),
        cost_estimate=cost(group_rows, tile),
        name="contract_far_group",
    )(rows, tile, *earlier)


def regroup_kernel(count, parts, *refs):
    sources, targets = refs[:count], refs[-parts:]
    part_rows = sources[0].shape[0] // parts
    for j, source in enumerate(sources):
        for i, target in enumerate(targets):
            target[j * part_rows : (j + 1) * part_rows, :] = source[i * part_rows : (i + 1) * part_rows, :]


def regroup(sources, parts, name, earlier=()):
    rows, tile_width = sources[0].shape
    target = jax.ShapeDtypeStruct((len(sources) * rows // parts, tile_width), sources[0].dtype)
    return pl.pallas_call(
        lambda *refs: regroup_kernel(len(sources), parts, *refs),
        out_shape=[target] * parts,
        in_specs=[VMEM] * len(sources) + [ANY] * len(earlier),
        out_specs=[VMEM] * parts,
        compiler_params=vmem_limit(*sources, *[target] * parts),
        name=name,
    )(*sources, *earlier)


def pieces_of(arrays, owner_rows):
    return [(i, first) for i, array in enumerate(arrays) for first in range(0, array.shape[0], CORES * owner_rows)]


def other_core_kernel(pieces, owner_rows, *refs):
    arrays, halves = refs[:-1], refs[-1]
    other = 1 - lax.axis_index("grp") % CORES
    for index, (array, first) in enumerate(pieces):
        source = pl.multiple_of(first + other * owner_rows, owner_rows)
        halves[index * owner_rows : (index + 1) * owner_rows, :] = arrays[array][pl.ds(source, owner_rows), :]


def other_core_rows(arrays, pieces, owner_rows, earlier=()):
    halves = jax.ShapeDtypeStruct((len(pieces) * owner_rows, arrays[0].shape[1]), arrays[0].dtype)
    return pl.pallas_call(
        lambda *refs: other_core_kernel(pieces, owner_rows, *refs),
        out_shape=halves,
        in_specs=[VMEM] * len(arrays) + [ANY] * len(earlier),
        out_specs=VMEM,
        compiler_params=vmem_limit(*arrays, halves),
        name="rows_of_other_core",
    )(*arrays, *earlier)


def write_kernel(parts, residual_in, *rest):
    residual, token, sems = rest[-3:]
    token[...] = jnp.zeros_like(token)
    ab_tiles = residual.shape[0]
    bounds = [ab_tiles * part // parts for part in range(parts + 1)]
    spans = [pl.ds(low, high - low) for low, high in zip(bounds[:-1], bounds[1:])]
    copies = [pltpu.make_async_copy(residual_in.at[span], residual.at[span], sems.at[i]) for i, span in enumerate(spans)]
    start_all(copies)
    wait_all(copies)


def write_residual(residual_in, earlier):
    parts = 5
    token = jax.ShapeDtypeStruct((8, LANES), jnp.int32)
    return pl.pallas_call(
        lambda *refs: write_kernel(parts, *refs),
        out_shape=[jax.ShapeDtypeStruct(residual_in.shape, residual_in.dtype), token],
        in_specs=[VMEM] + [ANY] * len(earlier),
        out_specs=[ANY, VMEM],
        scratch_shapes=[pltpu.SemaphoreType.DMA((parts,))],
        compiler_params=vmem_limit(residual_in),
        name="write_residual",
    )(residual_in, *earlier)


def tiles_of(count, core, tile_ab):
    blk, grp = lax.axis_index("blk"), lax.axis_index("grp")
    blk_count, chips = tile_ab.shape[0], tile_ab.shape[1] // CORES
    tiles = []
    for index in range(count):
        step = blk_steps(blk_count, core)[index // chips]
        chip = jnp.bitwise_xor(grp // CORES, chip_steps(chips)[index % chips])
        tiles.append((jnp.bitwise_xor(blk, step), chip * CORES + core))
    return tiles


def add_rows(tables, sources, tiles, held):
    tile_ab, tile_cd, pair_screen = tables
    grp = lax.axis_index("grp")
    group = 8
    for start in range(0, len(sources), group):
        terms = []
        for (source, span), (p, g) in zip(sources[start : start + group], tiles[start : start + group]):
            kept = pair_screen[tile_cd[p, g], grp].astype(jnp.float32)
            terms.append((source, span, row_scale(source[span, :LANES]) * kept, tile_ab[p, g]))
        for source, span, scale, ab in terms:
            for lane in range(0, held.shape[2], LANES):
                term = source[span, lane : lane + LANES].astype(jnp.float32) * scale
                held[ab, :, lane : lane + LANES] = held[ab, :, lane : lane + LANES] + term


def add_here_kernel(pieces, *refs):
    tables, arrays, (residual_in, held) = refs[:3], refs[3:-2], refs[-2:]
    core = lax.axis_index("grp") % CORES
    owner_rows = held.shape[1]

    def hold(ab, carry):
        held[ab] = residual_in[ab]
        return carry

    lax.fori_loop(0, held.shape[0], hold, 0)
    spans = [pl.ds(pl.multiple_of(first + core * owner_rows, owner_rows), owner_rows) for _, first in pieces]
    sources = [(arrays[array], span) for (array, _), span in zip(pieces, spans)]
    add_rows(tables, sources, tiles_of(len(pieces), core, tables[0]), held)


def add_here(tables, arrays, pieces, residual_in):
    return pl.pallas_call(
        lambda *refs: add_here_kernel(pieces, *refs),
        out_shape=jax.ShapeDtypeStruct(residual_in.shape, residual_in.dtype),
        in_specs=[SMEM] * 3 + [VMEM] * (len(arrays) + 1),
        out_specs=VMEM,
        compiler_params=vmem_limit(*arrays, residual_in, residual_in),
        name="add_contributions_here",
    )(*tables, *arrays, residual_in)


def add_there_kernel(count, *refs):
    tables, (swapped, partial, _, residual, held, touched, sems) = refs[:3], refs[3:]
    core = lax.axis_index("grp") % CORES
    owner_rows = held.shape[1]
    here, there = tiles_of(count, core, tables[0]), tiles_of(count, 1 - core, tables[0])

    def clear(ab, carry):
        touched[ab] = 0
        return carry

    def first_touch(tile):
        ab = tables[0][tile]
        fresh = touched[ab] == 0
        touched[ab] = 1
        return ab, fresh

    def copies_do(action, source, touches, first):
        for index, (ab, fresh) in enumerate(touches):
            copy = pltpu.make_async_copy(source.at[ab], residual.at[ab], sems.at[first + index])
            pl.when(fresh)(getattr(copy, action))

    lax.fori_loop(0, residual.shape[0], clear, 0)
    late = [first_touch(tile) for tile in there]
    early = [first_touch(tile) for tile in here]
    copies_do("start", partial, early, count)
    for ab, _ in late:
        held[ab] = partial[ab]
    sources = [(swapped, pl.ds(index * owner_rows, owner_rows)) for index in range(count)]
    add_rows(tables, sources, there, held)
    copies_do("start", held, late, 0)
    copies_do("wait", partial, early, count)
    copies_do("wait", held, late, 0)


def add_there(tables, swapped, partial, written):
    whole = jax.ShapeDtypeStruct(partial.shape, partial.dtype)
    count = swapped.shape[0] // partial.shape[1]
    return pl.pallas_call(
        lambda *refs: add_there_kernel(count, *refs),
        out_shape=whole,
        in_specs=[SMEM] * 3 + [VMEM] * 2 + [ANY],
        out_specs=ANY,
        scratch_shapes=[
            pltpu.VMEM(whole.shape, whole.dtype),
            pltpu.SMEM(whole.shape[:1], jnp.int32),
            pltpu.SemaphoreType.DMA((2 * count,)),
        ],
        input_output_aliases={5: 0},
        compiler_params=vmem_limit(swapped, partial, partial),
        name="add_contributions_there",
    )(*tables, swapped, partial, written)


def shards(amplitudes, pair_screen, integrals, tile_ab, tile_cd, residual_in):
    blk_count = lax.axis_size("blk")
    grp_count = lax.axis_size("grp")
    chips = grp_count // CORES
    owner_rows = residual_in.shape[0]
    far = blk_count - 1

    def swap(value, slot, chip_step, core_step=0):
        pairs = []
        for device in range(blk_count * grp_count):
            blk_step = blk_steps(blk_count, device % CORES)[slot]
            pairs.append((device, device ^ (blk_step * grp_count + chip_step * CORES + core_step)))
        return lax.ppermute(value, ("blk", "grp"), pairs)

    def along_chips(outgoing):
        steps = chip_steps(chips)
        return [outgoing[0]] + [swap(outgoing[slot], 0, steps[slot]) for slot in range(1, chips)]

    own_rows, *near_picked, far_picked = pick(tile_cd, amplitudes)
    near_rows = [swap(rows, index + 1, 0) for index, rows in enumerate(near_picked)]
    *own_out, tile, far_picked = contract_own(own_rows, integrals[0], far_picked, chips)
    own_in = along_chips(own_out)
    far_rows = swap(far_picked, far, 0)
    near_in = along_chips(contract_near(near_rows, tile, chips))
    by_tile = jnp.transpose(residual_in, (1, 0, 2))
    far_coded = contract_far(far_rows, tile, chips, own_in[1:])
    far_in = [swap(coded, far, step) for step, coded in zip(chip_steps(chips), far_coded)]
    written, token = write_residual(by_tile, far_coded[:1])
    near_back = regroup(near_in, blk_count - 2, "regroup_by_group", [token, *far_in[:2]])
    near_in = [swap(rows, index + 1, 0) for index, rows in enumerate(near_back)]

    tables = (tile_ab, tile_cd, pair_screen)
    arrays = [*own_in, *near_in, *far_in]
    pieces = pieces_of(arrays, owner_rows)
    swapped = swap(other_core_rows(arrays, pieces, owner_rows), 0, 0, 1)
    partial = add_here(tables, arrays, pieces, by_tile)
    return jnp.transpose(add_there(tables, swapped, partial, written), (1, 0, 2))


def solution(mesh):
    in_specs = (
        P(None, "blk", None),
        P(None, "blk"),
        P(("blk", "grp"), None, None),
        P(),
        P(),
        P(("blk", "grp"), None, None),
    )
    out_specs = P(("blk", "grp"), None, None)
    return jax.shard_map(shards, mesh=mesh, in_specs=in_specs, out_specs=out_specs, check_vma=False)
```

```python
import math

import jax
import jax.numpy as jnp
from jax import lax
from jax.experimental import pallas as pl
from jax.experimental.pallas import tpu as pltpu
from jax.sharding import PartitionSpec as P

LARGEST = 32766.0
SCALE_STEPS = 64.0
SCALE_SHIFT = 8192
SCALE_BITS = 16
LANES = 128
CORES = 2
MEBIBYTE = 1 << 20
SMEM = pl.BlockSpec(memory_space=pltpu.SMEM)
VMEM = pl.BlockSpec(memory_space=pltpu.VMEM)
ANY = pl.BlockSpec(memory_space=pl.ANY)


def vmem_limit(*arrays):
    total = sum(math.prod(array.shape) * jnp.dtype(array.dtype).itemsize for array in arrays)
    return pltpu.CompilerParams(vmem_limit_bytes=total + 4 * MEBIBYTE)


def encode(values):
    largest = jnp.max(jnp.abs(values), axis=1, keepdims=True)
    logarithm = jnp.log2(jnp.maximum(largest, 2.0**-100))
    exponent = jnp.floor(logarithm * SCALE_STEPS) + 2.0
    scaled = values * (LARGEST * jnp.exp2(exponent * (-1.0 / SCALE_STEPS)))
    scaled = jnp.clip(scaled, -LARGEST, LARGEST)
    code = jnp.floor(scaled + 0.5).astype(jnp.int32)
    head = code[:, :LANES]
    lane = lax.broadcasted_iota(jnp.int32, head.shape, 1)
    stored = exponent.astype(jnp.int32) + SCALE_SHIFT
    stored = jnp.broadcast_to(stored, head.shape)
    bit = lax.shift_right_logical(stored, jnp.minimum(lane, SCALE_BITS)) & 1
    head = jnp.where(lane < SCALE_BITS, (head & -2) | bit, head)
    return head.astype(jnp.int16), code[:, LANES:].astype(jnp.int16)


def row_scale(head):
    head = head.astype(jnp.int32)
    lane = lax.broadcasted_iota(jnp.int32, head.shape, 1)
    bits = lax.shift_left(head & 1, jnp.minimum(lane, SCALE_BITS))
    bits = jnp.where(lane < SCALE_BITS, bits, 0).astype(jnp.float32)
    stored = jnp.broadcast_to(jnp.sum(bits, axis=1, keepdims=True), head.shape)
    return jnp.exp2((stored - SCALE_SHIFT) * (1.0 / SCALE_STEPS)) * (1.0 / LARGEST)


def cost(rows, tile):
    flops = 2 * rows * tile.shape[-2] * tile.shape[-1]
    return pl.CostEstimate(flops=flops, bytes_accessed=2 * tile.shape[-2] * tile.shape[-1], transcendentals=0)


def blk_steps(blk_count, core):
    near = blk_count - 2
    steps = [slot + 1 + core * (near - 1 - 2 * slot) for slot in range(near)]
    return [0] + steps + [blk_count - 1]


def chip_steps(chips, core):
    return [0] + [slot + core * (chips - 2 * slot) for slot in range(1, chips)]


def start_all(copies):
    for copy in copies:
        copy.start()


def wait_all(copies):
    for copy in copies:
        copy.wait()


def pick_kernel(tile_cd, amplitudes, *rest):
    outgoing, sems = rest[:-1], rest[-1]
    blk, grp = lax.axis_index("blk"), lax.axis_index("grp")
    copies = []
    for slot, step in enumerate(blk_steps(len(outgoing), grp % CORES)):
        cd = tile_cd[jnp.bitwise_xor(blk, step), grp]
        copies.append(pltpu.make_async_copy(amplitudes.at[cd], outgoing[slot], sems.at[slot]))
    start_all(copies)
    wait_all(copies)


def pick(tile_cd, amplitudes):
    groups = tile_cd.shape[0]
    block = jax.ShapeDtypeStruct(amplitudes.shape[1:], amplitudes.dtype)
    return pl.pallas_call(
        pick_kernel,
        out_shape=[block] * groups,
        in_specs=[SMEM, ANY],
        out_specs=[VMEM] * groups,
        scratch_shapes=[pltpu.SemaphoreType.DMA((groups,))],
        compiler_params=vmem_limit(*[block] * groups),
        name="pick_cd_blocks",
    )(tile_cd, amplitudes)


def code_chips(rows, tile, product, outgoing, first):
    product[...] = jnp.dot(rows[...], tile[...], preferred_element_type=jnp.float32)
    chip_rows = product.shape[0] // len(outgoing)
    grp = lax.axis_index("grp")
    chip = grp // CORES
    for step, coded in zip(chip_steps(len(outgoing), grp % CORES), outgoing):
        source = pl.multiple_of(jnp.bitwise_xor(chip, step) * chip_rows, chip_rows)
        code, tail = encode(product[pl.ds(source, chip_rows), :])
        coded[first : first + chip_rows, :LANES] = code
        coded[first : first + chip_rows, LANES:] = tail


def own_kernel(rows, tile, far_picked, *rest):
    outgoing, (tile_out, far_out, product, sem) = rest[:-4], rest[-4:]
    copy = pltpu.make_async_copy(tile, tile_out, sem)
    copy.start()
    far_out[...] = far_picked[...]
    code_chips(rows, tile, product, outgoing, 0)
    copy.wait()


def contract_own(rows, tile, far_picked, chips):
    group_rows, tile_width = rows.shape[0], tile.shape[1]
    coded = jax.ShapeDtypeStruct((group_rows // chips, tile_width), jnp.int16)
    product = jax.ShapeDtypeStruct((group_rows, tile_width), jnp.float32)
    outputs = [coded] * chips + [jax.ShapeDtypeStruct(array.shape, array.dtype) for array in (tile, far_picked)]
    return pl.pallas_call(
        own_kernel,
        out_shape=outputs,
        in_specs=[VMEM] * 3,
        out_specs=[VMEM] * len(outputs),
        scratch_shapes=[pltpu.VMEM(product.shape, product.dtype), pltpu.SemaphoreType.DMA],
        compiler_params=vmem_limit(rows, tile, far_picked, *outputs, product),
        cost_estimate=cost(group_rows, tile),
        name="contract_own_group",
    )(rows, tile, far_picked)


def near_kernel(near, *refs):
    groups, tile, outgoing, product = refs[:near], refs[near], refs[near + 1 : -1], refs[-1]
    chip_rows = product.shape[0] // len(outgoing)
    for index, rows in enumerate(groups):
        code_chips(rows, tile, product, outgoing, index * chip_rows)


def contract_near(groups, tile, chips):
    group_rows, tile_width = groups[0].shape[0], tile.shape[1]
    coded = jax.ShapeDtypeStruct((len(groups) * group_rows // chips, tile_width), jnp.int16)
    product = jax.ShapeDtypeStruct((group_rows, tile_width), jnp.float32)
    return pl.pallas_call(
        lambda *refs: near_kernel(len(groups), *refs),
        out_shape=[coded] * chips,
        in_specs=[VMEM] * (len(groups) + 1),
        out_specs=[VMEM] * chips,
        scratch_shapes=[pltpu.VMEM(product.shape, product.dtype)],
        compiler_params=vmem_limit(*groups, tile, *[coded] * chips, product),
        cost_estimate=cost(len(groups) * group_rows, tile),
        name="contract_near_groups",
    )(*groups, tile)


def far_kernel(chips, rows, tile, *rest):
    coded, product = rest[-2:]
    chip_rows = product.shape[0] // chips
    parts = [coded.at[pl.ds(step * chip_rows, chip_rows)] for step in range(chips)]
    code_chips(rows, tile, product, parts, 0)


def contract_far(rows, tile, chips, earlier):
    coded = jax.ShapeDtypeStruct((rows.shape[0], tile.shape[1]), jnp.int16)
    product = jax.ShapeDtypeStruct(coded.shape, jnp.float32)
    return pl.pallas_call(
        lambda *refs: far_kernel(chips, *refs),
        out_shape=coded,
        in_specs=[VMEM] * 2 + [ANY] * len(earlier),
        out_specs=VMEM,
        scratch_shapes=[pltpu.VMEM(product.shape, product.dtype)],
        compiler_params=vmem_limit(rows, tile, coded, product),
        cost_estimate=cost(rows.shape[0], tile),
        name="contract_far_group",
    )(rows, tile, *earlier)


def regroup_kernel(count, parts, *refs):
    sources, targets = refs[:count], refs[-parts:]
    part_rows = sources[0].shape[0] // parts
    for j, source in enumerate(sources):
        for i, target in enumerate(targets):
            target[j * part_rows : (j + 1) * part_rows, :] = source[i * part_rows : (i + 1) * part_rows, :]


def regroup(sources, parts, name, earlier=()):
    rows, tile_width = sources[0].shape
    target = jax.ShapeDtypeStruct((len(sources) * rows // parts, tile_width), sources[0].dtype)
    return pl.pallas_call(
        lambda *refs: regroup_kernel(len(sources), parts, *refs),
        out_shape=[target] * parts,
        in_specs=[VMEM] * len(sources) + [ANY] * len(earlier),
        out_specs=[VMEM] * parts,
        compiler_params=vmem_limit(*sources, *[target] * parts),
        name=name,
    )(*sources, *earlier)


def pieces_of(arrays, owner_rows):
    return [(i, first) for i, array in enumerate(arrays) for first in range(0, array.shape[0], CORES * owner_rows)]


def other_core_kernel(pieces, owner_rows, *refs):
    arrays, halves = refs[:-1], refs[-1]
    other = 1 - lax.axis_index("grp") % CORES
    for index, (array, first) in enumerate(pieces):
        source = pl.multiple_of(first + other * owner_rows, owner_rows)
        halves[index * owner_rows : (index + 1) * owner_rows, :] = arrays[array][pl.ds(source, owner_rows), :]


def other_core_rows(arrays, pieces, owner_rows, earlier=()):
    halves = jax.ShapeDtypeStruct((len(pieces) * owner_rows, arrays[0].shape[1]), arrays[0].dtype)
    return pl.pallas_call(
        lambda *refs: other_core_kernel(pieces, owner_rows, *refs),
        out_shape=halves,
        in_specs=[VMEM] * len(arrays) + [ANY] * len(earlier),
        out_specs=VMEM,
        compiler_params=vmem_limit(*arrays, halves),
        name="rows_of_other_core",
    )(*arrays, *earlier)


def write_kernel(parts, residual_in, *rest):
    residual, token, sems = rest[-3:]
    token[...] = jnp.zeros_like(token)
    ab_tiles = residual.shape[0]
    bounds = [ab_tiles * part // parts for part in range(parts + 1)]
    spans = [pl.ds(low, high - low) for low, high in zip(bounds[:-1], bounds[1:])]
    copies = [pltpu.make_async_copy(residual_in.at[span], residual.at[span], sems.at[i]) for i, span in enumerate(spans)]
    start_all(copies)
    wait_all(copies)


def write_residual(residual_in, earlier):
    parts = 5
    token = jax.ShapeDtypeStruct((8, LANES), jnp.int32)
    return pl.pallas_call(
        lambda *refs: write_kernel(parts, *refs),
        out_shape=[jax.ShapeDtypeStruct(residual_in.shape, residual_in.dtype), token],
        in_specs=[VMEM] + [ANY] * len(earlier),
        out_specs=[ANY, VMEM],
        scratch_shapes=[pltpu.SemaphoreType.DMA((parts,))],
        compiler_params=vmem_limit(residual_in),
        name="write_residual",
    )(residual_in, *earlier)


def tiles_of(count, core, tile_ab):
    blk, grp = lax.axis_index("blk"), lax.axis_index("grp")
    blk_count, chips = tile_ab.shape[0], tile_ab.shape[1] // CORES
    tiles = []
    for index in range(count):
        step = blk_steps(blk_count, core)[index // chips]
        chip = jnp.bitwise_xor(grp // CORES, chip_steps(chips, core)[index % chips])
        tiles.append((jnp.bitwise_xor(blk, step), chip * CORES + core))
    return tiles


def add_rows(tables, sources, tiles, held):
    tile_ab, tile_cd, pair_screen = tables
    grp = lax.axis_index("grp")
    group = 8
    for start in range(0, len(sources), group):
        terms = []
        for (source, span), (p, g) in zip(sources[start : start + group], tiles[start : start + group]):
            kept = pair_screen[tile_cd[p, g], grp].astype(jnp.float32)
            terms.append((source, span, row_scale(source[span, :LANES]) * kept, tile_ab[p, g]))
        for source, span, scale, ab in terms:
            for lane in range(0, held.shape[2], LANES):
                term = source[span, lane : lane + LANES].astype(jnp.float32) * scale
                held[ab, :, lane : lane + LANES] = held[ab, :, lane : lane + LANES] + term


def add_here_kernel(pieces, *refs):
    tables, arrays, (residual_in, held) = refs[:3], refs[3:-2], refs[-2:]
    core = lax.axis_index("grp") % CORES
    owner_rows = held.shape[1]

    def hold(ab, carry):
        held[ab] = residual_in[ab]
        return carry

    lax.fori_loop(0, held.shape[0], hold, 0)
    spans = [pl.ds(pl.multiple_of(first + core * owner_rows, owner_rows), owner_rows) for _, first in pieces]
    sources = [(arrays[array], span) for (array, _), span in zip(pieces, spans)]
    add_rows(tables, sources, tiles_of(len(pieces), core, tables[0]), held)


def add_here(tables, arrays, pieces, residual_in):
    return pl.pallas_call(
        lambda *refs: add_here_kernel(pieces, *refs),
        out_shape=jax.ShapeDtypeStruct(residual_in.shape, residual_in.dtype),
        in_specs=[SMEM] * 3 + [VMEM] * (len(arrays) + 1),
        out_specs=VMEM,
        compiler_params=vmem_limit(*arrays, residual_in, residual_in),
        name="add_contributions_here",
    )(*tables, *arrays, residual_in)


def add_there_kernel(count, *refs):
    tables, (swapped, partial, _, residual, held, touched, sems) = refs[:3], refs[3:]
    core = lax.axis_index("grp") % CORES
    owner_rows = held.shape[1]
    here, there = tiles_of(count, core, tables[0]), tiles_of(count, 1 - core, tables[0])

    def clear(ab, carry):
        touched[ab] = 0
        return carry

    def first_touch(tile):
        ab = tables[0][tile]
        fresh = touched[ab] == 0
        touched[ab] = 1
        return ab, fresh

    def copies_do(action, source, touches, first):
        for index, (ab, fresh) in enumerate(touches):
            copy = pltpu.make_async_copy(source.at[ab], residual.at[ab], sems.at[first + index])
            pl.when(fresh)(getattr(copy, action))

    lax.fori_loop(0, residual.shape[0], clear, 0)
    late = [first_touch(tile) for tile in there]
    early = [first_touch(tile) for tile in here]
    copies_do("start", partial, early, count)
    for ab, _ in late:
        held[ab] = partial[ab]
    sources = [(swapped, pl.ds(index * owner_rows, owner_rows)) for index in range(count)]
    add_rows(tables, sources, there, held)
    copies_do("start", held, late, 0)
    copies_do("wait", partial, early, count)
    copies_do("wait", held, late, 0)


def add_there(tables, swapped, partial, written):
    whole = jax.ShapeDtypeStruct(partial.shape, partial.dtype)
    count = swapped.shape[0] // partial.shape[1]
    return pl.pallas_call(
        lambda *refs: add_there_kernel(count, *refs),
        out_shape=whole,
        in_specs=[SMEM] * 3 + [VMEM] * 2 + [ANY],
        out_specs=ANY,
        scratch_shapes=[
            pltpu.VMEM(whole.shape, whole.dtype),
            pltpu.SMEM(whole.shape[:1], jnp.int32),
            pltpu.SemaphoreType.DMA((2 * count,)),
        ],
        input_output_aliases={5: 0},
        compiler_params=vmem_limit(swapped, partial, partial),
        name="add_contributions_there",
    )(*tables, swapped, partial, written)


def shards(amplitudes, pair_screen, integrals, tile_ab, tile_cd, residual_in):
    blk_count = lax.axis_size("blk")
    grp_count = lax.axis_size("grp")
    chips = grp_count // CORES
    owner_rows = residual_in.shape[0]
    far = blk_count - 1

    def swap(value, blk_slot, chip_slot, core_step=0):
        pairs = []
        for device in range(blk_count * grp_count):
            blk_step = blk_steps(blk_count, device % CORES)[blk_slot]
            chip_step = chip_steps(chips, device % CORES)[chip_slot]
            pairs.append((device, device ^ (blk_step * grp_count + chip_step * CORES + core_step)))
        return lax.ppermute(value, ("blk", "grp"), pairs)

    def along_chips(outgoing):
        return [outgoing[0]] + [swap(outgoing[slot], 0, slot) for slot in range(1, chips)]

    own_rows, *near_picked, far_picked = pick(tile_cd, amplitudes)
    near_rows = [swap(rows, index + 1, 0) for index, rows in enumerate(near_picked)]
    *own_out, tile, far_picked = contract_own(own_rows, integrals[0], far_picked, chips)
    own_in = along_chips(own_out)
    far_rows = swap(far_picked, far, 0)
    near_in = along_chips(contract_near(near_rows, tile, chips))
    by_tile = jnp.transpose(residual_in, (1, 0, 2))
    far_coded = contract_far(far_rows, tile, chips, own_in[1:])
    written, token = write_residual(by_tile, [far_coded])
    near_back = regroup(near_in, blk_count - 2, "regroup_by_group", [token])
    near_in = [swap(rows, index + 1, 0) for index, rows in enumerate(near_back)]
    far_in = along_chips(regroup([swap(far_coded, far, 0)], chips, "regroup_by_chip"))

    tables = (tile_ab, tile_cd, pair_screen)
    arrays = [*own_in, *near_in, *far_in]
    pieces = pieces_of(arrays, owner_rows)
    swapped = swap(other_core_rows(arrays, pieces, owner_rows), 0, 0, 1)
    partial = add_here(tables, arrays, pieces, by_tile)
    return jnp.transpose(add_there(tables, swapped, partial, written), (1, 0, 2))


def solution(mesh):
    in_specs = (
        P(None, "blk", None),
        P(None, "blk"),
        P(("blk", "grp"), None, None),
        P(),
        P(),
        P(("blk", "grp"), None, None),
    )
    out_specs = P(("blk", "grp"), None, None)
    return jax.shard_map(shards, mesh=mesh, in_specs=in_specs, out_specs=out_specs, check_vma=False)
```

```python
import math

import jax
import jax.numpy as jnp
from jax import lax
from jax.experimental import pallas as pl
from jax.experimental.pallas import tpu as pltpu
from jax.sharding import PartitionSpec as P

LARGEST = 32766.0
SCALE_STEPS = 64.0
SCALE_SHIFT = 8192
SCALE_BITS = 16
LANES = 128
CORES = 2
MEBIBYTE = 1 << 20
SMEM = pl.BlockSpec(memory_space=pltpu.SMEM)
VMEM = pl.BlockSpec(memory_space=pltpu.VMEM)
ANY = pl.BlockSpec(memory_space=pl.ANY)


def vmem_limit(*arrays):
    total = sum(math.prod(array.shape) * jnp.dtype(array.dtype).itemsize for array in arrays)
    return pltpu.CompilerParams(vmem_limit_bytes=total + 4 * MEBIBYTE)


def encode(values):
    largest = jnp.max(jnp.abs(values), axis=1, keepdims=True)
    logarithm = jnp.log2(jnp.maximum(largest, 2.0**-100))
    exponent = jnp.floor(logarithm * SCALE_STEPS) + 2.0
    scaled = values * (LARGEST * jnp.exp2(exponent * (-1.0 / SCALE_STEPS)))
    scaled = jnp.clip(scaled, -LARGEST, LARGEST)
    code = jnp.floor(scaled + 0.5).astype(jnp.int32)
    head = code[:, :LANES]
    lane = lax.broadcasted_iota(jnp.int32, head.shape, 1)
    stored = exponent.astype(jnp.int32) + SCALE_SHIFT
    stored = jnp.broadcast_to(stored, head.shape)
    bit = lax.shift_right_logical(stored, jnp.minimum(lane, SCALE_BITS)) & 1
    head = jnp.where(lane < SCALE_BITS, (head & -2) | bit, head)
    return head.astype(jnp.int16), code[:, LANES:].astype(jnp.int16)


def row_scale(head):
    head = head.astype(jnp.int32)
    lane = lax.broadcasted_iota(jnp.int32, head.shape, 1)
    bits = lax.shift_left(head & 1, jnp.minimum(lane, SCALE_BITS))
    bits = jnp.where(lane < SCALE_BITS, bits, 0).astype(jnp.float32)
    stored = jnp.broadcast_to(jnp.sum(bits, axis=1, keepdims=True), head.shape)
    return jnp.exp2((stored - SCALE_SHIFT) * (1.0 / SCALE_STEPS)) * (1.0 / LARGEST)


def cost(rows, tile):
    flops = 2 * rows * tile.shape[-2] * tile.shape[-1]
    return pl.CostEstimate(flops=flops, bytes_accessed=2 * tile.shape[-2] * tile.shape[-1], transcendentals=0)


def blk_steps(blk_count, core):
    near = blk_count - 2
    steps = [slot + 1 + core * (near - 1 - 2 * slot) for slot in range(near)]
    return [0] + steps + [blk_count - 1]


def chip_steps(chips):
    return list(range(chips))


def start_all(copies):
    for copy in copies:
        copy.start()


def wait_all(copies):
    for copy in copies:
        copy.wait()


def pick_kernel(tile_cd, amplitudes, *rest):
    outgoing, sems = rest[:-1], rest[-1]
    blk, grp = lax.axis_index("blk"), lax.axis_index("grp")
    copies = []
    for slot, step in enumerate(blk_steps(len(outgoing), grp % CORES)):
        cd = tile_cd[jnp.bitwise_xor(blk, step), grp]
        copies.append(pltpu.make_async_copy(amplitudes.at[cd], outgoing[slot], sems.at[slot]))
    start_all(copies)
    wait_all(copies)


def pick(tile_cd, amplitudes):
    groups = tile_cd.shape[0]
    block = jax.ShapeDtypeStruct(amplitudes.shape[1:], amplitudes.dtype)
    return pl.pallas_call(
        pick_kernel,
        out_shape=[block] * groups,
        in_specs=[SMEM, ANY],
        out_specs=[VMEM] * groups,
        scratch_shapes=[pltpu.SemaphoreType.DMA((groups,))],
        compiler_params=vmem_limit(*[block] * groups),
        name="pick_cd_blocks",
    )(tile_cd, amplitudes)


def code_chips(rows, tile, product, outgoing, first):
    product[...] = jnp.dot(rows[...], tile[...], preferred_element_type=jnp.float32)
    chip_rows = product.shape[0] // len(outgoing)
    chip = lax.axis_index("grp") // CORES
    for step, coded in zip(chip_steps(len(outgoing)), outgoing):
        source = pl.multiple_of(jnp.bitwise_xor(chip, step) * chip_rows, chip_rows)
        code, tail = encode(product[pl.ds(source, chip_rows), :])
        coded[first : first + chip_rows, :LANES] = code
        coded[first : first + chip_rows, LANES:] = tail


def own_kernel(rows, tile, far_picked, *rest):
    outgoing, (tile_out, far_out, product, sem) = rest[:-4], rest[-4:]
    copy = pltpu.make_async_copy(tile, tile_out, sem)
    copy.start()
    far_out[...] = far_picked[...]
    code_chips(rows, tile, product, outgoing, 0)
    copy.wait()


def contract_own(rows, tile, far_picked, chips):
    group_rows, tile_width = rows.shape[0], tile.shape[1]
    coded = jax.ShapeDtypeStruct((group_rows // chips, tile_width), jnp.int16)
    product = jax.ShapeDtypeStruct((group_rows, tile_width), jnp.float32)
    outputs = [coded] * chips + [jax.ShapeDtypeStruct(array.shape, array.dtype) for array in (tile, far_picked)]
    return pl.pallas_call(
        own_kernel,
        out_shape=outputs,
        in_specs=[VMEM] * 3,
        out_specs=[VMEM] * len(outputs),
        scratch_shapes=[pltpu.VMEM(product.shape, product.dtype), pltpu.SemaphoreType.DMA],
        compiler_params=vmem_limit(rows, tile, far_picked, *outputs, product),
        cost_estimate=cost(group_rows, tile),
        name="contract_own_group",
    )(rows, tile, far_picked)


def near_kernel(near, *refs):
    groups, tile, outgoing, product = refs[:near], refs[near], refs[near + 1 : -1], refs[-1]
    chip_rows = product.shape[0] // len(outgoing)
    for index, rows in enumerate(groups):
        code_chips(rows, tile, product, outgoing, index * chip_rows)


def contract_near(groups, tile, chips):
    group_rows, tile_width = groups[0].shape[0], tile.shape[1]
    coded = jax.ShapeDtypeStruct((len(groups) * group_rows // chips, tile_width), jnp.int16)
    product = jax.ShapeDtypeStruct((group_rows, tile_width), jnp.float32)
    return pl.pallas_call(
        lambda *refs: near_kernel(len(groups), *refs),
        out_shape=[coded] * chips,
        in_specs=[VMEM] * (len(groups) + 1),
        out_specs=[VMEM] * chips,
        scratch_shapes=[pltpu.VMEM(product.shape, product.dtype)],
        compiler_params=vmem_limit(*groups, tile, *[coded] * chips, product),
        cost_estimate=cost(len(groups) * group_rows, tile),
        name="contract_near_groups",
    )(*groups, tile)


def far_kernel(chips, rows, tile, *rest):
    coded, product = rest[-2:]
    chip_rows = product.shape[0] // chips
    parts = [coded.at[pl.ds(step * chip_rows, chip_rows)] for step in range(chips)]
    code_chips(rows, tile, product, parts, 0)


def contract_far(rows, tile, chips, earlier):
    coded = jax.ShapeDtypeStruct((rows.shape[0], tile.shape[1]), jnp.int16)
    product = jax.ShapeDtypeStruct(coded.shape, jnp.float32)
    return pl.pallas_call(
        lambda *refs: far_kernel(chips, *refs),
        out_shape=coded,
        in_specs=[VMEM] * 2 + [ANY] * len(earlier),
        out_specs=VMEM,
        scratch_shapes=[pltpu.VMEM(product.shape, product.dtype)],
        compiler_params=vmem_limit(rows, tile, coded, product),
        cost_estimate=cost(rows.shape[0], tile),
        name="contract_far_group",
    )(rows, tile, *earlier)


def regroup_kernel(count, parts, *refs):
    sources, targets = refs[:count], refs[-parts:]
    part_rows = sources[0].shape[0] // parts
    for j, source in enumerate(sources):
        for i, target in enumerate(targets):
            target[j * part_rows : (j + 1) * part_rows, :] = source[i * part_rows : (i + 1) * part_rows, :]


def regroup(sources, parts, name, earlier=()):
    rows, tile_width = sources[0].shape
    target = jax.ShapeDtypeStruct((len(sources) * rows // parts, tile_width), sources[0].dtype)
    return pl.pallas_call(
        lambda *refs: regroup_kernel(len(sources), parts, *refs),
        out_shape=[target] * parts,
        in_specs=[VMEM] * len(sources) + [ANY] * len(earlier),
        out_specs=[VMEM] * parts,
        compiler_params=vmem_limit(*sources, *[target] * parts),
        name=name,
    )(*sources, *earlier)


def pieces_of(arrays, owner_rows):
    return [(i, first) for i, array in enumerate(arrays) for first in range(0, array.shape[0], CORES * owner_rows)]


def other_core_kernel(pieces, owner_rows, *refs):
    arrays, halves = refs[:-1], refs[-1]
    other = 1 - lax.axis_index("grp") % CORES
    for index, (array, first) in enumerate(pieces):
        source = pl.multiple_of(first + other * owner_rows, owner_rows)
        halves[index * owner_rows : (index + 1) * owner_rows, :] = arrays[array][pl.ds(source, owner_rows), :]


def other_core_rows(arrays, pieces, owner_rows, earlier=()):
    halves = jax.ShapeDtypeStruct((len(pieces) * owner_rows, arrays[0].shape[1]), arrays[0].dtype)
    return pl.pallas_call(
        lambda *refs: other_core_kernel(pieces, owner_rows, *refs),
        out_shape=halves,
        in_specs=[VMEM] * len(arrays) + [ANY] * len(earlier),
        out_specs=VMEM,
        compiler_params=vmem_limit(*arrays, halves),
        name="rows_of_other_core",
    )(*arrays, *earlier)


def write_kernel(parts, residual_in, *rest):
    residual, token, sems = rest[-3:]
    token[...] = jnp.zeros_like(token)
    ab_tiles = residual.shape[0]
    bounds = [ab_tiles * part // parts for part in range(parts + 1)]
    spans = [pl.ds(low, high - low) for low, high in zip(bounds[:-1], bounds[1:])]
    copies = [pltpu.make_async_copy(residual_in.at[span], residual.at[span], sems.at[i]) for i, span in enumerate(spans)]
    start_all(copies)
    wait_all(copies)


def write_residual(residual_in, earlier):
    parts = 5
    token = jax.ShapeDtypeStruct((8, LANES), jnp.int32)
    return pl.pallas_call(
        lambda *refs: write_kernel(parts, *refs),
        out_shape=[jax.ShapeDtypeStruct(residual_in.shape, residual_in.dtype), token],
        in_specs=[VMEM] + [ANY] * len(earlier),
        out_specs=[ANY, VMEM],
        scratch_shapes=[pltpu.SemaphoreType.DMA((parts,))],
        compiler_params=vmem_limit(residual_in),
        name="write_residual",
    )(residual_in, *earlier)


def tiles_of(count, core, tile_ab):
    blk, grp = lax.axis_index("blk"), lax.axis_index("grp")
    blk_count, chips = tile_ab.shape[0], tile_ab.shape[1] // CORES
    tiles = []
    for index in range(count):
        step = blk_steps(blk_count, core)[index // chips]
        chip = jnp.bitwise_xor(grp // CORES, chip_steps(chips)[index % chips])
        tiles.append((jnp.bitwise_xor(blk, step), chip * CORES + core))
    return tiles


def add_rows(tables, sources, tiles, held):
    tile_ab, tile_cd, pair_screen = tables
    grp = lax.axis_index("grp")
    group = 8
    for start in range(0, len(sources), group):
        terms = []
        for (source, span), (p, g) in zip(sources[start : start + group], tiles[start : start + group]):
            kept = pair_screen[tile_cd[p, g], grp].astype(jnp.float32)
            terms.append((source, span, row_scale(source[span, :LANES]) * kept, tile_ab[p, g]))
        for source, span, scale, ab in terms:
            for lane in range(0, held.shape[2], LANES):
                term = source[span, lane : lane + LANES].astype(jnp.float32) * scale
                held[ab, :, lane : lane + LANES] = held[ab, :, lane : lane + LANES] + term


def add_here_kernel(pieces, *refs):
    tables, arrays, (residual_in, held) = refs[:3], refs[3:-2], refs[-2:]
    core = lax.axis_index("grp") % CORES
    owner_rows = held.shape[1]

    def hold(ab, carry):
        held[ab] = residual_in[ab]
        return carry

    lax.fori_loop(0, held.shape[0], hold, 0)
    spans = [pl.ds(pl.multiple_of(first + core * owner_rows, owner_rows), owner_rows) for _, first in pieces]
    sources = [(arrays[array], span) for (array, _), span in zip(pieces, spans)]
    add_rows(tables, sources, tiles_of(len(pieces), core, tables[0]), held)


def add_here(tables, arrays, pieces, residual_in):
    return pl.pallas_call(
        lambda *refs: add_here_kernel(pieces, *refs),
        out_shape=jax.ShapeDtypeStruct(residual_in.shape, residual_in.dtype),
        in_specs=[SMEM] * 3 + [VMEM] * (len(arrays) + 1),
        out_specs=VMEM,
        compiler_params=vmem_limit(*arrays, residual_in, residual_in),
        name="add_contributions_here",
    )(*tables, *arrays, residual_in)


def add_there_kernel(count, *refs):
    tables, (swapped, partial, _, residual, held, touched, sems) = refs[:3], refs[3:]
    core = lax.axis_index("grp") % CORES
    owner_rows = held.shape[1]
    here, there = tiles_of(count, core, tables[0]), tiles_of(count, 1 - core, tables[0])

    def clear(ab, carry):
        touched[ab] = 0
        return carry

    def first_touch(tile):
        ab = tables[0][tile]
        fresh = touched[ab] == 0
        touched[ab] = 1
        return ab, fresh

    def copies_do(action, source, touches, first):
        for index, (ab, fresh) in enumerate(touches):
            copy = pltpu.make_async_copy(source.at[ab], residual.at[ab], sems.at[first + index])
            pl.when(fresh)(getattr(copy, action))

    lax.fori_loop(0, residual.shape[0], clear, 0)
    late = [first_touch(tile) for tile in there]
    early = [first_touch(tile) for tile in here]
    copies_do("start", partial, early, count)
    for ab, _ in late:
        held[ab] = partial[ab]
    sources = [(swapped, pl.ds(index * owner_rows, owner_rows)) for index in range(count)]
    add_rows(tables, sources, there, held)
    copies_do("start", held, late, 0)
    copies_do("wait", partial, early, count)
    copies_do("wait", held, late, 0)


def add_there(tables, swapped, partial, written):
    whole = jax.ShapeDtypeStruct(partial.shape, partial.dtype)
    count = swapped.shape[0] // partial.shape[1]
    return pl.pallas_call(
        lambda *refs: add_there_kernel(count, *refs),
        out_shape=whole,
        in_specs=[SMEM] * 3 + [VMEM] * 2 + [ANY],
        out_specs=ANY,
        scratch_shapes=[
            pltpu.VMEM(whole.shape, whole.dtype),
            pltpu.SMEM(whole.shape[:1], jnp.int32),
            pltpu.SemaphoreType.DMA((2 * count,)),
        ],
        input_output_aliases={5: 0},
        compiler_params=vmem_limit(swapped, partial, partial),
        name="add_contributions_there",
    )(*tables, swapped, partial, written)


def shards(amplitudes, pair_screen, integrals, tile_ab, tile_cd, residual_in):
    blk_count = lax.axis_size("blk")
    grp_count = lax.axis_size("grp")
    chips = grp_count // CORES
    owner_rows = residual_in.shape[0]
    far = blk_count - 1

    def swap(value, slot, chip_step, core_step=0):
        pairs = []
        for device in range(blk_count * grp_count):
            blk_step = blk_steps(blk_count, device % CORES)[slot]
            pairs.append((device, device ^ (blk_step * grp_count + chip_step * CORES + core_step)))
        return lax.ppermute(value, ("blk", "grp"), pairs)

    def along_chips(outgoing):
        steps = chip_steps(chips)
        return [outgoing[0]] + [swap(outgoing[slot], 0, steps[slot]) for slot in range(1, chips)]

    own_rows, *near_picked, far_picked = pick(tile_cd, amplitudes)
    near_rows = [swap(rows, index + 1, 0) for index, rows in enumerate(near_picked)]
    *own_out, tile, far_picked = contract_own(own_rows, integrals[0], far_picked, chips)
    own_in = along_chips(own_out)
    far_rows = swap(far_picked, far, 0)
    near_in = along_chips(contract_near(near_rows, tile, chips))
    by_tile = jnp.transpose(residual_in, (1, 0, 2))
    far_coded = contract_far(far_rows, tile, chips, own_in[1:])
    written, token = write_residual(by_tile, [far_coded])
    half = chips // 2
    first_back = regroup(near_in[:half], blk_count - 2, "regroup_first_chips", [token])
    last_back = regroup(near_in[half:], blk_count - 2, "regroup_last_chips", [token])
    near_in = []
    for index in range(blk_count - 2):
        near_in += [swap(back[index], index + 1, 0) for back in (first_back, last_back)]
    far_in = along_chips(regroup([swap(far_coded, far, 0)], chips, "regroup_by_chip"))

    tables = (tile_ab, tile_cd, pair_screen)
    arrays = [*own_in, *near_in, *far_in]
    pieces = pieces_of(arrays, owner_rows)
    swapped = swap(other_core_rows(arrays, pieces, owner_rows), 0, 0, 1)
    partial = add_here(tables, arrays, pieces, by_tile)
    return jnp.transpose(add_there(tables, swapped, partial, written), (1, 0, 2))


def solution(mesh):
    in_specs = (
        P(None, "blk", None),
        P(None, "blk"),
        P(("blk", "grp"), None, None),
        P(),
        P(),
        P(("blk", "grp"), None, None),
    )
    out_specs = P(("blk", "grp"), None, None)
    return jax.shard_map(shards, mesh=mesh, in_specs=in_specs, out_specs=out_specs, check_vma=False)
```

```python
import math

import jax
import jax.numpy as jnp
from jax import lax
from jax.experimental import pallas as pl
from jax.experimental.pallas import tpu as pltpu
from jax.sharding import PartitionSpec as P

LARGEST = 32766.0
SCALE_STEPS = 64.0
SCALE_SHIFT = 8192
SCALE_BITS = 16
LANES = 128
CORES = 2
MEBIBYTE = 1 << 20
SMEM = pl.BlockSpec(memory_space=pltpu.SMEM)
VMEM = pl.BlockSpec(memory_space=pltpu.VMEM)
ANY = pl.BlockSpec(memory_space=pl.ANY)


def vmem_limit(*arrays):
    total = sum(math.prod(array.shape) * jnp.dtype(array.dtype).itemsize for array in arrays)
    return pltpu.CompilerParams(vmem_limit_bytes=total + 4 * MEBIBYTE)


def encode(values):
    largest = jnp.max(jnp.abs(values), axis=1, keepdims=True)
    logarithm = jnp.log2(jnp.maximum(largest, 2.0**-100))
    exponent = jnp.floor(logarithm * SCALE_STEPS) + 2.0
    scaled = values * (LARGEST * jnp.exp2(exponent * (-1.0 / SCALE_STEPS)))
    scaled = jnp.clip(scaled, -LARGEST, LARGEST)
    code = jnp.floor(scaled + 0.5).astype(jnp.int32)
    head = code[:, :LANES]
    lane = lax.broadcasted_iota(jnp.int32, head.shape, 1)
    stored = exponent.astype(jnp.int32) + SCALE_SHIFT
    stored = jnp.broadcast_to(stored, head.shape)
    bit = lax.shift_right_logical(stored, jnp.minimum(lane, SCALE_BITS)) & 1
    head = jnp.where(lane < SCALE_BITS, (head & -2) | bit, head)
    return head.astype(jnp.int16), code[:, LANES:].astype(jnp.int16)


def row_scale(head):
    head = head.astype(jnp.int32)
    lane = lax.broadcasted_iota(jnp.int32, head.shape, 1)
    bits = lax.shift_left(head & 1, jnp.minimum(lane, SCALE_BITS))
    bits = jnp.where(lane < SCALE_BITS, bits, 0).astype(jnp.float32)
    stored = jnp.broadcast_to(jnp.sum(bits, axis=1, keepdims=True), head.shape)
    return jnp.exp2((stored - SCALE_SHIFT) * (1.0 / SCALE_STEPS)) * (1.0 / LARGEST)


def cost(rows, tile):
    flops = 2 * rows * tile.shape[-2] * tile.shape[-1]
    return pl.CostEstimate(flops=flops, bytes_accessed=2 * tile.shape[-2] * tile.shape[-1], transcendentals=0)


def blk_steps(blk_count, core):
    near = blk_count - 2
    steps = [slot + 1 + core * (near - 1 - 2 * slot) for slot in range(near)]
    return [0] + steps + [blk_count - 1]


def chip_steps(chips, core):
    return [0] + [slot + (1 - core) * (chips - 2 * slot) for slot in range(1, chips)]


def start_all(copies):
    for copy in copies:
        copy.start()


def wait_all(copies):
    for copy in copies:
        copy.wait()


def pick_kernel(tile_cd, amplitudes, *rest):
    outgoing, sems = rest[:-1], rest[-1]
    blk, grp = lax.axis_index("blk"), lax.axis_index("grp")
    copies = []
    for slot, step in enumerate(blk_steps(len(outgoing), grp % CORES)):
        cd = tile_cd[jnp.bitwise_xor(blk, step), grp]
        copies.append(pltpu.make_async_copy(amplitudes.at[cd], outgoing[slot], sems.at[slot]))
    start_all(copies)
    wait_all(copies)


def pick(tile_cd, amplitudes):
    groups = tile_cd.shape[0]
    block = jax.ShapeDtypeStruct(amplitudes.shape[1:], amplitudes.dtype)
    return pl.pallas_call(
        pick_kernel,
        out_shape=[block] * groups,
        in_specs=[SMEM, ANY],
        out_specs=[VMEM] * groups,
        scratch_shapes=[pltpu.SemaphoreType.DMA((groups,))],
        compiler_params=vmem_limit(*[block] * groups),
        name="pick_cd_blocks",
    )(tile_cd, amplitudes)


def code_chips(rows, tile, product, outgoing, first):
    product[...] = jnp.dot(rows[...], tile[...], preferred_element_type=jnp.float32)
    chip_rows = product.shape[0] // len(outgoing)
    grp = lax.axis_index("grp")
    chip = grp // CORES
    for step, coded in zip(chip_steps(len(outgoing), grp % CORES), outgoing):
        source = pl.multiple_of(jnp.bitwise_xor(chip, step) * chip_rows, chip_rows)
        code, tail = encode(product[pl.ds(source, chip_rows), :])
        coded[first : first + chip_rows, :LANES] = code
        coded[first : first + chip_rows, LANES:] = tail


def own_kernel(rows, tile, far_picked, *rest):
    outgoing, (tile_out, far_out, product, sem) = rest[:-4], rest[-4:]
    copy = pltpu.make_async_copy(tile, tile_out, sem)
    copy.start()
    far_out[...] = far_picked[...]
    code_chips(rows, tile, product, outgoing, 0)
    copy.wait()


def contract_own(rows, tile, far_picked, chips):
    group_rows, tile_width = rows.shape[0], tile.shape[1]
    coded = jax.ShapeDtypeStruct((group_rows // chips, tile_width), jnp.int16)
    product = jax.ShapeDtypeStruct((group_rows, tile_width), jnp.float32)
    outputs = [coded] * chips + [jax.ShapeDtypeStruct(array.shape, array.dtype) for array in (tile, far_picked)]
    return pl.pallas_call(
        own_kernel,
        out_shape=outputs,
        in_specs=[VMEM] * 3,
        out_specs=[VMEM] * len(outputs),
        scratch_shapes=[pltpu.VMEM(product.shape, product.dtype), pltpu.SemaphoreType.DMA],
        compiler_params=vmem_limit(rows, tile, far_picked, *outputs, product),
        cost_estimate=cost(group_rows, tile),
        name="contract_own_group",
    )(rows, tile, far_picked)


def near_kernel(near, *refs):
    groups, tile, outgoing, product = refs[:near], refs[near], refs[near + 1 : -1], refs[-1]
    chip_rows = product.shape[0] // len(outgoing)
    for index, rows in enumerate(groups):
        code_chips(rows, tile, product, outgoing, index * chip_rows)


def contract_near(groups, tile, chips):
    group_rows, tile_width = groups[0].shape[0], tile.shape[1]
    coded = jax.ShapeDtypeStruct((len(groups) * group_rows // chips, tile_width), jnp.int16)
    product = jax.ShapeDtypeStruct((group_rows, tile_width), jnp.float32)
    return pl.pallas_call(
        lambda *refs: near_kernel(len(groups), *refs),
        out_shape=[coded] * chips,
        in_specs=[VMEM] * (len(groups) + 1),
        out_specs=[VMEM] * chips,
        scratch_shapes=[pltpu.VMEM(product.shape, product.dtype)],
        compiler_params=vmem_limit(*groups, tile, *[coded] * chips, product),
        cost_estimate=cost(len(groups) * group_rows, tile),
        name="contract_near_groups",
    )(*groups, tile)


def far_kernel(chips, rows, tile, *rest):
    coded, product = rest[-2:]
    chip_rows = product.shape[0] // chips
    parts = [coded.at[pl.ds(step * chip_rows, chip_rows)] for step in range(chips)]
    code_chips(rows, tile, product, parts, 0)


def contract_far(rows, tile, chips, earlier):
    coded = jax.ShapeDtypeStruct((rows.shape[0], tile.shape[1]), jnp.int16)
    product = jax.ShapeDtypeStruct(coded.shape, jnp.float32)
    return pl.pallas_call(
        lambda *refs: far_kernel(chips, *refs),
        out_shape=coded,
        in_specs=[VMEM] * 2 + [ANY] * len(earlier),
        out_specs=VMEM,
        scratch_shapes=[pltpu.VMEM(product.shape, product.dtype)],
        compiler_params=vmem_limit(rows, tile, coded, product),
        cost_estimate=cost(rows.shape[0], tile),
        name="contract_far_group",
    )(rows, tile, *earlier)


def regroup_kernel(count, parts, *refs):
    sources, targets = refs[:count], refs[-parts:]
    part_rows = sources[0].shape[0] // parts
    for j, source in enumerate(sources):
        for i, target in enumerate(targets):
            target[j * part_rows : (j + 1) * part_rows, :] = source[i * part_rows : (i + 1) * part_rows, :]


def regroup(sources, parts, name, earlier=()):
    rows, tile_width = sources[0].shape
    target = jax.ShapeDtypeStruct((len(sources) * rows // parts, tile_width), sources[0].dtype)
    return pl.pallas_call(
        lambda *refs: regroup_kernel(len(sources), parts, *refs),
        out_shape=[target] * parts,
        in_specs=[VMEM] * len(sources) + [ANY] * len(earlier),
        out_specs=[VMEM] * parts,
        compiler_params=vmem_limit(*sources, *[target] * parts),
        name=name,
    )(*sources, *earlier)


def pieces_of(arrays, owner_rows):
    return [(i, first) for i, array in enumerate(arrays) for first in range(0, array.shape[0], CORES * owner_rows)]


def other_core_kernel(pieces, owner_rows, *refs):
    arrays, halves = refs[:-1], refs[-1]
    other = 1 - lax.axis_index("grp") % CORES
    for index, (array, first) in enumerate(pieces):
        source = pl.multiple_of(first + other * owner_rows, owner_rows)
        halves[index * owner_rows : (index + 1) * owner_rows, :] = arrays[array][pl.ds(source, owner_rows), :]


def other_core_rows(arrays, pieces, owner_rows, earlier=()):
    halves = jax.ShapeDtypeStruct((len(pieces) * owner_rows, arrays[0].shape[1]), arrays[0].dtype)
    return pl.pallas_call(
        lambda *refs: other_core_kernel(pieces, owner_rows, *refs),
        out_shape=halves,
        in_specs=[VMEM] * len(arrays) + [ANY] * len(earlier),
        out_specs=VMEM,
        compiler_params=vmem_limit(*arrays, halves),
        name="rows_of_other_core",
    )(*arrays, *earlier)


def write_kernel(parts, residual_in, *rest):
    residual, token, sems = rest[-3:]
    token[...] = jnp.zeros_like(token)
    ab_tiles = residual.shape[0]
    bounds = [ab_tiles * part // parts for part in range(parts + 1)]
    spans = [pl.ds(low, high - low) for low, high in zip(bounds[:-1], bounds[1:])]
    copies = [pltpu.make_async_copy(residual_in.at[span], residual.at[span], sems.at[i]) for i, span in enumerate(spans)]
    start_all(copies)
    wait_all(copies)


def write_residual(residual_in, earlier):
    parts = 5
    token = jax.ShapeDtypeStruct((8, LANES), jnp.int32)
    return pl.pallas_call(
        lambda *refs: write_kernel(parts, *refs),
        out_shape=[jax.ShapeDtypeStruct(residual_in.shape, residual_in.dtype), token],
        in_specs=[VMEM] + [ANY] * len(earlier),
        out_specs=[ANY, VMEM],
        scratch_shapes=[pltpu.SemaphoreType.DMA((parts,))],
        compiler_params=vmem_limit(residual_in),
        name="write_residual",
    )(residual_in, *earlier)


def tiles_of(count, core, tile_ab):
    blk, grp = lax.axis_index("blk"), lax.axis_index("grp")
    blk_count, chips = tile_ab.shape[0], tile_ab.shape[1] // CORES
    tiles = []
    for index in range(count):
        step = blk_steps(blk_count, core)[index // chips]
        chip = jnp.bitwise_xor(grp // CORES, chip_steps(chips, core)[index % chips])
        tiles.append((jnp.bitwise_xor(blk, step), chip * CORES + core))
    return tiles


def add_rows(tables, sources, tiles, held):
    tile_ab, tile_cd, pair_screen = tables
    grp = lax.axis_index("grp")
    group = 8
    for start in range(0, len(sources), group):
        terms = []
        for (source, span), (p, g) in zip(sources[start : start + group], tiles[start : start + group]):
            kept = pair_screen[tile_cd[p, g], grp].astype(jnp.float32)
            terms.append((source, span, row_scale(source[span, :LANES]) * kept, tile_ab[p, g]))
        for source, span, scale, ab in terms:
            for lane in range(0, held.shape[2], LANES):
                term = source[span, lane : lane + LANES].astype(jnp.float32) * scale
                held[ab, :, lane : lane + LANES] = held[ab, :, lane : lane + LANES] + term


def add_here_kernel(pieces, *refs):
    tables, arrays, (residual_in, held) = refs[:3], refs[3:-2], refs[-2:]
    core = lax.axis_index("grp") % CORES
    owner_rows = held.shape[1]

    def hold(ab, carry):
        held[ab] = residual_in[ab]
        return carry

    lax.fori_loop(0, held.shape[0], hold, 0)
    spans = [pl.ds(pl.multiple_of(first + core * owner_rows, owner_rows), owner_rows) for _, first in pieces]
    sources = [(arrays[array], span) for (array, _), span in zip(pieces, spans)]
    add_rows(tables, sources, tiles_of(len(pieces), core, tables[0]), held)


def add_here(tables, arrays, pieces, residual_in):
    return pl.pallas_call(
        lambda *refs: add_here_kernel(pieces, *refs),
        out_shape=jax.ShapeDtypeStruct(residual_in.shape, residual_in.dtype),
        in_specs=[SMEM] * 3 + [VMEM] * (len(arrays) + 1),
        out_specs=VMEM,
        compiler_params=vmem_limit(*arrays, residual_in, residual_in),
        name="add_contributions_here",
    )(*tables, *arrays, residual_in)


def add_there_kernel(count, *refs):
    tables, (swapped, partial, _, residual, held, touched, sems) = refs[:3], refs[3:]
    core = lax.axis_index("grp") % CORES
    owner_rows = held.shape[1]
    here, there = tiles_of(count, core, tables[0]), tiles_of(count, 1 - core, tables[0])

    def clear(ab, carry):
        touched[ab] = 0
        return carry

    def first_touch(tile):
        ab = tables[0][tile]
        fresh = touched[ab] == 0
        touched[ab] = 1
        return ab, fresh

    def copies_do(action, source, touches, first):
        for index, (ab, fresh) in enumerate(touches):
            copy = pltpu.make_async_copy(source.at[ab], residual.at[ab], sems.at[first + index])
            pl.when(fresh)(getattr(copy, action))

    lax.fori_loop(0, residual.shape[0], clear, 0)
    late = [first_touch(tile) for tile in there]
    early = [first_touch(tile) for tile in here]
    copies_do("start", partial, early, count)
    for ab, _ in late:
        held[ab] = partial[ab]
    sources = [(swapped, pl.ds(index * owner_rows, owner_rows)) for index in range(count)]
    add_rows(tables, sources, there, held)
    copies_do("start", held, late, 0)
    copies_do("wait", partial, early, count)
    copies_do("wait", held, late, 0)


def add_there(tables, swapped, partial, written):
    whole = jax.ShapeDtypeStruct(partial.shape, partial.dtype)
    count = swapped.shape[0] // partial.shape[1]
    return pl.pallas_call(
        lambda *refs: add_there_kernel(count, *refs),
        out_shape=whole,
        in_specs=[SMEM] * 3 + [VMEM] * 2 + [ANY],
        out_specs=ANY,
        scratch_shapes=[
            pltpu.VMEM(whole.shape, whole.dtype),
            pltpu.SMEM(whole.shape[:1], jnp.int32),
            pltpu.SemaphoreType.DMA((2 * count,)),
        ],
        input_output_aliases={5: 0},
        compiler_params=vmem_limit(swapped, partial, partial),
        name="add_contributions_there",
    )(*tables, swapped, partial, written)


def shards(amplitudes, pair_screen, integrals, tile_ab, tile_cd, residual_in):
    blk_count = lax.axis_size("blk")
    grp_count = lax.axis_size("grp")
    chips = grp_count // CORES
    owner_rows = residual_in.shape[0]
    far = blk_count - 1

    def swap(value, blk_slot, chip_slot, core_step=0):
        pairs = []
        for device in range(blk_count * grp_count):
            blk_step = blk_steps(blk_count, device % CORES)[blk_slot]
            chip_step = chip_steps(chips, device % CORES)[chip_slot]
            pairs.append((device, device ^ (blk_step * grp_count + chip_step * CORES + core_step)))
        return lax.ppermute(value, ("blk", "grp"), pairs)

    def along_chips(outgoing):
        return [outgoing[0]] + [swap(outgoing[slot], 0, slot) for slot in range(1, chips)]

    own_rows, *near_picked, far_picked = pick(tile_cd, amplitudes)
    near_rows = [swap(rows, index + 1, 0) for index, rows in enumerate(near_picked)]
    *own_out, tile, far_picked = contract_own(own_rows, integrals[0], far_picked, chips)
    own_in = along_chips(own_out)
    far_rows = swap(far_picked, far, 0)
    near_in = along_chips(contract_near(near_rows, tile, chips))
    by_tile = jnp.transpose(residual_in, (1, 0, 2))
    far_coded = contract_far(far_rows, tile, chips, own_in[1:])
    written, token = write_residual(by_tile, [far_coded])
    near_back = regroup(near_in, blk_count - 2, "regroup_by_group", [token])
    near_in = [swap(rows, index + 1, 0) for index, rows in enumerate(near_back)]
    far_in = along_chips(regroup([swap(far_coded, far, 0)], chips, "regroup_by_chip"))

    tables = (tile_ab, tile_cd, pair_screen)
    arrays = [*own_in, *near_in, *far_in]
    pieces = pieces_of(arrays, owner_rows)
    swapped = swap(other_core_rows(arrays, pieces, owner_rows), 0, 0, 1)
    partial = add_here(tables, arrays, pieces, by_tile)
    return jnp.transpose(add_there(tables, swapped, partial, written), (1, 0, 2))


def solution(mesh):
    in_specs = (
        P(None, "blk", None),
        P(None, "blk"),
        P(("blk", "grp"), None, None),
        P(),
        P(),
        P(("blk", "grp"), None, None),
    )
    out_specs = P(("blk", "grp"), None, None)
    return jax.shard_map(shards, mesh=mesh, in_specs=in_specs, out_specs=out_specs, check_vma=False)
```
